32 devices in a mesh: win: 8 (over z, y), var: 4 (over x, core).
Axes of the slice: x: 2, y: 2, z: 4, core: 2. Of those that a mesh axis runs over, the one named last changes fastest.
Arguments:
- inputs: bfloat16 [96, 256, 512], P('win', 'var'), may hold values from -6 to 6
- counts: int32 [96], P('win'), may hold values from 8 to 256, as said below
- row_index: int32 [96, 256], P('win'), may hold values from 0 to 255, each once within a row
- w_qkv: bfloat16 [2, 512, 1536], replicated, may hold values from -0.25 to 0.25
- bias_qv: float32 [2, 1024], replicated, may hold values from -2 to 2
- w_attn_out: bfloat16 [2, 512, 512], replicated, may hold values from -0.75 to 0.75
- out_bias: float32 [2, 2, 512], replicated, may hold values from -2 to 2
- w_in: bfloat16 [2, 512, 2048], replicated, may hold values from -0.25 to 0.25
- bias_in: float32 [2, 2048], replicated, may hold values from -2 to 2
- w_ffn_out: bfloat16 [2, 2048, 512], replicated, may hold values from -0.125 to 0.125
- norm_gain: float32 [2, 2, 512], replicated, may hold values from 0.5 to 1.5
- norm_bias: float32 [2, 2, 512], replicated, may hold values from -2 to 2
- cotangent: bfloat16 [96, 256, 512], P('win', 'var'), may hold values from -6 to 6
Outputs:
- layer_out: bfloat16 [96, 256, 512], P('win', 'var')
- grad_inputs: float32 [96, 256, 512], P('win', 'var')
- grad_qkv: float32 [2, 512, 1536], P(None, 'var')
- grad_bias_qv: float32 [2, 1024], P(None, 'var')
- grad_attn_out: float32 [2, 512, 512], P(None, 'var')
- grad_out_bias: float32 [2, 2, 512], P(None, None, 'var')
- grad_in: float32 [2, 512, 2048], P(None, 'var')
- grad_bias_in: float32 [2, 2048], P(None, 'var')
- grad_ffn_out: float32 [2, 2048, 512], P(None, 'var')
- grad_gain: float32 [2, 2, 512], P(None, None, 'var')
- grad_norm_bias: float32 [2, 2, 512], P(None, None, 'var')
The draws below stay inside these ranges and needn't reach their ends.
Inputs may be any that keep to these rules, and one draw needn't show every extreme that they name: `counts`: in every aligned block of 12 windows one window has exactly 256 live variates. `row_index`: each window's list names every slot once; its first counts[w] entries are the live slots.
All inputs are finite; a program needn't handle non-finite values.
Results may differ from the reference program's by a relative error of at most 0.019.
Values may be sent and summed in bfloat16 or wider, within the bound.
A program may use at most 384 MiB of HBM per device.

```python
import math
import jax
import jax.numpy as jnp
from jax import lax

D = 512
HEADS = 8
HD = 64
FF = 2048
LAYERS = 2
WIN_DEV = 12
L = 256
NWIN = 96
MOST = 256


def draw_counts(key, part):
    key = jax.random.fold_in(key, 7)
    first, second, fourth = jax.random.split(key, 3)
    span = MOST - 8
    upper = max(span, 1)
    left = jax.random.randint(first, (NWIN,), 0, span + 1)
    middle = jax.random.randint(second, (NWIN,), 0, span + 1)
    base = 8 + left * middle // upper
    chosen = jax.random.randint(fourth, (NWIN // WIN_DEV,), 0, WIN_DEV)
    marked = jnp.arange(NWIN, dtype=jnp.int32) % WIN_DEV == jnp.repeat(chosen, WIN_DEV)
    return jnp.where(marked, MOST, base).astype(jnp.int32)


def shard_levels(own_key, dims, cuts, least, largest):
    level, own = 1.0, jax.random.fold_in(own_key, 6)
    for dim, parts in cuts:
        steps = jnp.exp(jax.random.uniform(jax.random.fold_in(own, dim), (parts,), jnp.float32, least / len(cuts), largest / len(cuts)))
        level = level * jnp.repeat(steps, dims[dim] // parts).reshape([-1 if axis == dim else 1 for axis in range(len(dims))])
    return level


def centred(own_key, extent, scale, reach, cuts=(), held_as=jnp.bfloat16):
    values = scale * jax.random.normal(own_key, extent, jnp.float32)
    if cuts:
        values = values * shard_levels(own_key, extent, cuts, -0.22, 0.18)
    return jnp.clip(values, -reach, reach).astype(held_as)


def setup_inputs(seed: int = 0) -> dict:
    key_of = jax.random.split(jax.random.key(seed), 14)
    return {
        "inputs": centred(key_of[0], (NWIN, L, D), 1.0, 6.0, ((0, 8), (1, 4))),
        "counts": draw_counts(jax.random.fold_in(key_of[13], 71), 0),
        "row_index": jax.vmap(lambda own: jax.random.permutation(own, L))(jax.random.split(key_of[2], NWIN)).reshape((NWIN, L)).astype(jnp.int32),
        "w_qkv": centred(key_of[3], (LAYERS, D, 3 * D), D ** -0.5, 0.25),
        "bias_qv": centred(key_of[4], (LAYERS, 2 * D), 0.3, 2.0, (), jnp.float32),
        "w_attn_out": centred(key_of[5], (LAYERS, D, D), (D // 8) ** -0.5, 0.75),
        "out_bias": centred(key_of[6], (LAYERS, 2, D), 0.3, 2.0, (), jnp.float32),
        "w_in": centred(key_of[7], (LAYERS, D, FF), D ** -0.5, 0.25),
        "bias_in": centred(key_of[8], (LAYERS, FF), 0.3, 2.0, (), jnp.float32),
        "w_ffn_out": centred(key_of[9], (LAYERS, FF, D), FF ** -0.5, 0.125),
        "norm_gain": jnp.clip(1.0 + 0.1 * jax.random.normal(key_of[10], (LAYERS, 2, D), jnp.float32), 0.5, 1.5),
        "norm_bias": centred(key_of[11], (LAYERS, 2, D), 0.3, 2.0, (), jnp.float32),
        "cotangent": centred(key_of[12], (NWIN, L, D), 1.0, 6.0, ((0, 8), (1, 4))),
    }


EPS = 1e-05

@jax.custom_vjp
def low(v):
    return lax.optimization_barrier(v.astype(jnp.bfloat16)).astype(jnp.float32)

@jax.custom_vjp
def low_back(v):
    return v

def low_keep(v):
    return (low(v), None)

def low_pass(kept, grad):
    return (grad,)

def back_keep(v):
    return (v, None)

def back_low(kept, grad):
    return (low(grad),)
low.defvjp(low_keep, low_pass)
low_back.defvjp(back_keep, back_low)

def layer_norm(values, gain, shift):
    centre = values - lax.optimization_barrier(jnp.mean(values, axis=-1, keepdims=True))
    spread = lax.optimization_barrier(jnp.mean(centre * centre, axis=-1, keepdims=True))
    return centre * lax.rsqrt(spread + EPS) * gain + shift

def product(left, right):
    return jnp.einsum('gld,de->gle', left, right, precision=lax.Precision.HIGHEST)

def attend(query, keys, values, key_valid):
    groups, length, width = query.shape
    query_heads = query.reshape(groups, length, HEADS, HD)
    key_heads = keys.reshape(groups, length, HEADS, HD)
    value_heads = values.reshape(groups, length, HEADS, HD)
    scores = jnp.einsum('gqhd,gkhd->ghqk', query_heads, key_heads, precision=lax.Precision.HIGHEST) * HD ** (-0.5)
    scores = low_back(scores)
    scores = jnp.where(key_valid[:, None, None, :], scores, -1e+30)
    peak = lax.optimization_barrier(jnp.max(scores, axis=-1, keepdims=True))
    expo = jnp.exp(scores - peak)
    probs = low(expo / lax.optimization_barrier(jnp.sum(expo, axis=-1, keepdims=True)))
    mixed = jnp.einsum('ghqk,gkhd->gqhd', probs, value_heads, precision=lax.Precision.HIGHEST)
    return low(low_back(mixed.reshape(groups, length, width)))

def encoder_layer(state, layer_weights, key_valid):
    w_qkv, bias_qv, w_attn_out, out_bias, w_in, bias_in, w_ffn_out, norm_gain, norm_bias = layer_weights
    x_low = low(state)
    joint = product(x_low, w_qkv)
    query = low(low_back(joint[..., :D] + bias_qv[:D]))
    keys = low(low_back(joint[..., D:2 * D]))
    values = low(low_back(joint[..., 2 * D:] + bias_qv[D:]))
    mixed = attend(query, keys, values, key_valid)
    attn = low_back(product(mixed, w_attn_out) + out_bias[0])
    normed = layer_norm(state + attn, norm_gain[0], norm_bias[0])
    hidden = low_back(product(low(normed), w_in) + bias_in)
    active = low(jax.nn.gelu(hidden, approximate=True))
    ffn = low_back(product(active, w_ffn_out) + out_bias[1])
    return layer_norm(normed + ffn, norm_gain[1], norm_bias[1])

def reference(inputs, counts, row_index, w_qkv, bias_qv, w_attn_out, out_bias, w_in, bias_in, w_ffn_out, norm_gain, norm_bias, cotangent):
    slots = jnp.arange(L, dtype=jnp.int32)
    live = (slots[None, :] < counts[:, None]).astype(jnp.float32)
    window_ids = jnp.arange(NWIN, dtype=jnp.int32)[:, None]
    valid = jnp.zeros((NWIN, L), jnp.float32).at[window_ids, row_index].add(live)
    group = math.gcd(NWIN, max(1, 4096 // L))
    steps_count = NWIN // group
    weights = (w_qkv.astype(jnp.float32), bias_qv.astype(jnp.float32), w_attn_out.astype(jnp.float32), out_bias.astype(jnp.float32), w_in.astype(jnp.float32), bias_in.astype(jnp.float32), w_ffn_out.astype(jnp.float32), norm_gain.astype(jnp.float32), norm_bias.astype(jnp.float32))

    def forward(tokens, params):

        def one_group(carry, items):
            block_tokens, block_valid = items
            state = block_tokens
            for which_layer in range(LAYERS):
                layer_weights = tuple((entry[which_layer] for entry in params))
                state = encoder_layer(state, layer_weights, block_valid > 0.5)
            return (carry, state * block_valid[:, :, None])
        _, results = lax.scan(jax.checkpoint(one_group), None, (tokens.reshape(steps_count, group, L, D), valid.reshape(steps_count, group, L)))
        return results.reshape(NWIN, L, D)
    result, pullback = jax.vjp(forward, inputs.astype(jnp.float32), weights)
    grad_inputs, grads = pullback(cotangent.astype(jnp.float32))
    return (result.astype(jnp.bfloat16), grad_inputs, grads[0], grads[1], grads[2], grads[3], grads[4], grads[5], grads[6], grads[7], grads[8])
```

```python
import functools

import jax
import jax.numpy as jnp
from jax import lax
from jax.experimental import pallas as pl
from jax.experimental.pallas import tpu as pltpu
from jax.sharding import PartitionSpec as P

HEADS = 8
LAYERS = 2


EPS = 1e-05
LOW = jnp.bfloat16
F32 = jnp.float32
MESH = pl.DeviceIdType.MESH
VMEM_BYTES = 60 << 20
SMOOTH = 0.7978845608028654
CUBIC = 0.044715


def layer_norm(values, gain, shift):
    centre = values - jnp.mean(values, axis=-1, keepdims=True)
    spread = jnp.mean(centre * centre, axis=-1, keepdims=True)
    return centre * lax.rsqrt(spread + EPS) * gain + shift


def smooth(values):
    return jax.nn.gelu(values, approximate=True)


def scores_of(query_heads, key_heads, key_valid, scale):
    raw = (
        jnp.einsum("wqhd,wkhd->whqk", query_heads, key_heads, preferred_element_type=jnp.float32)
        * scale
    )
    return jnp.where(key_valid[:, None, None, :], raw, -1e30)


def per_device(
    inputs,
    counts,
    row_index,
    w_qkv,
    bias_qv,
    w_attn_out,
    out_bias,
    w_in,
    bias_in,
    w_ffn_out,
    norm_gain,
    norm_bias,
    cotangent,
):
    wins, rows, width = inputs.shape
    cycle_size = lax.axis_size("var")
    length = rows * cycle_size
    first_row = lax.axis_index("var") * rows
    head_count = HEADS
    head_size = width // head_count
    scale = head_size ** (-0.5)
    flat = wins * rows
    slots = jnp.arange(length, dtype=jnp.int32)
    live = (slots[None, :] < counts[:, None]).astype(jnp.float32)
    window_ids = jnp.arange(wins, dtype=jnp.int32)[:, None]
    valid = jnp.zeros((wins, length), jnp.float32).at[window_ids, row_index].add(live)
    key_valid = valid > 0.5
    own_valid = lax.dynamic_slice_in_dim(valid, first_row, rows, 1).reshape(flat, 1)
    state = inputs.astype(jnp.float32).reshape(flat, width)
    kept = []
    for which_layer in range(LAYERS):
        x_low = state.astype(jnp.bfloat16)
        joint = jnp.dot(x_low, w_qkv[which_layer], preferred_element_type=jnp.float32)
        query = (joint[:, :width] + bias_qv[which_layer, :width]).astype(jnp.bfloat16)
        keys_low = joint[:, width : 2 * width].astype(jnp.bfloat16)
        values_low = (joint[:, 2 * width :] + bias_qv[which_layer, width:]).astype(jnp.bfloat16)
        pair = jnp.concatenate([keys_low, values_low], axis=1).reshape(wins, rows, 2 * width)
        whole = lax.all_gather(pair, "var", axis=1, tiled=True)
        query_heads = query.reshape(wins, rows, head_count, head_size)
        key_heads = whole[:, :, :width].reshape(wins, length, head_count, head_size)
        value_heads = whole[:, :, width:].reshape(wins, length, head_count, head_size)
        scores = scores_of(query_heads, key_heads, key_valid, scale)
        peak = jnp.max(scores, axis=-1, keepdims=True)
        expo = jnp.exp(scores - peak)
        total = jnp.sum(expo, axis=-1, keepdims=True)
        probs = expo / total
        top = peak + jnp.log(total)
        mixed = (
            jnp.einsum(
                "whqk,wkhd->wqhd",
                probs.astype(jnp.bfloat16),
                value_heads,
                preferred_element_type=jnp.float32,
            )
            .reshape(flat, width)
            .astype(jnp.bfloat16)
        )
        attn = (
            jnp.dot(mixed, w_attn_out[which_layer], preferred_element_type=jnp.float32)
            + out_bias[which_layer, 0]
        )
        normed, norm_one = jax.vjp(
            layer_norm, state + attn, norm_gain[which_layer, 0], norm_bias[which_layer, 0]
        )
        normed_low = normed.astype(jnp.bfloat16)
        hidden = (
            jnp.dot(normed_low, w_in[which_layer], preferred_element_type=jnp.float32)
            + bias_in[which_layer]
        )
        active, gelu_back = jax.vjp(smooth, hidden)
        active_low = active.astype(jnp.bfloat16)
        ffn = (
            jnp.dot(active_low, w_ffn_out[which_layer], preferred_element_type=jnp.float32)
            + out_bias[which_layer, 1]
        )
        state, norm_two = jax.vjp(
            layer_norm, normed + ffn, norm_gain[which_layer, 1], norm_bias[which_layer, 1]
        )
        stored = whole
        kept.append(
            (
                x_low,
                query_heads,
                stored,
                top,
                mixed,
                norm_one,
                normed_low,
                gelu_back,
                active_low,
                norm_two,
            )
        )
    layer_out = (state * own_valid).astype(jnp.bfloat16).reshape(wins, rows, width)
    grad = cotangent.astype(jnp.float32).reshape(flat, width) * own_valid
    collected = []
    for which_layer in reversed(range(LAYERS)):
        (
            x_low,
            query_heads,
            stored,
            top,
            mixed,
            norm_one,
            normed_low,
            gelu_back,
            active_low,
            norm_two,
        ) = kept[which_layer]
        dz_two, gain_two, shift_two = norm_two(grad)
        d_ffn = dz_two.astype(jnp.bfloat16)
        g_ffn_out = jnp.einsum("rf,rd->fd", active_low, d_ffn, preferred_element_type=jnp.float32)
        bias_two = jnp.sum(d_ffn.astype(jnp.float32), axis=0)
        d_active = jnp.einsum(
            "rd,fd->rf", d_ffn, w_ffn_out[which_layer], preferred_element_type=jnp.float32
        )
        (d_hidden,) = gelu_back(d_active)
        d_hidden = d_hidden.astype(jnp.bfloat16)
        g_in = jnp.einsum("rd,rf->df", normed_low, d_hidden, preferred_element_type=jnp.float32)
        g_bias_in = jnp.sum(d_hidden.astype(jnp.float32), axis=0)
        d_normed = dz_two + jnp.einsum(
            "rf,df->rd", d_hidden, w_in[which_layer], preferred_element_type=jnp.float32
        )
        dz_one, gain_one, shift_one = norm_one(d_normed)
        d_attn = dz_one.astype(jnp.bfloat16)
        g_attn_out = jnp.einsum("re,rd->ed", mixed, d_attn, preferred_element_type=jnp.float32)
        bias_one = jnp.sum(d_attn.astype(jnp.float32), axis=0)
        d_mixed = jnp.einsum(
            "rd,ed->re", d_attn, w_attn_out[which_layer], preferred_element_type=jnp.float32
        ).astype(jnp.bfloat16)
        whole = stored
        key_heads = whole[:, :, :width].reshape(wins, length, head_count, head_size)
        value_heads = whole[:, :, width:].reshape(wins, length, head_count, head_size)
        scores = scores_of(query_heads, key_heads, key_valid, scale)
        probs = jnp.exp(scores - top)
        grad_heads = d_mixed.reshape(wins, rows, head_count, head_size)
        d_probs = jnp.einsum(
            "wqhd,wkhd->whqk", grad_heads, value_heads, preferred_element_type=jnp.float32
        )
        centre = jnp.sum(probs * d_probs, axis=-1, keepdims=True)
        d_scores = (probs * (d_probs - centre)).astype(jnp.bfloat16)
        probs_low = probs.astype(jnp.bfloat16)
        d_query = (
            jnp.einsum("whqk,wkhd->wqhd", d_scores, key_heads, preferred_element_type=jnp.float32)
            * scale
        )
        d_query = d_query.reshape(flat, width).astype(jnp.bfloat16)
        span_rows = lax.axis_size("var") * rows
        d_key = (
            jnp.einsum("whqk,wqhd->kwhd", d_scores, query_heads, preferred_element_type=jnp.float32)
            * scale
        )
        d_value = jnp.einsum(
            "whqk,wqhd->kwhd", probs_low, grad_heads, preferred_element_type=jnp.float32
        )
        key_grads = lax.psum_scatter(
            jnp.concatenate(
                [d_key.reshape(span_rows, wins, width), d_value.reshape(span_rows, wins, width)],
                axis=2,
            ).astype(jnp.bfloat16),
            "var",
            scatter_dimension=0,
            tiled=True,
        ).astype(jnp.float32)
        key_grads = (
            jnp.transpose(key_grads, (1, 0, 2)).reshape(flat, 2 * width).astype(jnp.bfloat16)
        )
        d_joint = jnp.concatenate([d_query, key_grads], axis=1)
        g_qkv = jnp.einsum("rd,re->de", x_low, d_joint, preferred_element_type=jnp.float32)
        g_bias_qv = jnp.concatenate(
            [
                jnp.sum(d_query.astype(jnp.float32), axis=0),
                jnp.sum(key_grads[:, width:].astype(jnp.float32), axis=0),
            ]
        )
        grad = dz_one + jnp.einsum(
            "re,de->rd", d_joint, w_qkv[which_layer], preferred_element_type=jnp.float32
        )
        g_out_bias = jnp.stack([bias_one, bias_two])
        g_gain = jnp.stack([gain_one, gain_two])
        g_shift = jnp.stack([shift_one, shift_two])
        terms = (
            g_qkv,
            g_bias_qv,
            g_attn_out,
            g_out_bias,
            g_in,
            g_bias_in,
            g_ffn_out,
            g_gain,
            g_shift,
        )
        collected.append(terms)
    collected = collected[::-1]
    stacked = tuple((jnp.stack([entry[position] for entry in collected]) for position in range(9)))
    shards = (
        lax.psum_scatter(
            stacked[0].astype(jnp.bfloat16), "var", scatter_dimension=1, tiled=True
        ).astype(jnp.float32),
        lax.psum_scatter(
            stacked[1].astype(jnp.bfloat16), "var", scatter_dimension=1, tiled=True
        ).astype(jnp.float32),
        lax.psum_scatter(
            stacked[2].astype(jnp.bfloat16), "var", scatter_dimension=1, tiled=True
        ).astype(jnp.float32),
        lax.psum_scatter(
            stacked[3].astype(jnp.bfloat16), "var", scatter_dimension=2, tiled=True
        ).astype(jnp.float32),
        lax.psum_scatter(
            stacked[4].astype(jnp.bfloat16), "var", scatter_dimension=1, tiled=True
        ).astype(jnp.float32),
        lax.psum_scatter(
            stacked[5].astype(jnp.bfloat16), "var", scatter_dimension=1, tiled=True
        ).astype(jnp.float32),
        lax.psum_scatter(
            stacked[6].astype(jnp.bfloat16), "var", scatter_dimension=1, tiled=True
        ).astype(jnp.float32),
        lax.psum_scatter(
            stacked[7].astype(jnp.bfloat16), "var", scatter_dimension=2, tiled=True
        ).astype(jnp.float32),
        lax.psum_scatter(
            stacked[8].astype(jnp.bfloat16), "var", scatter_dimension=2, tiled=True
        ).astype(jnp.float32),
    )
    stacked = (
        lax.psum(shards[0].astype(jnp.bfloat16), "win").astype(jnp.float32),
        lax.psum(shards[1].astype(jnp.bfloat16), "win").astype(jnp.float32),
        lax.psum(shards[2].astype(jnp.bfloat16), "win").astype(jnp.float32),
        lax.psum(shards[3].astype(jnp.bfloat16), "win").astype(jnp.float32),
        lax.psum(shards[4].astype(jnp.bfloat16), "win").astype(jnp.float32),
        lax.psum(shards[5].astype(jnp.bfloat16), "win").astype(jnp.float32),
        lax.psum(shards[6].astype(jnp.bfloat16), "win").astype(jnp.float32),
        lax.psum(shards[7].astype(jnp.bfloat16), "win").astype(jnp.float32),
        lax.psum(shards[8].astype(jnp.bfloat16), "win").astype(jnp.float32),
    )
    grad_inputs = grad.reshape(wins, rows, width)
    return (
        layer_out,
        grad_inputs,
        stacked[0],
        stacked[1],
        stacked[2],
        stacked[3],
        stacked[4],
        stacked[5],
        stacked[6],
        stacked[7],
        stacked[8],
    )


def dot(left, right, left_dim, right_dim):
    return lax.dot_general(
        left, right, (((left_dim,), (right_dim,)), ((), ())), preferred_element_type=F32
    )


def flip(index, bit):
    return index + bit - 2 * bit * lax.rem(index // bit, 2)


def half_of(index, bit):
    return lax.rem(index // bit, 2)


def partner(axis, bit):
    win, var = lax.axis_index("win"), lax.axis_index("var")
    if axis == "win":
        return (flip(win, bit), var)
    return (win, flip(var, bit))


def greet(partners):
    barrier = pltpu.get_barrier_semaphore()
    for other in partners:
        pl.semaphore_signal(barrier, inc=1, device_id=other, device_id_type=MESH)
    pl.semaphore_wait(barrier, len(partners))


def assign(counts, wins, owners):
    each = wins // owners
    keys = [counts[w] * wins + w for w in range(wins)]
    for stop in range(wins - 1, 0, -1):
        for low in range(stop):
            first, second = keys[low], keys[low + 1]
            keys[low], keys[low + 1] = jnp.maximum(first, second), jnp.minimum(first, second)
    load = [jnp.int32(0)] * owners
    held = [jnp.int32(0)] * owners
    slots, names = [], []
    for key in keys:
        count, name = key // wins, lax.rem(key, wins)
        best, which = load[0] + (held[0] // each) * 1000000, jnp.int32(0)
        for owner in range(1, owners):
            price = load[owner] + (held[owner] // each) * 1000000
            better = price < best
            best = jnp.where(better, price, best)
            which = jnp.where(better, owner, which)
        slot = jnp.int32(0)
        for owner in range(owners):
            mine = which == owner
            slot = jnp.where(mine, owner * each + held[owner], slot)
            load[owner] = jnp.where(mine, load[owner] + ((count + 15) // 16) * 16, load[owner])
            held[owner] = jnp.where(mine, held[owner] + 1, held[owner])
        slots.append(slot)
        names.append(name)
    order = []
    for place in range(wins):
        window = jnp.int32(0)
        for slot, name in zip(slots, names):
            window = jnp.where(slot == place, name, window)
        order.append(window)
    return order


def spread_kernel(
    owners, counts, x, g, x_out, g_out, meta, x_stage, g_stage, x_send, x_recv, g_send, g_recv, own_sem
):
    wins, rows = x.shape[0], x.shape[1]
    each = wins // owners
    me = lax.axis_index("var")
    others = [flip(me, 1), flip(me, 2), flip(flip(me, 1), 2)]
    win = lax.axis_index("win")
    barrier = pltpu.get_barrier_semaphore()
    for other in others:
        pl.semaphore_signal(barrier, inc=1, device_id=(win, other), device_id_type=MESH)
    order = assign(counts, wins, owners)
    for place in range(wins):
        meta[place] = order[place]
        x_stage[place] = x[order[place]]
    pl.semaphore_wait(barrier, len(others))

    def copies(stage, out, send, recv):
        sent = []
        for place, other in enumerate(others):
            sent.append(
                pltpu.make_async_remote_copy(
                    src_ref=stage.at[pl.ds(other * each, each)],
                    dst_ref=out.at[:, pl.ds(pl.multiple_of(me * rows, rows), rows), :],
                    send_sem=send.at[place],
                    recv_sem=recv.at[place],
                    device_id=(win, other),
                    device_id_type=MESH,
                )
            )
        return sent

    x_sent = copies(x_stage, x_out, x_send, x_recv)
    for copy in x_sent:
        copy.start()
    for place in range(wins):
        g_stage[place] = g[order[place]]
    g_sent = copies(g_stage, g_out, g_send, g_recv)
    for copy in g_sent:
        copy.start()
    own = pl.ds(pl.multiple_of(me * rows, rows), rows)
    own_x = pltpu.make_async_copy(
        x_stage.at[pl.ds(me * each, each)], x_out.at[:, own, :], own_sem.at[0]
    )
    own_g = pltpu.make_async_copy(
        g_stage.at[pl.ds(me * each, each)], g_out.at[:, own, :], own_sem.at[1]
    )
    own_x.start()
    own_g.start()
    total = jnp.int32(0)
    for place in range(each):
        name = jnp.int32(0)
        for owner in range(owners):
            name = jnp.where(me == owner, order[owner * each + place], name)
        meta[wins + place] = name
        meta[wins + each + place] = counts[name]
        total = total + ((counts[name] + 15) // 16) * 16
    meta[wins + 2 * each] = me
    meta[wins + 2 * each + 1] = total
    own_x.wait()
    own_g.wait()
    for copy in x_sent + g_sent:
        copy.wait()


class Plan:
    def __init__(self, meta, wins, each):
        self.names = [meta[wins + place] for place in range(each)]
        self.counts = [meta[wins + each + place] for place in range(each)]
        self.starts = []
        total = jnp.int32(0)
        for count in self.counts:
            self.starts.append(total)
            total = total + ((count + 15) // 16) * 16
        self.total = total
        self.tall = jnp.logical_or(jnp.logical_and(total > 256, total <= 384), total > 512)
        self.blocks = jnp.where(total <= 384, 1, 2)

    def each_block(self, body):
        for size in (256, 384):

            @pl.when(self.tall if size == 384 else jnp.logical_not(self.tall))
            def _(size=size):
                def step(block, carry):
                    body(size, block, pl.ds(pl.multiple_of(block * size, 128), size))
                    return carry

                lax.fori_loop(0, self.blocks, step, 0)

    def pick(self, values, window):
        chosen = values[0]
        for place in range(1, len(values)):
            chosen = jnp.where(window == place, values[place], chosen)
        return chosen

    def each_window(self, body):
        def step(window, carry):
            count = self.pick(self.counts, window)
            start = pl.multiple_of(self.pick(self.starts, window), 16)
            for size in (64, 128, 192, 256):

                @pl.when(jnp.logical_and(count <= size, count > size - 64))
                def _(size=size):
                    body(size, count, pl.ds(start, size))

            return carry

        lax.fori_loop(0, len(self.counts), step, 0)


def marks(row_index, name, count, length):
    listed = row_index[pl.ds(name, 1), :]
    slot = lax.broadcasted_iota(jnp.int32, (length, length), 0)
    place = lax.broadcasted_iota(jnp.int32, (length, length), 1)
    hit = jnp.logical_and(slot == listed, place < count)
    return jnp.where(hit, 1.0, 0.0).astype(LOW)


def mean_of(values):
    return jnp.mean(values, axis=-1, keepdims=True)


def normalize(values):
    centre = values - mean_of(values)
    inverse = lax.rsqrt(mean_of(centre * centre) + EPS)
    return centre * inverse, inverse


def normalize_back(grad, gain, normal, inverse):
    scaled = grad * gain
    return inverse * (scaled - mean_of(scaled) - normal * mean_of(scaled * normal))


def two_heads(pair, lane_low, lane_high):
    return jnp.concatenate([pair * lane_low, pair * lane_high], axis=0)


def lane_masks(lanes):
    lane = lax.broadcasted_iota(jnp.int32, (1, lanes), 1)
    low = jnp.where(lane < lanes // 2, 1.0, 0.0)
    return low.astype(LOW), (1.0 - low).astype(LOW)


def join_heads(stacked):
    size, lanes = stacked.shape[0] // 2, stacked.shape[1]
    lane = lax.broadcasted_iota(jnp.int32, (size, lanes), 1)
    return jnp.where(lane < lanes // 2, stacked[:size], stacked[size:])


def forward_kernel(
    meta, row_index, x, w_qkv, w_attn, w_in, w_out, bias_qv, out_bias, bias_in, gain, shift,
    lefts_out, qkv_out, slope_out, normal_out, inverse_out, top_out, layer_out,
    wv_qkv, wv_attn, wv_in, wv_out, lefts, qkv, slope, normal, inverse, top, state,
    weight_sem, out_sem,
):
    each, length, width = x.shape
    wins = row_index.shape[0]
    layers = w_qkv.shape[0]
    hidden_width = w_in.shape[2]
    pieces = hidden_width // width
    part = width // pieces
    plan = Plan(meta, wins, each)
    weights = ((w_qkv, wv_qkv), (w_attn, wv_attn), (w_in, wv_in), (w_out, wv_out))

    def fetch(layer, which):
        source, target = weights[which]
        return pltpu.make_async_copy(
            source.at[layer], target.at[layer], weight_sem.at[layer, which]
        )

    for layer in range(layers):
        for which in range(4):
            fetch(layer, which).start()

    state[...] = jnp.zeros_like(state)
    for layer in range(layers):
        lefts[layer, 1] = jnp.zeros(lefts.shape[2:], LOW)
        qkv[layer] = jnp.zeros(qkv.shape[1:], LOW)
    for place in range(each):
        hits = marks(row_index, plan.names[place], plan.counts[place], length)
        start = pl.multiple_of(plan.starts[place], 16)
        state[pl.ds(start, length), :] = dot(hits, x[place], 0, 0)

    kept = (
        (lefts, lefts_out, lambda ref, layer, rows: ref.at[layer, :, rows, :]),
        (qkv, qkv_out, lambda ref, layer, rows: ref.at[layer, rows, :]),
        (slope, slope_out, lambda ref, layer, rows: ref.at[layer, rows, :]),
        (normal, normal_out, lambda ref, layer, rows: ref.at[layer, :, rows, :]),
        (inverse, inverse_out, lambda ref, layer, rows: ref.at[layer, rows, :]),
        (top, top_out, lambda ref, layer, rows: ref.at[layer, rows, :]),
    )

    def stores(layer, block, rows):
        return [
            pltpu.make_async_copy(
                view(source, layer, rows), view(target, layer, rows), out_sem.at[layer, which, block]
            )
            for which, (source, target, view) in enumerate(kept)
        ]

    lane_low, lane_high = lane_masks(128)

    def one_layer(layer, carry):
        fetch(layer, 0).wait()

        def project(size, block, rows):
            tokens = state[rows, :].astype(LOW)
            lefts[layer, 0, rows, :] = tokens
            for which in range(3):
                columns = slice(which * width, (which + 1) * width)
                joint = dot(tokens, wv_qkv[layer, :, columns], 1, 0)
                if which == 0:
                    joint = (joint + bias_qv[pl.ds(layer, 1), :width]).astype(LOW) * LOW(0.125)
                elif which == 2:
                    joint = (joint + bias_qv[pl.ds(layer, 1), width:]).astype(LOW)
                else:
                    joint = joint.astype(LOW)
                qkv[layer, rows, columns] = joint

        plan.each_block(project)

        def attend(size, count, rows):
            column = lax.broadcasted_iota(jnp.int32, (2 * size, size), 1)
            live = column < count

            def pair(which, carry):
                at = pl.multiple_of(which * 128, 128)
                query = two_heads(qkv[layer, rows, pl.ds(at, 128)], lane_low, lane_high)
                key = qkv[layer, rows, pl.ds(pl.multiple_of(at + width, 128), 128)]
                value = qkv[layer, rows, pl.ds(pl.multiple_of(at + 2 * width, 128), 128)]
                scores = jnp.where(live, dot(query, key, 1, 1), -1e30)
                peak = jnp.max(scores, axis=-1, keepdims=True)
                expo = jnp.exp(scores - peak)
                total = jnp.sum(expo, axis=-1, keepdims=True)
                probs = (expo * (1.0 / total)).astype(LOW)
                lefts[layer, 1, rows, pl.ds(at, 128)] = join_heads(dot(probs, value, 1, 0)).astype(LOW)
                logs = jnp.broadcast_to(peak + jnp.log(total), (2 * size, 128))
                top[layer, rows, pl.ds(at, 128)] = join_heads(logs)
                return carry

            lax.fori_loop(0, width // 128, pair, 0)

        plan.each_window(attend)
        for which in range(1, 4):
            fetch(layer, which).wait()

        def feed(size, block, rows):
            first = dot(lefts[layer, 1, rows, :], wv_attn[layer], 1, 0) + out_bias[layer, 0:1, :]
            one, inverse_one = normalize(state[rows, :] + first)
            normal[layer, 0, rows, :] = one
            after = one * gain[layer, 0:1, :] + shift[layer, 0:1, :]
            after_low = after.astype(LOW)
            lefts[layer, 2, rows, :] = after_low
            second = jnp.zeros((size, width), F32)
            for piece in range(pieces):
                columns = slice(piece * width, (piece + 1) * width)
                hidden = dot(after_low, wv_in[layer, :, columns], 1, 0) + bias_in[pl.ds(layer, 1), columns]
                squared = hidden * hidden
                bend = jnp.tanh(SMOOTH * hidden * (1.0 + CUBIC * squared))
                half = 0.5 * (1.0 + bend)
                active = (hidden * half).astype(LOW)
                rise = half + 0.5 * hidden * (1.0 - bend * bend) * (
                    SMOOTH * (1.0 + 3.0 * CUBIC * squared)
                )
                slope[layer, rows, columns] = rise.astype(LOW)
                for sub in range(pieces):
                    lefts[layer, 3 + sub, rows, piece * part : (piece + 1) * part] = active[
                        :, sub * part : (sub + 1) * part
                    ]
                second = second + dot(active, wv_out[layer, columns, :], 1, 0)
            two, inverse_two = normalize(after + second + out_bias[layer, 1:2, :])
            normal[layer, 1, rows, :] = two
            state[rows, :] = two * gain[layer, 1:2, :] + shift[layer, 1:2, :]
            lane = lax.broadcasted_iota(jnp.int32, (size, 128), 1)
            inverse[layer, rows, :] = jnp.where(lane < 64, inverse_one, inverse_two)
            for copy in stores(layer, block, rows):
                copy.start()

        plan.each_block(feed)
        return carry

    lax.fori_loop(0, layers, one_layer, 0)
    for place in range(each):
        hits = marks(row_index, plan.names[place], plan.counts[place], length)
        start = pl.multiple_of(plan.starts[place], 16)
        layer_out[place] = dot(hits, state[pl.ds(start, length), :].astype(LOW), 1, 0).astype(LOW)

    for layer in range(layers):

        def finish(size, block, rows, layer=layer):
            for copy in stores(layer, block, rows):
                copy.wait()

        plan.each_block(finish)


def backward_kernel(
    meta, row_index, g, w_qkv, w_attn, w_in, w_out, gain,
    qkv_in, slope_in, normal_in, inverse_in, top_in,
    rights_out, grad_out, sums,
    wv_qkv, wv_attn, wv_in, wv_out, rights, qkv, slope, normal, inverse, top, state, mixed_grad,
    weight_sem, in_sem, out_sem,
):
    each, length, width = g.shape
    wins = row_index.shape[0]
    layers = w_qkv.shape[0]
    hidden_width = w_in.shape[2]
    pieces = hidden_width // width
    plan = Plan(meta, wins, each)
    weights = ((w_out, wv_out), (w_in, wv_in), (w_attn, wv_attn), (w_qkv, wv_qkv))

    def fetch(layer, which):
        source, target = weights[which]
        return pltpu.make_async_copy(
            source.at[layer], target.at[layer], weight_sem.at[layer, which]
        )

    kept = (
        (normal_in, normal, lambda ref, layer, rows: ref.at[layer, :, rows, :]),
        (inverse_in, inverse, lambda ref, layer, rows: ref.at[layer, rows, :]),
        (slope_in, slope, lambda ref, layer, rows: ref.at[layer, rows, :]),
        (qkv_in, qkv, lambda ref, layer, rows: ref.at[layer, rows, :]),
        (top_in, top, lambda ref, layer, rows: ref.at[layer, rows, :]),
    )

    def loads(layer, block, rows):
        return [
            pltpu.make_async_copy(
                view(source, layer, rows), view(target, layer, rows), in_sem.at[layer, which, block]
            )
            for which, (source, target, view) in enumerate(kept)
        ]

    for layer in range(layers):
        qkv[layer, 256:] = jnp.zeros((qkv.shape[1] - 256, qkv.shape[2]), LOW)
    for layer in reversed(range(layers)):

        def begin(size, block, rows, layer=layer):
            for copy in loads(layer, block, rows):
                copy.start()

        fetch(layer, 0).start()
        plan.each_block(begin)
        for which in range(1, 4):
            fetch(layer, which).start()

    state[...] = jnp.zeros_like(state)
    mixed_grad[...] = jnp.zeros_like(mixed_grad)
    sums[...] = jnp.zeros_like(sums)
    for layer in range(layers):
        rights[layer, 0:3] = jnp.zeros((3,) + rights.shape[2:], LOW)
    for place in range(each):
        hits = marks(row_index, plan.names[place], plan.counts[place], length)
        start = pl.multiple_of(plan.starts[place], 16)
        state[pl.ds(start, length), :] = dot(hits, g[place], 0, 0)

    lane_low, lane_high = lane_masks(128)

    def add_rows(layer, place, values):
        sums[layer, place : place + 1, :] += jnp.sum(values, axis=0, keepdims=True)

    def one_layer(step, carry):
        layer = layers - 1 - step
        for which in range(3):
            fetch(layer, which).wait()

        def feed(size, block, rows):
            for copy in loads(layer, block, rows):
                copy.wait()
            grad = state[rows, :]
            two = normal[layer, 1, rows, :]
            add_rows(layer, 9, grad * two)
            add_rows(layer, 11, grad)
            back = normalize_back(grad, gain[layer, 1:2, :], two, inverse[layer, rows, 64:65])
            back_low = back.astype(LOW)
            rights[layer, 8, rows, :] = back_low
            add_rows(layer, 3, back_low.astype(F32))
            for piece in range(pieces):
                columns = slice(piece * width, (piece + 1) * width)
                active = dot(back_low, wv_out[layer, columns, :], 1, 1)
                hidden = (active * slope[layer, rows, columns].astype(F32)).astype(LOW)
                rights[layer, 4 + piece, rows, :] = hidden
                add_rows(layer, 4 + piece, hidden.astype(F32))
                back = back + dot(hidden, wv_in[layer, :, columns], 1, 1)
            one = normal[layer, 0, rows, :]
            add_rows(layer, 8, back * one)
            add_rows(layer, 10, back)
            back = normalize_back(back, gain[layer, 0:1, :], one, inverse[layer, rows, 0:1])
            back_low = back.astype(LOW)
            rights[layer, 3, rows, :] = back_low
            add_rows(layer, 2, back_low.astype(F32))
            mixed_grad[rows, :] = dot(back_low, wv_attn[layer], 1, 1).astype(LOW)
            state[rows, :] = back

        plan.each_block(feed)

        def attend(size, count, rows):
            row = lax.broadcasted_iota(jnp.int32, (2 * size, size), 0)
            column = lax.broadcasted_iota(jnp.int32, (2 * size, size), 1)
            row = jnp.where(row < size, row, row - size)
            live = jnp.logical_and(column < count, row < count)

            def pair(which, carry):
                at = pl.multiple_of(which * 128, 128)
                query = two_heads(qkv[layer, rows, pl.ds(at, 128)], lane_low, lane_high)
                key = qkv[layer, rows, pl.ds(pl.multiple_of(at + width, 128), 128)]
                value = qkv[layer, rows, pl.ds(pl.multiple_of(at + 2 * width, 128), 128)]
                grad = two_heads(mixed_grad[rows, pl.ds(at, 128)], lane_low, lane_high)
                logs = top[layer, rows, pl.ds(at, 128)]
                logs = jnp.concatenate([logs[:, 0:1], logs[:, 64:65]], axis=0)
                probs = jnp.where(live, jnp.exp(dot(query, key, 1, 1) - logs), 0.0)
                d_probs = dot(grad, value, 1, 1)
                centre = jnp.sum(probs * d_probs, axis=-1, keepdims=True)
                d_scores = (probs * (d_probs - centre)).astype(LOW)
                d_query = join_heads(dot(d_scores, key, 1, 0)) * 0.125
                rights[layer, 0, rows, pl.ds(at, 128)] = d_query.astype(LOW)
                rights[layer, 1, rows, pl.ds(at, 128)] = dot(d_scores, query, 0, 0).astype(LOW)
                rights[layer, 2, rows, pl.ds(at, 128)] = dot(probs.astype(LOW), grad, 0, 0).astype(LOW)
                return carry

            lax.fori_loop(0, width // 128, pair, 0)

        plan.each_window(attend)
        fetch(layer, 3).wait()

        def project(size, block, rows):
            grad = state[rows, :]
            for which in range(3):
                columns = slice(which * width, (which + 1) * width)
                piece = rights[layer, which, rows, :]
                grad = grad + dot(piece, wv_qkv[layer, :, columns], 1, 1)
                if which != 1:
                    add_rows(layer, which // 2, piece.astype(F32))
            state[rows, :] = grad
            pltpu.make_async_copy(
                rights.at[layer, :, rows, :], rights_out.at[layer, :, rows, :], out_sem.at[layer, block]
            ).start()

        plan.each_block(project)
        return carry

    lax.fori_loop(0, layers, one_layer, 0)
    for place in range(each):
        hits = marks(row_index, plan.names[place], plan.counts[place], length)
        start = pl.multiple_of(plan.starts[place], 16)
        grad_out[place] = dot(hits, state[pl.ds(start, length), :].astype(LOW), 1, 0).astype(LOW)

    for layer in range(layers):

        def finish(size, block, rows, layer=layer):
            pltpu.make_async_copy(
                rights.at[layer, :, rows, :], rights_out.at[layer, :, rows, :], out_sem.at[layer, block]
            ).wait()

        plan.each_block(finish)


LAGS = (0, 1, 3, 4, 5, 6, 7, 8, 9)
ROUTE = (("var", 1), ("var", 2), ("win", 1), ("win", 2), ("win", 4))


def merge_kernel(
    owners, meta, lefts, rights, sums, layer_out, grad,
    merged, sums_out, layer_back, grad_back,
    left_in, right_in, part, got_core, hold_x, got_x, hold_y, got_y, hold_a, got_a, hold_b, got_b,
    whole, sums_hold, sums_got,
    in_sem, send_sem, recv_sem, out_sem, sums_send, sums_recv, back_send, back_recv, own_sem,
):
    chunks = merged.shape[0]
    layers = lefts.shape[0]
    per_layer = chunks // layers
    packed, width = left_in.shape[1], left_in.shape[2]
    part_rows = part.shape[3]
    each = layer_out.shape[0]
    rows = layer_back.shape[1]
    win, var = lax.axis_index("win"), lax.axis_index("var")
    core, x_half = half_of(var, 1), half_of(var, 2)
    y_half, a_half, b_half = half_of(win, 1), half_of(win, 2), half_of(win, 4)
    others = [flip(var, 1), flip(var, 2), flip(flip(var, 1), 2)]
    route = [partner(axis, bit) for axis, bit in ROUTE]
    greet(route + [(win, others[2])])
    total = meta[meta.shape[0] - 1]

    def block_of(chunk):
        layer, place = layers - 1 - chunk // per_layer, lax.rem(chunk, per_layer)
        late = (place + 4) // 8
        far = place // 8
        left = (1 - late) * (place // 3) + late * (2 + far * (lax.rem(place, 8) + 1))
        right = place - far * lax.rem(place, 8)
        return layer, left, right

    def loads(chunk):
        layer, left, right = block_of(chunk)
        slot = lax.rem(chunk, 2)
        return (
            pltpu.make_async_copy(lefts.at[layer, left], left_in.at[slot], in_sem.at[0, slot]),
            pltpu.make_async_copy(rights.at[layer, right], right_in.at[slot], in_sem.at[1, slot]),
        )

    quarter = part_rows // 2
    eighth = quarter // 2
    sixteenth = eighth // 2
    at_y = pl.multiple_of(y_half * quarter, sixteenth)
    at_a = pl.multiple_of(at_y + a_half * eighth, sixteenth)
    at_b = pl.multiple_of(at_a + b_half * sixteenth, sixteenth)

    def exchange(stage, chunk):
        if stage == 0:
            source, target = part.at[chunk, 1 - core], got_core.at[chunk]
        elif stage == 1:
            source, target = hold_x.at[chunk, 1 - x_half], got_x.at[chunk]
        elif stage == 2:
            source, target = hold_y.at[chunk, 1 - y_half], got_y.at[chunk]
        elif stage == 3:
            source, target = hold_a.at[chunk, 1 - a_half], got_a.at[chunk]
        elif stage == 4:
            source, target = hold_b.at[chunk, 1 - b_half], got_b.at[chunk]
        else:
            at, size = ((at_b, sixteenth), (at_a, eighth), (at_y, quarter))[stage - 5]
            source = whole.at[chunk, pl.ds(at, size), :]
            target = source
        return pltpu.make_async_remote_copy(
            src_ref=source,
            dst_ref=target,
            send_sem=send_sem.at[stage, chunk],
            recv_sem=recv_sem.at[stage, chunk],
            device_id=route[(0, 1, 2, 3, 4, 4, 3, 2)[stage]],
            device_id_type=MESH,
        )

    def out_copy(chunk):
        return pltpu.make_async_copy(whole.at[chunk], merged.at[chunk], out_sem.at[chunk])

    def produce(chunk):
        for copy in loads(chunk):
            copy.wait()
        slot = lax.rem(chunk, 2)
        live = lax.broadcasted_iota(jnp.int32, (packed, width), 0) < total
        left = jnp.where(live, left_in[slot], LOW(0))
        right = jnp.where(live, right_in[slot], LOW(0))
        product = dot(left, right, 0, 0).astype(LOW)
        for shard in range(owners):
            part[chunk, shard % 2, shard // 2] = product[shard * part_rows : (shard + 1) * part_rows]
        exchange(0, chunk).start()

    def add(mine, theirs):
        return (mine.astype(F32) + theirs.astype(F32)).astype(LOW)

    def take(stage, chunk):
        exchange(stage - 1, chunk).wait_recv()
        if stage == 1:
            hold_x[chunk] = add(part[chunk, core], got_core[chunk])
        elif stage == 2:
            hold_y[chunk] = add(hold_x[chunk, x_half], got_x[chunk]).reshape(hold_y.shape[1:])
        elif stage == 3:
            hold_a[chunk] = add(hold_y[chunk, y_half], got_y[chunk]).reshape(hold_a.shape[1:])
        elif stage == 4:
            hold_b[chunk] = add(hold_a[chunk, a_half], got_a[chunk]).reshape(hold_b.shape[1:])
        elif stage == 5:
            whole[chunk, pl.ds(at_b, sixteenth), :] = add(hold_b[chunk, b_half], got_b[chunk])
        if stage < 8:
            exchange(stage, chunk).start()
        else:
            out_copy(chunk).start()

    def sums_exchange(turn):
        return pltpu.make_async_remote_copy(
            src_ref=sums_hold.at[turn],
            dst_ref=sums_got.at[turn],
            send_sem=sums_send.at[turn],
            recv_sem=sums_recv.at[turn],
            device_id=route[turn],
            device_id_type=MESH,
        )

    def back_copies():
        sent = []
        for which, (source, target) in enumerate(((grad, grad_back), (layer_out, layer_back))):
            for place, other in enumerate(others):
                sent.append(
                    pltpu.make_async_remote_copy(
                        src_ref=source.at[:, pl.ds(pl.multiple_of(other * rows, rows), rows), :],
                        dst_ref=target.at[pl.ds(var * each, each)],
                        send_sem=back_send.at[which, place],
                        recv_sem=back_recv.at[which, place],
                        device_id=(win, other),
                        device_id_type=MESH,
                    )
                )
        return sent

    def own_copies():
        return [
            pltpu.make_async_copy(
                source.at[:, pl.ds(pl.multiple_of(var * rows, rows), rows), :],
                target.at[pl.ds(var * each, each)],
                own_sem.at[which],
            )
            for which, (source, target) in enumerate(((grad, grad_back), (layer_out, layer_back)))
        ]

    for copy in loads(0):
        copy.start()
    for copy in own_copies():
        copy.start()
    sums_hold[0] = sums[...]
    sums_exchange(0).start()

    def step(now, carry):
        @pl.when(now + 1 < chunks)
        def _():
            for copy in loads(now + 1):
                copy.start()

        @pl.when(now < chunks)
        def _():
            produce(now)

        for stage in range(1, 9):
            lag = LAGS[stage]

            @pl.when(jnp.logical_and(now >= lag, now < chunks + lag))
            def _(stage=stage, lag=lag):
                take(stage, now - lag)

        for turn in range(5):

            @pl.when(now == 2 * turn + 4)
            def _(turn=turn):
                sums_exchange(turn).wait_recv()
                summed = sums_hold[turn] + sums_got[turn]
                if turn < 4:
                    sums_hold[turn + 1] = summed
                    sums_exchange(turn + 1).start()
                else:
                    sums_out[...] = summed

        @pl.when(now == chunks + 1)
        def _():
            for copy in back_copies():
                copy.start()

        return carry

    lax.fori_loop(0, chunks + LAGS[8], step, 0)

    def settle(chunk, carry):
        for stage in range(8):
            exchange(stage, chunk).wait_send()
        out_copy(chunk).wait()
        return carry

    lax.fori_loop(0, chunks, settle, 0)
    for turn in range(5):
        sums_exchange(turn).wait_send()
    for copy in own_copies():
        copy.wait()
    for copy in back_copies():
        copy.wait()


def finish_kernel(
    meta, merged, sums, layer_back, grad_back,
    layer_out, grad_inputs, qkv, bias_qv, attn, out_bias, in_, bias_in, out, gain, shift,
):
    wins = layer_back.shape[0]
    layers, width = qkv.shape[0], merged.shape[2]
    part_rows = merged.shape[1]
    per_layer = merged.shape[0] // layers
    var = meta[meta.shape[0] - 2]
    for place in range(wins):
        window = meta[place]
        layer_out[window] = layer_back[place]
        grad_inputs[window] = grad_back[place].astype(F32)
    narrow = out_bias.shape[2]
    at = pl.multiple_of(var * narrow, narrow)
    wide = bias_qv.shape[1]
    for layer in range(layers):
        base = (layers - 1 - layer) * per_layer
        for which in range(3):
            qkv[layer, :, which * width : (which + 1) * width] = merged[base + which].astype(F32)
        attn[layer] = merged[base + 3].astype(F32)
        for which in range(4):
            in_[layer, :, which * width : (which + 1) * width] = merged[base + 4 + which].astype(F32)
            out[layer, which * part_rows : (which + 1) * part_rows, :] = merged[base + 8 + which].astype(F32)
        half = width // wide
        bias_qv[layer : layer + 1, :] = sums[
            layer, pl.ds(var // half, 1), pl.ds(pl.multiple_of(lax.rem(var, half) * wide, wide), wide)
        ]
        bias_in[layer : layer + 1, :] = sums[layer, pl.ds(4 + var, 1), :]
        out_bias[layer] = sums[layer, 2:4, pl.ds(at, narrow)]
        gain[layer] = sums[layer, 8:10, pl.ds(at, narrow)]
        shift[layer] = sums[layer, 10:12, pl.ds(at, narrow)]


def in_vmem(count):
    return [pl.BlockSpec(memory_space=pltpu.VMEM)] * count


def anywhere(count):
    return [pl.BlockSpec(memory_space=pl.ANY)] * count


def in_smem():
    return [pl.BlockSpec(memory_space=pltpu.SMEM)]


def shaped(shape, kind=LOW):
    return jax.ShapeDtypeStruct(shape, kind)


def whole_windows(
    inputs, counts, row_index, w_qkv, bias_qv, w_attn_out, out_bias, w_in, bias_in, w_ffn_out,
    norm_gain, norm_bias, cotangent,
):
    wins, rows, width = inputs.shape
    owners, groups = lax.axis_size("var"), lax.axis_size("win")
    each, length = wins // owners, rows * owners
    packed = each * length
    layers, hidden_width = w_in.shape[0], w_in.shape[2]
    dma = pltpu.SemaphoreType.DMA

    def params(**more):
        return pltpu.CompilerParams(vmem_limit_bytes=VMEM_BYTES, **more)

    x, g, meta = pl.pallas_call(
        functools.partial(spread_kernel, owners),
        name="spread",
        out_shape=[shaped((each, length, width))] * 2 + [shaped((wins + 2 * each + 2,), jnp.int32)],
        in_specs=in_smem() + in_vmem(2),
        out_specs=anywhere(2) + in_smem(),
        scratch_shapes=[pltpu.VMEM((wins, rows, width), LOW)] * 2 + [dma((owners - 1,))] * 4 + [dma((2,))],
        compiler_params=params(collective_id=0, has_side_effects=True),
    )(counts, inputs, cotangent)

    weights = (w_qkv, w_attn_out, w_in, w_ffn_out)
    weight_space = [pltpu.VMEM(weight.shape, LOW) for weight in weights]
    kept = [
        shaped((layers, packed, 3 * width)),
        shaped((layers, packed, hidden_width)),
        shaped((layers, 2, packed, width), F32),
        shaped((layers, packed, 128), F32),
        shaped((layers, packed, width), F32),
    ]
    kept_space = [pltpu.VMEM(entry.shape, entry.dtype) for entry in kept]
    lefts_shape = shaped((layers, 7, packed, width))
    lefts, *stash, layer_rows = pl.pallas_call(
        forward_kernel,
        name="forward",
        out_shape=[lefts_shape] + kept + [shaped((each, length, width))],
        in_specs=in_smem() + in_vmem(2) + anywhere(4) + in_vmem(5),
        out_specs=anywhere(6) + in_vmem(1),
        scratch_shapes=weight_space
        + [pltpu.VMEM(lefts_shape.shape, LOW)]
        + kept_space
        + [pltpu.VMEM((packed, width), F32), dma((layers, 4)), dma((layers, 6, 2))],
        compiler_params=params(),
    )(meta, row_index, x, *weights, bias_qv, out_bias, bias_in, norm_gain, norm_bias)

    rights_shape = shaped((layers, 9, packed, width))
    rights, grad_rows, sums = pl.pallas_call(
        backward_kernel,
        name="backward",
        out_shape=[rights_shape, shaped((each, length, width)), shaped((layers, 16, width), F32)],
        in_specs=in_smem() + in_vmem(2) + anywhere(4) + in_vmem(1) + anywhere(5),
        out_specs=anywhere(1) + in_vmem(2),
        scratch_shapes=weight_space
        + [pltpu.VMEM(rights_shape.shape, LOW)]
        + kept_space
        + [
            pltpu.VMEM((packed, width), F32),
            pltpu.VMEM((packed, width), LOW),
            dma((layers, 4)),
            dma((layers, 5, 2)),
            dma((layers, 2)),
        ],
        compiler_params=params(),
    )(meta, row_index, g, *weights, norm_gain, *stash)

    chunks = layers * 12
    part_rows = width // owners
    half, quarter, eighth = part_rows // 2, part_rows // 4, part_rows // 8

    def space(*shape):
        return pltpu.VMEM((chunks,) + shape + (width,), LOW)

    merged, sums, layer_back, grad_back = pl.pallas_call(
        functools.partial(merge_kernel, owners),
        name="merge",
        out_shape=[
            shaped((chunks, part_rows, width)),
            shaped(sums.shape, F32),
            shaped((wins, rows, width)),
            shaped((wins, rows, width)),
        ],
        in_specs=in_smem() + anywhere(2) + in_vmem(3),
        out_specs=anywhere(1) + in_vmem(1) + anywhere(2),
        scratch_shapes=[pltpu.VMEM((2, packed, width), LOW)] * 2
        + [
            space(2, 2, part_rows),
            space(2, part_rows),
            space(2, part_rows),
            space(part_rows),
            space(2, half),
            space(half),
            space(2, quarter),
            space(quarter),
            space(2, eighth),
            space(eighth),
            space(part_rows),
        ]
        + [pltpu.VMEM((5,) + sums.shape, F32)] * 2
        + [dma((2, 2)), dma((8, chunks)), dma((8, chunks)), dma((chunks,))]
        + [dma((5,))] * 2
        + [dma((2, owners - 1))] * 2
        + [dma((2,))],
        compiler_params=params(collective_id=1, has_side_effects=True),
    )(meta, lefts, rights, sums, layer_rows, grad_rows)

    narrow = width // owners
    return pl.pallas_call(
        finish_kernel,
        name="finish",
        out_shape=[
            shaped((wins, rows, width)),
            shaped((wins, rows, width), F32),
            shaped((layers, narrow, 3 * width), F32),
            shaped((layers, 2 * narrow), F32),
            shaped((layers, narrow, width), F32),
            shaped((layers, 2, narrow), F32),
            shaped((layers, narrow, hidden_width), F32),
            shaped((layers, hidden_width // owners), F32),
            shaped((layers, hidden_width // owners, width), F32),
            shaped((layers, 2, narrow), F32),
            shaped((layers, 2, narrow), F32),
        ],
        in_specs=in_smem() + in_vmem(4),
        out_specs=in_vmem(11),
        compiler_params=params(),
    )(meta, merged, sums, layer_back, grad_back)


def choose(*arrays):
    wins, rows, width = arrays[0].shape
    owners, groups = lax.axis_size("var"), lax.axis_size("win")
    fits = owners == 4 and groups == 8 and wins % owners == 0 and rows % 16 == 0
    fits = fits and (wins // owners, rows * owners, width, arrays[7].shape[2]) == (3, 256, 512, 2048)
    return whole_windows(*arrays) if fits else per_device(*arrays)


def solution(mesh):
    return jax.shard_map(
        choose,
        mesh=mesh,
        in_specs=(
            P("win", "var", None),
            P("win"),
            P("win", None),
            P(),
            P(),
            P(),
            P(),
            P(),
            P(),
            P(),
            P(),
            P(),
            P("win", "var", None),
        ),
        out_specs=(
            P("win", "var", None),
            P("win", "var", None),
            P(None, "var", None),
            P(None, "var"),
            P(None, "var", None),
            P(None, None, "var"),
            P(None, "var", None),
            P(None, "var"),
            P(None, "var", None),
            P(None, None, "var"),
            P(None, None, "var"),
        ),
        check_vma=False,
    )
```

```python
import functools

import jax
import jax.numpy as jnp
from jax import lax
from jax.experimental import pallas as pl
from jax.experimental.pallas import tpu as pltpu
from jax.sharding import PartitionSpec as P

HEADS = 8
LAYERS = 2


EPS = 1e-05
LOW = jnp.bfloat16
F32 = jnp.float32
MESH = pl.DeviceIdType.MESH
VMEM_BYTES = 60 << 20
PACKED = 384
SMOOTH = 0.7978845608028654
CUBIC = 0.044715


def layer_norm(values, gain, shift):
    centre = values - jnp.mean(values, axis=-1, keepdims=True)
    spread = jnp.mean(centre * centre, axis=-1, keepdims=True)
    return centre * lax.rsqrt(spread + EPS) * gain + shift


def smooth(values):
    return jax.nn.gelu(values, approximate=True)


def scores_of(query_heads, key_heads, key_valid, scale):
    raw = (
        jnp.einsum("wqhd,wkhd->whqk", query_heads, key_heads, preferred_element_type=jnp.float32)
        * scale
    )
    return jnp.where(key_valid[:, None, None, :], raw, -1e30)


def per_device(
    inputs,
    counts,
    row_index,
    w_qkv,
    bias_qv,
    w_attn_out,
    out_bias,
    w_in,
    bias_in,
    w_ffn_out,
    norm_gain,
    norm_bias,
    cotangent,
):
    wins, rows, width = inputs.shape
    cycle_size = lax.axis_size("var")
    length = rows * cycle_size
    first_row = lax.axis_index("var") * rows
    head_count = HEADS
    head_size = width // head_count
    scale = head_size ** (-0.5)
    flat = wins * rows
    slots = jnp.arange(length, dtype=jnp.int32)
    live = (slots[None, :] < counts[:, None]).astype(jnp.float32)
    window_ids = jnp.arange(wins, dtype=jnp.int32)[:, None]
    valid = jnp.zeros((wins, length), jnp.float32).at[window_ids, row_index].add(live)
    key_valid = valid > 0.5
    own_valid = lax.dynamic_slice_in_dim(valid, first_row, rows, 1).reshape(flat, 1)
    state = inputs.astype(jnp.float32).reshape(flat, width)
    kept = []
    for which_layer in range(LAYERS):
        x_low = state.astype(jnp.bfloat16)
        joint = jnp.dot(x_low, w_qkv[which_layer], preferred_element_type=jnp.float32)
        query = (joint[:, :width] + bias_qv[which_layer, :width]).astype(jnp.bfloat16)
        keys_low = joint[:, width : 2 * width].astype(jnp.bfloat16)
        values_low = (joint[:, 2 * width :] + bias_qv[which_layer, width:]).astype(jnp.bfloat16)
        pair = jnp.concatenate([keys_low, values_low], axis=1).reshape(wins, rows, 2 * width)
        whole = lax.all_gather(pair, "var", axis=1, tiled=True)
        query_heads = query.reshape(wins, rows, head_count, head_size)
        key_heads = whole[:, :, :width].reshape(wins, length, head_count, head_size)
        value_heads = whole[:, :, width:].reshape(wins, length, head_count, head_size)
        scores = scores_of(query_heads, key_heads, key_valid, scale)
        peak = jnp.max(scores, axis=-1, keepdims=True)
        expo = jnp.exp(scores - peak)
        total = jnp.sum(expo, axis=-1, keepdims=True)
        probs = expo / total
        top = peak + jnp.log(total)
        mixed = (
            jnp.einsum(
                "whqk,wkhd->wqhd",
                probs.astype(jnp.bfloat16),
                value_heads,
                preferred_element_type=jnp.float32,
            )
            .reshape(flat, width)
            .astype(jnp.bfloat16)
        )
        attn = (
            jnp.dot(mixed, w_attn_out[which_layer], preferred_element_type=jnp.float32)
            + out_bias[which_layer, 0]
        )
        normed, norm_one = jax.vjp(
            layer_norm, state + attn, norm_gain[which_layer, 0], norm_bias[which_layer, 0]
        )
        normed_low = normed.astype(jnp.bfloat16)
        hidden = (
            jnp.dot(normed_low, w_in[which_layer], preferred_element_type=jnp.float32)
            + bias_in[which_layer]
        )
        active, gelu_back = jax.vjp(smooth, hidden)
        active_low = active.astype(jnp.bfloat16)
        ffn = (
            jnp.dot(active_low, w_ffn_out[which_layer], preferred_element_type=jnp.float32)
            + out_bias[which_layer, 1]
        )
        state, norm_two = jax.vjp(
            layer_norm, normed + ffn, norm_gain[which_layer, 1], norm_bias[which_layer, 1]
        )
        stored = whole
        kept.append(
            (
                x_low,
                query_heads,
                stored,
                top,
                mixed,
                norm_one,
                normed_low,
                gelu_back,
                active_low,
                norm_two,
            )
        )
    layer_out = (state * own_valid).astype(jnp.bfloat16).reshape(wins, rows, width)
    grad = cotangent.astype(jnp.float32).reshape(flat, width) * own_valid
    collected = []
    for which_layer in reversed(range(LAYERS)):
        (
            x_low,
            query_heads,
            stored,
            top,
            mixed,
            norm_one,
            normed_low,
            gelu_back,
            active_low,
            norm_two,
        ) = kept[which_layer]
        dz_two, gain_two, shift_two = norm_two(grad)
        d_ffn = dz_two.astype(jnp.bfloat16)
        g_ffn_out = jnp.einsum("rf,rd->fd", active_low, d_ffn, preferred_element_type=jnp.float32)
        bias_two = jnp.sum(d_ffn.astype(jnp.float32), axis=0)
        d_active = jnp.einsum(
            "rd,fd->rf", d_ffn, w_ffn_out[which_layer], preferred_element_type=jnp.float32
        )
        (d_hidden,) = gelu_back(d_active)
        d_hidden = d_hidden.astype(jnp.bfloat16)
        g_in = jnp.einsum("rd,rf->df", normed_low, d_hidden, preferred_element_type=jnp.float32)
        g_bias_in = jnp.sum(d_hidden.astype(jnp.float32), axis=0)
        d_normed = dz_two + jnp.einsum(
            "rf,df->rd", d_hidden, w_in[which_layer], preferred_element_type=jnp.float32
        )
        dz_one, gain_one, shift_one = norm_one(d_normed)
        d_attn = dz_one.astype(jnp.bfloat16)
        g_attn_out = jnp.einsum("re,rd->ed", mixed, d_attn, preferred_element_type=jnp.float32)
        bias_one = jnp.sum(d_attn.astype(jnp.float32), axis=0)
        d_mixed = jnp.einsum(
            "rd,ed->re", d_attn, w_attn_out[which_layer], preferred_element_type=jnp.float32
        ).astype(jnp.bfloat16)
        whole = stored
        key_heads = whole[:, :, :width].reshape(wins, length, head_count, head_size)
        value_heads = whole[:, :, width:].reshape(wins, length, head_count, head_size)
        scores = scores_of(query_heads, key_heads, key_valid, scale)
        probs = jnp.exp(scores - top)
        grad_heads = d_mixed.reshape(wins, rows, head_count, head_size)
        d_probs = jnp.einsum(
            "wqhd,wkhd->whqk", grad_heads, value_heads, preferred_element_type=jnp.float32
        )
        centre = jnp.sum(probs * d_probs, axis=-1, keepdims=True)
        d_scores = (probs * (d_probs - centre)).astype(jnp.bfloat16)
        probs_low = probs.astype(jnp.bfloat16)
        d_query = (
            jnp.einsum("whqk,wkhd->wqhd", d_scores, key_heads, preferred_element_type=jnp.float32)
            * scale
        )
        d_query = d_query.reshape(flat, width).astype(jnp.bfloat16)
        span_rows = lax.axis_size("var") * rows
        d_key = (
            jnp.einsum("whqk,wqhd->kwhd", d_scores, query_heads, preferred_element_type=jnp.float32)
            * scale
        )
        d_value = jnp.einsum(
            "whqk,wqhd->kwhd", probs_low, grad_heads, preferred_element_type=jnp.float32
        )
        key_grads = lax.psum_scatter(
            jnp.concatenate(
                [d_key.reshape(span_rows, wins, width), d_value.reshape(span_rows, wins, width)],
                axis=2,
            ).astype(jnp.bfloat16),
            "var",
            scatter_dimension=0,
            tiled=True,
        ).astype(jnp.float32)
        key_grads = (
            jnp.transpose(key_grads, (1, 0, 2)).reshape(flat, 2 * width).astype(jnp.bfloat16)
        )
        d_joint = jnp.concatenate([d_query, key_grads], axis=1)
        g_qkv = jnp.einsum("rd,re->de", x_low, d_joint, preferred_element_type=jnp.float32)
        g_bias_qv = jnp.concatenate(
            [
                jnp.sum(d_query.astype(jnp.float32), axis=0),
                jnp.sum(key_grads[:, width:].astype(jnp.float32), axis=0),
            ]
        )
        grad = dz_one + jnp.einsum(
            "re,de->rd", d_joint, w_qkv[which_layer], preferred_element_type=jnp.float32
        )
        g_out_bias = jnp.stack([bias_one, bias_two])
        g_gain = jnp.stack([gain_one, gain_two])
        g_shift = jnp.stack([shift_one, shift_two])
        terms = (
            g_qkv,
            g_bias_qv,
            g_attn_out,
            g_out_bias,
            g_in,
            g_bias_in,
            g_ffn_out,
            g_gain,
            g_shift,
        )
        collected.append(terms)
    collected = collected[::-1]
    stacked = tuple((jnp.stack([entry[position] for entry in collected]) for position in range(9)))
    shards = (
        lax.psum_scatter(
            stacked[0].astype(jnp.bfloat16), "var", scatter_dimension=1, tiled=True
        ).astype(jnp.float32),
        lax.psum_scatter(
            stacked[1].astype(jnp.bfloat16), "var", scatter_dimension=1, tiled=True
        ).astype(jnp.float32),
        lax.psum_scatter(
            stacked[2].astype(jnp.bfloat16), "var", scatter_dimension=1, tiled=True
        ).astype(jnp.float32),
        lax.psum_scatter(
            stacked[3].astype(jnp.bfloat16), "var", scatter_dimension=2, tiled=True
        ).astype(jnp.float32),
        lax.psum_scatter(
            stacked[4].astype(jnp.bfloat16), "var", scatter_dimension=1, tiled=True
        ).astype(jnp.float32),
        lax.psum_scatter(
            stacked[5].astype(jnp.bfloat16), "var", scatter_dimension=1, tiled=True
        ).astype(jnp.float32),
        lax.psum_scatter(
            stacked[6].astype(jnp.bfloat16), "var", scatter_dimension=1, tiled=True
        ).astype(jnp.float32),
        lax.psum_scatter(
            stacked[7].astype(jnp.bfloat16), "var", scatter_dimension=2, tiled=True
        ).astype(jnp.float32),
        lax.psum_scatter(
            stacked[8].astype(jnp.bfloat16), "var", scatter_dimension=2, tiled=True
        ).astype(jnp.float32),
    )
    stacked = (
        lax.psum(shards[0].astype(jnp.bfloat16), "win").astype(jnp.float32),
        lax.psum(shards[1].astype(jnp.bfloat16), "win").astype(jnp.float32),
        lax.psum(shards[2].astype(jnp.bfloat16), "win").astype(jnp.float32),
        lax.psum(shards[3].astype(jnp.bfloat16), "win").astype(jnp.float32),
        lax.psum(shards[4].astype(jnp.bfloat16), "win").astype(jnp.float32),
        lax.psum(shards[5].astype(jnp.bfloat16), "win").astype(jnp.float32),
        lax.psum(shards[6].astype(jnp.bfloat16), "win").astype(jnp.float32),
        lax.psum(shards[7].astype(jnp.bfloat16), "win").astype(jnp.float32),
        lax.psum(shards[8].astype(jnp.bfloat16), "win").astype(jnp.float32),
    )
    grad_inputs = grad.reshape(wins, rows, width)
    return (
        layer_out,
        grad_inputs,
        stacked[0],
        stacked[1],
        stacked[2],
        stacked[3],
        stacked[4],
        stacked[5],
        stacked[6],
        stacked[7],
        stacked[8],
    )


def dot(left, right, left_dim, right_dim):
    return lax.dot_general(
        left, right, (((left_dim,), (right_dim,)), ((), ())), preferred_element_type=F32
    )


def flip(index, bit):
    return index + bit - 2 * bit * lax.rem(index // bit, 2)


def half_of(index, bit):
    return lax.rem(index // bit, 2)


def partner(axis, bit):
    win, var = lax.axis_index("win"), lax.axis_index("var")
    if axis == "win":
        return (flip(win, bit), var)
    return (win, flip(var, bit))


def greet(partners):
    barrier = pltpu.get_barrier_semaphore()
    for other in partners:
        pl.semaphore_signal(barrier, inc=1, device_id=other, device_id_type=MESH)
    pl.semaphore_wait(barrier, len(partners))


def assign(counts, wins, owners):
    each = wins // owners
    keys = [counts[w] * wins + w for w in range(wins)]
    for stop in range(wins - 1, 0, -1):
        for low in range(stop):
            first, second = keys[low], keys[low + 1]
            keys[low], keys[low + 1] = jnp.maximum(first, second), jnp.minimum(first, second)
    load = [jnp.int32(0)] * owners
    held = [jnp.int32(0)] * owners
    slots, names = [], []
    for key in keys:
        count, name = key // wins, lax.rem(key, wins)
        best, which = load[0] + (held[0] // each) * 1000000, jnp.int32(0)
        for owner in range(1, owners):
            price = load[owner] + (held[owner] // each) * 1000000
            better = price < best
            best = jnp.where(better, price, best)
            which = jnp.where(better, owner, which)
        slot = jnp.int32(0)
        for owner in range(owners):
            mine = which == owner
            slot = jnp.where(mine, owner * each + held[owner], slot)
            load[owner] = jnp.where(mine, load[owner] + ((count + 15) // 16) * 16, load[owner])
            held[owner] = jnp.where(mine, held[owner] + 1, held[owner])
        slots.append(slot)
        names.append(name)
    order = []
    for place in range(wins):
        window = jnp.int32(0)
        for slot, name in zip(slots, names):
            window = jnp.where(slot == place, name, window)
        order.append(window)
    return order


def spread_kernel(
    owners, counts, x, x_out, meta, x_stage, most, most_got, x_send, x_recv, most_send, most_recv, own_sem
):
    wins, rows = x.shape[0], x.shape[1]
    each = wins // owners
    me, win = lax.axis_index("var"), lax.axis_index("win")
    others = [flip(me, 1), flip(me, 2), flip(flip(me, 1), 2)]
    across = [(flip(win, bit), me) for bit in (1, 2, 4)]
    barrier = pltpu.get_barrier_semaphore()
    for friend in [(win, other) for other in others] + across:
        pl.semaphore_signal(barrier, inc=1, device_id=friend, device_id_type=MESH)
    order = assign(counts, wins, owners)
    for place in range(wins):
        meta[place] = order[place]
        x_stage[place] = x[order[place]]
    pl.semaphore_wait(barrier, len(others) + len(across))

    sent = []
    for place, other in enumerate(others):
        sent.append(
            pltpu.make_async_remote_copy(
                src_ref=x_stage.at[pl.ds(other * each, each)],
                dst_ref=x_out.at[:, pl.ds(pl.multiple_of(me * rows, rows), rows), :],
                send_sem=x_send.at[place],
                recv_sem=x_recv.at[place],
                device_id=(win, other),
                device_id_type=MESH,
            )
        )
    for copy in sent:
        copy.start()
    own = pl.ds(pl.multiple_of(me * rows, rows), rows)
    own_x = pltpu.make_async_copy(x_stage.at[pl.ds(me * each, each)], x_out.at[:, own, :], own_sem)
    own_x.start()
    padded = jnp.int32(0)
    for place in range(each):
        name = jnp.int32(0)
        for owner in range(owners):
            name = jnp.where(me == owner, order[owner * each + place], name)
        meta[wins + place] = name
        meta[wins + each + place] = counts[name]
        padded = padded + ((counts[name] + 15) // 16) * 16
    meta[wins + 2 * each] = me
    meta[wins + 2 * each + 1] = padded

    largest = jnp.int32(0)
    for owner in range(owners):
        total = jnp.int32(0)
        for place in range(each):
            total = total + counts[order[owner * each + place]]
        largest = jnp.maximum(largest, total)
    most[0] = jnp.full(most.shape[1:], largest, jnp.int32)
    for turn, friend in enumerate(across):
        copy = pltpu.make_async_remote_copy(
            src_ref=most.at[turn],
            dst_ref=most_got.at[turn],
            send_sem=most_send.at[turn],
            recv_sem=most_recv.at[turn],
            device_id=friend,
            device_id_type=MESH,
        )
        copy.start()
        copy.wait()
        most[turn + 1] = jnp.maximum(most[turn], most_got[turn])
    meta[wins + 2 * each + 2] = jnp.max(most[len(across)])
    own_x.wait()
    for copy in sent:
        copy.wait()


class Plan:
    def __init__(self, meta, wins, each):
        self.names = [meta[wins + place] for place in range(each)]
        self.counts = [meta[wins + each + place] for place in range(each)]
        self.starts = []
        total = jnp.int32(0)
        for count in self.counts:
            self.starts.append(total)
            total = total + ((count + 15) // 16) * 16
        self.total = total
        self.tall = jnp.logical_or(jnp.logical_and(total > 256, total <= 384), total > 512)
        self.blocks = jnp.where(total <= 384, 1, 2)

    def each_block(self, body):
        for size in (256, 384):

            @pl.when(self.tall if size == 384 else jnp.logical_not(self.tall))
            def _(size=size):
                def step(block, carry):
                    body(size, block, pl.ds(pl.multiple_of(block * size, 128), size))
                    return carry

                lax.fori_loop(0, self.blocks, step, 0)

    def pick(self, values, window):
        chosen = values[0]
        for place in range(1, len(values)):
            chosen = jnp.where(window == place, values[place], chosen)
        return chosen

    def each_window(self, body):
        def step(window, carry):
            count = self.pick(self.counts, window)
            start = pl.multiple_of(self.pick(self.starts, window), 16)
            for size in (64, 128, 192, 256):

                @pl.when(jnp.logical_and(count <= size, count > size - 64))
                def _(size=size):
                    body(size, count, pl.ds(start, size))

            return carry

        lax.fori_loop(0, len(self.counts), step, 0)


def marks(row_index, name, count, length):
    listed = row_index[pl.ds(name, 1), :]
    slot = lax.broadcasted_iota(jnp.int32, (length, length), 0)
    place = lax.broadcasted_iota(jnp.int32, (length, length), 1)
    hit = jnp.logical_and(slot == listed, place < count)
    return jnp.where(hit, 1.0, 0.0).astype(LOW)


def mean_of(values):
    return jnp.mean(values, axis=-1, keepdims=True)


def normalize(values):
    centre = values - mean_of(values)
    inverse = lax.rsqrt(mean_of(centre * centre) + EPS)
    return centre * inverse, inverse


def normalize_back(grad, gain, normal, inverse):
    scaled = grad * gain
    return inverse * (scaled - mean_of(scaled) - normal * mean_of(scaled * normal))


def two_heads(pair, lane_low, lane_high):
    return jnp.concatenate([pair * lane_low, pair * lane_high], axis=0)


def lane_masks(lanes):
    lane = lax.broadcasted_iota(jnp.int32, (1, lanes), 1)
    low = jnp.where(lane < lanes // 2, 1.0, 0.0)
    return low.astype(LOW), (1.0 - low).astype(LOW)


def join_heads(stacked):
    size, lanes = stacked.shape[0] // 2, stacked.shape[1]
    lane = lax.broadcasted_iota(jnp.int32, (size, lanes), 1)
    return jnp.where(lane < lanes // 2, stacked[:size], stacked[size:])


def forward_kernel(
    meta, row_index, x, w_qkv, w_attn, w_in, w_out, bias_qv, out_bias, bias_in, gain, shift,
    lefts_out, qkv_out, slope_out, normal_out, inverse_out, top_out, layer_out,
    wv_qkv, wv_attn, wv_in, wv_out, lefts, qkv, slope, normal, inverse, top, state,
    weight_sem, out_sem,
):
    each, length, width = x.shape
    wins = row_index.shape[0]
    layers = w_qkv.shape[0]
    hidden_width = w_in.shape[2]
    pieces = hidden_width // width
    part = width // pieces
    plan = Plan(meta, wins, each)
    weights = ((w_qkv, wv_qkv), (w_attn, wv_attn), (w_in, wv_in), (w_out, wv_out))

    def fetch(layer, which):
        source, target = weights[which]
        return pltpu.make_async_copy(
            source.at[layer], target.at[layer], weight_sem.at[layer, which]
        )

    for layer in range(layers):
        for which in range(4):
            fetch(layer, which).start()

    state[...] = jnp.zeros_like(state)
    for layer in range(layers):
        lefts[layer, 1] = jnp.zeros(lefts.shape[2:], LOW)
        qkv[layer] = jnp.zeros(qkv.shape[1:], LOW)
    for place in range(each):
        hits = marks(row_index, plan.names[place], plan.counts[place], length)
        start = pl.multiple_of(plan.starts[place], 16)
        state[pl.ds(start, length), :] = dot(hits, x[place], 0, 0)

    kept = (
        (lefts, lefts_out, lambda ref, layer, rows: ref.at[layer, :, rows, :]),
        (qkv, qkv_out, lambda ref, layer, rows: ref.at[layer, rows, :]),
        (slope, slope_out, lambda ref, layer, rows: ref.at[layer, rows, :]),
        (normal, normal_out, lambda ref, layer, rows: ref.at[layer, :, rows, :]),
        (inverse, inverse_out, lambda ref, layer, rows: ref.at[layer, rows, :]),
        (top, top_out, lambda ref, layer, rows: ref.at[layer, rows, :]),
    )

    def stores(layer, block, rows):
        return [
            pltpu.make_async_copy(
                view(source, layer, rows), view(target, layer, rows), out_sem.at[layer, which, block]
            )
            for which, (source, target, view) in enumerate(kept)
        ]

    lane_low, lane_high = lane_masks(128)

    def one_layer(layer, carry):
        fetch(layer, 0).wait()

        def project(size, block, rows):
            tokens = state[rows, :].astype(LOW)
            lefts[layer, 0, rows, :] = tokens
            for which in range(3):
                columns = slice(which * width, (which + 1) * width)
                joint = dot(tokens, wv_qkv[layer, :, columns], 1, 0)
                if which == 0:
                    joint = (joint + bias_qv[pl.ds(layer, 1), :width]).astype(LOW) * LOW(0.125)
                elif which == 2:
                    joint = (joint + bias_qv[pl.ds(layer, 1), width:]).astype(LOW)
                else:
                    joint = joint.astype(LOW)
                qkv[layer, rows, columns] = joint

        plan.each_block(project)

        def attend(size, count, rows):
            column = lax.broadcasted_iota(jnp.int32, (2 * size, size), 1)
            live = column < count

            def pair(which, carry):
                at = pl.multiple_of(which * 128, 128)
                query = two_heads(qkv[layer, rows, pl.ds(at, 128)], lane_low, lane_high)
                key = qkv[layer, rows, pl.ds(pl.multiple_of(at + width, 128), 128)]
                value = qkv[layer, rows, pl.ds(pl.multiple_of(at + 2 * width, 128), 128)]
                scores = jnp.where(live, dot(query, key, 1, 1), -1e30)
                peak = jnp.max(scores, axis=-1, keepdims=True)
                expo = jnp.exp(scores - peak)
                total = jnp.sum(expo, axis=-1, keepdims=True)
                probs = (expo * (1.0 / total)).astype(LOW)
                lefts[layer, 1, rows, pl.ds(at, 128)] = join_heads(dot(probs, value, 1, 0)).astype(LOW)
                logs = jnp.broadcast_to(peak + jnp.log(total), (2 * size, 128))
                top[layer, rows, pl.ds(at, 128)] = join_heads(logs)
                return carry

            lax.fori_loop(0, width // 128, pair, 0)

        plan.each_window(attend)
        for which in range(1, 4):
            fetch(layer, which).wait()

        def feed(size, block, rows):
            first = dot(lefts[layer, 1, rows, :], wv_attn[layer], 1, 0) + out_bias[layer, 0:1, :]
            one, inverse_one = normalize(state[rows, :] + first)
            normal[layer, 0, rows, :] = one
            after = one * gain[layer, 0:1, :] + shift[layer, 0:1, :]
            after_low = after.astype(LOW)
            lefts[layer, 2, rows, :] = after_low
            second = jnp.zeros((size, width), F32)
            for piece in range(pieces):
                columns = slice(piece * width, (piece + 1) * width)
                hidden = dot(after_low, wv_in[layer, :, columns], 1, 0) + bias_in[pl.ds(layer, 1), columns]
                squared = hidden * hidden
                bend = jnp.tanh(SMOOTH * hidden * (1.0 + CUBIC * squared))
                half = 0.5 * (1.0 + bend)
                active = (hidden * half).astype(LOW)
                rise = half + 0.5 * hidden * (1.0 - bend * bend) * (
                    SMOOTH * (1.0 + 3.0 * CUBIC * squared)
                )
                slope[layer, rows, columns] = rise.astype(LOW)
                for sub in range(pieces):
                    lefts[layer, 3 + sub, rows, piece * part : (piece + 1) * part] = active[
                        :, sub * part : (sub + 1) * part
                    ]
                second = second + dot(active, wv_out[layer, columns, :], 1, 0)
            two, inverse_two = normalize(after + second + out_bias[layer, 1:2, :])
            normal[layer, 1, rows, :] = two
            state[rows, :] = two * gain[layer, 1:2, :] + shift[layer, 1:2, :]
            lane = lax.broadcasted_iota(jnp.int32, (size, 128), 1)
            inverse[layer, rows, :] = jnp.where(lane < 64, inverse_one, inverse_two)
            for copy in stores(layer, block, rows):
                copy.start()

        plan.each_block(feed)
        return carry

    lax.fori_loop(0, layers, one_layer, 0)
    for place in range(each):
        hits = marks(row_index, plan.names[place], plan.counts[place], length)
        start = pl.multiple_of(plan.starts[place], 16)
        layer_out[place] = dot(hits, state[pl.ds(start, length), :].astype(LOW), 1, 0).astype(LOW)

    for layer in range(layers):

        def finish(size, block, rows, layer=layer):
            for copy in stores(layer, block, rows):
                copy.wait()

        plan.each_block(finish)


def backward_kernel(
    meta, row_index, g, w_qkv, w_attn, w_in, w_out, gain,
    qkv_in, slope_in, normal_in, inverse_in, top_in,
    rights_out, grad_out, sums,
    wv_qkv, wv_attn, wv_in, wv_out, rights, qkv, slope, normal, inverse, top, state, mixed_grad,
    weight_sem, in_sem, out_sem,
):
    each, length, width = g.shape
    wins = row_index.shape[0]
    layers = w_qkv.shape[0]
    hidden_width = w_in.shape[2]
    pieces = hidden_width // width
    plan = Plan(meta, wins, each)
    weights = ((w_out, wv_out), (w_in, wv_in), (w_attn, wv_attn), (w_qkv, wv_qkv))

    def fetch(layer, which):
        source, target = weights[which]
        return pltpu.make_async_copy(
            source.at[layer], target.at[layer], weight_sem.at[layer, which]
        )

    kept = (
        (normal_in, normal, lambda ref, layer, rows: ref.at[layer, :, rows, :]),
        (inverse_in, inverse, lambda ref, layer, rows: ref.at[layer, rows, :]),
        (slope_in, slope, lambda ref, layer, rows: ref.at[layer, rows, :]),
        (qkv_in, qkv, lambda ref, layer, rows: ref.at[layer, rows, :]),
        (top_in, top, lambda ref, layer, rows: ref.at[layer, rows, :]),
    )

    def loads(layer, block, rows):
        return [
            pltpu.make_async_copy(
                view(source, layer, rows), view(target, layer, rows), in_sem.at[layer, which, block]
            )
            for which, (source, target, view) in enumerate(kept)
        ]

    for layer in range(layers):
        qkv[layer, 256:] = jnp.zeros((qkv.shape[1] - 256, qkv.shape[2]), LOW)
    for layer in reversed(range(layers)):

        def begin(size, block, rows, layer=layer):
            for copy in loads(layer, block, rows):
                copy.start()

        fetch(layer, 0).start()
        plan.each_block(begin)
        for which in range(1, 4):
            fetch(layer, which).start()

    state[...] = jnp.zeros_like(state)
    mixed_grad[...] = jnp.zeros_like(mixed_grad)
    sums[...] = jnp.zeros_like(sums)
    for layer in range(layers):
        rights[layer, 0:3] = jnp.zeros((3,) + rights.shape[2:], LOW)
    for place in range(each):
        hits = marks(row_index, plan.names[place], plan.counts[place], length)
        start = pl.multiple_of(plan.starts[place], 16)
        state[pl.ds(start, length), :] = dot(hits, g[place], 0, 0)

    lane_low, lane_high = lane_masks(128)

    def add_rows(layer, place, values):
        sums[layer, place : place + 1, :] += jnp.sum(values, axis=0, keepdims=True)

    def one_layer(step, carry):
        layer = layers - 1 - step
        for which in range(3):
            fetch(layer, which).wait()

        def feed(size, block, rows):
            for copy in loads(layer, block, rows):
                copy.wait()
            grad = state[rows, :]
            two = normal[layer, 1, rows, :]
            add_rows(layer, 9, grad * two)
            add_rows(layer, 11, grad)
            back = normalize_back(grad, gain[layer, 1:2, :], two, inverse[layer, rows, 64:65])
            back_low = back.astype(LOW)
            rights[layer, 8, rows, :] = back_low
            add_rows(layer, 3, back_low.astype(F32))
            for piece in range(pieces):
                columns = slice(piece * width, (piece + 1) * width)
                active = dot(back_low, wv_out[layer, columns, :], 1, 1)
                hidden = (active * slope[layer, rows, columns].astype(F32)).astype(LOW)
                rights[layer, 4 + piece, rows, :] = hidden
                add_rows(layer, 4 + piece, hidden.astype(F32))
                back = back + dot(hidden, wv_in[layer, :, columns], 1, 1)
            one = normal[layer, 0, rows, :]
            add_rows(layer, 8, back * one)
            add_rows(layer, 10, back)
            back = normalize_back(back, gain[layer, 0:1, :], one, inverse[layer, rows, 0:1])
            back_low = back.astype(LOW)
            rights[layer, 3, rows, :] = back_low
            add_rows(layer, 2, back_low.astype(F32))
            mixed_grad[rows, :] = dot(back_low, wv_attn[layer], 1, 1).astype(LOW)
            state[rows, :] = back

        plan.each_block(feed)

        def attend(size, count, rows):
            row = lax.broadcasted_iota(jnp.int32, (2 * size, size), 0)
            column = lax.broadcasted_iota(jnp.int32, (2 * size, size), 1)
            row = jnp.where(row < size, row, row - size)
            live = jnp.logical_and(column < count, row < count)

            def pair(which, carry):
                at = pl.multiple_of(which * 128, 128)
                query = two_heads(qkv[layer, rows, pl.ds(at, 128)], lane_low, lane_high)
                key = qkv[layer, rows, pl.ds(pl.multiple_of(at + width, 128), 128)]
                value = qkv[layer, rows, pl.ds(pl.multiple_of(at + 2 * width, 128), 128)]
                grad = two_heads(mixed_grad[rows, pl.ds(at, 128)], lane_low, lane_high)
                logs = top[layer, rows, pl.ds(at, 128)]
                logs = jnp.concatenate([logs[:, 0:1], logs[:, 64:65]], axis=0)
                probs = jnp.where(live, jnp.exp(dot(query, key, 1, 1) - logs), 0.0)
                d_probs = dot(grad, value, 1, 1)
                centre = jnp.sum(probs * d_probs, axis=-1, keepdims=True)
                d_scores = (probs * (d_probs - centre)).astype(LOW)
                d_query = join_heads(dot(d_scores, key, 1, 0)) * 0.125
                rights[layer, 0, rows, pl.ds(at, 128)] = d_query.astype(LOW)
                rights[layer, 1, rows, pl.ds(at, 128)] = dot(d_scores, query, 0, 0).astype(LOW)
                rights[layer, 2, rows, pl.ds(at, 128)] = dot(probs.astype(LOW), grad, 0, 0).astype(LOW)
                return carry

            lax.fori_loop(0, width // 128, pair, 0)

        plan.each_window(attend)
        fetch(layer, 3).wait()

        def project(size, block, rows):
            grad = state[rows, :]
            for which in range(3):
                columns = slice(which * width, (which + 1) * width)
                piece = rights[layer, which, rows, :]
                grad = grad + dot(piece, wv_qkv[layer, :, columns], 1, 1)
                if which != 1:
                    add_rows(layer, which // 2, piece.astype(F32))
            state[rows, :] = grad
            pltpu.make_async_copy(
                rights.at[layer, :, rows, :], rights_out.at[layer, :, rows, :], out_sem.at[layer, block]
            ).start()

        plan.each_block(project)
        return carry

    lax.fori_loop(0, layers, one_layer, 0)
    for place in range(each):
        hits = marks(row_index, plan.names[place], plan.counts[place], length)
        start = pl.multiple_of(plan.starts[place], 16)
        grad_out[place] = dot(hits, state[pl.ds(start, length), :].astype(LOW), 1, 0).astype(LOW)

    for layer in range(layers):

        def finish(size, block, rows, layer=layer):
            pltpu.make_async_copy(
                rights.at[layer, :, rows, :], rights_out.at[layer, :, rows, :], out_sem.at[layer, block]
            ).wait()

        plan.each_block(finish)


LAGS = (0, 1, 3, 4, 5, 6, 7, 8, 9)
ROUTE = (("var", 1), ("var", 2), ("win", 1), ("win", 2), ("win", 4))


def merge_kernel(
    owners, meta, lefts, rights, sums, layer_out, grad,
    merged, sums_out, layer_back, grad_back,
    left_in, right_in, part, got_core, hold_x, got_x, hold_y, got_y, hold_a, got_a, hold_b, got_b,
    whole, sums_hold, sums_got,
    in_sem, send_sem, recv_sem, out_sem, sums_send, sums_recv, back_send, back_recv, own_sem,
):
    chunks = merged.shape[0]
    layers = lefts.shape[0]
    per_layer = chunks // layers
    packed, width = left_in.shape[1], left_in.shape[2]
    part_rows = part.shape[3]
    each = layer_out.shape[0]
    rows = layer_back.shape[1]
    win, var = lax.axis_index("win"), lax.axis_index("var")
    core, x_half = half_of(var, 1), half_of(var, 2)
    y_half, a_half, b_half = half_of(win, 1), half_of(win, 2), half_of(win, 4)
    others = [flip(var, 1), flip(var, 2), flip(flip(var, 1), 2)]
    route = [partner(axis, bit) for axis, bit in ROUTE]
    greet(route + [(win, others[2])])
    total = meta[meta.shape[0] - 2]

    def block_of(chunk):
        layer, place = layers - 1 - chunk // per_layer, lax.rem(chunk, per_layer)
        late = (place + 4) // 8
        far = place // 8
        left = (1 - late) * (place // 3) + late * (2 + far * (lax.rem(place, 8) + 1))
        right = place - far * lax.rem(place, 8)
        return layer, left, right

    def loads(chunk):
        layer, left, right = block_of(chunk)
        slot = lax.rem(chunk, 2)
        return (
            pltpu.make_async_copy(lefts.at[layer, left], left_in.at[slot], in_sem.at[0, slot]),
            pltpu.make_async_copy(rights.at[layer, right], right_in.at[slot], in_sem.at[1, slot]),
        )

    quarter = part_rows // 2
    eighth = quarter // 2
    sixteenth = eighth // 2
    at_y = pl.multiple_of(y_half * quarter, sixteenth)
    at_a = pl.multiple_of(at_y + a_half * eighth, sixteenth)
    at_b = pl.multiple_of(at_a + b_half * sixteenth, sixteenth)

    def exchange(stage, chunk):
        if stage == 0:
            source, target = part.at[chunk, 1 - core], got_core.at[chunk]
        elif stage == 1:
            source, target = hold_x.at[chunk, 1 - x_half], got_x.at[chunk]
        elif stage == 2:
            source, target = hold_y.at[chunk, 1 - y_half], got_y.at[chunk]
        elif stage == 3:
            source, target = hold_a.at[chunk, 1 - a_half], got_a.at[chunk]
        elif stage == 4:
            source, target = hold_b.at[chunk, 1 - b_half], got_b.at[chunk]
        else:
            at, size = ((at_b, sixteenth), (at_a, eighth), (at_y, quarter))[stage - 5]
            source = whole.at[chunk, pl.ds(at, size), :]
            target = source
        return pltpu.make_async_remote_copy(
            src_ref=source,
            dst_ref=target,
            send_sem=send_sem.at[stage, chunk],
            recv_sem=recv_sem.at[stage, chunk],
            device_id=route[(0, 1, 2, 3, 4, 4, 3, 2)[stage]],
            device_id_type=MESH,
        )

    def out_copy(chunk):
        return pltpu.make_async_copy(whole.at[chunk], merged.at[chunk], out_sem.at[chunk])

    def produce(chunk):
        for copy in loads(chunk):
            copy.wait()
        slot = lax.rem(chunk, 2)
        live = lax.broadcasted_iota(jnp.int32, (packed, width), 0) < total
        left = jnp.where(live, left_in[slot], LOW(0))
        right = jnp.where(live, right_in[slot], LOW(0))
        product = dot(left, right, 0, 0).astype(LOW)
        for shard in range(owners):
            part[chunk, shard % 2, shard // 2] = product[shard * part_rows : (shard + 1) * part_rows]
        exchange(0, chunk).start()

    def add(mine, theirs):
        return (mine.astype(F32) + theirs.astype(F32)).astype(LOW)

    def take(stage, chunk):
        exchange(stage - 1, chunk).wait_recv()
        if stage == 1:
            hold_x[chunk] = add(part[chunk, core], got_core[chunk])
        elif stage == 2:
            hold_y[chunk] = add(hold_x[chunk, x_half], got_x[chunk]).reshape(hold_y.shape[1:])
        elif stage == 3:
            hold_a[chunk] = add(hold_y[chunk, y_half], got_y[chunk]).reshape(hold_a.shape[1:])
        elif stage == 4:
            hold_b[chunk] = add(hold_a[chunk, a_half], got_a[chunk]).reshape(hold_b.shape[1:])
        elif stage == 5:
            whole[chunk, pl.ds(at_b, sixteenth), :] = add(hold_b[chunk, b_half], got_b[chunk])
        if stage < 8:
            exchange(stage, chunk).start()
        else:
            out_copy(chunk).start()

    def sums_exchange(turn):
        return pltpu.make_async_remote_copy(
            src_ref=sums_hold.at[turn],
            dst_ref=sums_got.at[turn],
            send_sem=sums_send.at[turn],
            recv_sem=sums_recv.at[turn],
            device_id=route[turn],
            device_id_type=MESH,
        )

    def back_copies():
        sent = []
        for which, (source, target) in enumerate(((grad, grad_back), (layer_out, layer_back))):
            for place, other in enumerate(others):
                sent.append(
                    pltpu.make_async_remote_copy(
                        src_ref=source.at[:, pl.ds(pl.multiple_of(other * rows, rows), rows), :],
                        dst_ref=target.at[pl.ds(var * each, each)],
                        send_sem=back_send.at[which, place],
                        recv_sem=back_recv.at[which, place],
                        device_id=(win, other),
                        device_id_type=MESH,
                    )
                )
        return sent

    def own_copies():
        return [
            pltpu.make_async_copy(
                source.at[:, pl.ds(pl.multiple_of(var * rows, rows), rows), :],
                target.at[pl.ds(var * each, each)],
                own_sem.at[which],
            )
            for which, (source, target) in enumerate(((grad, grad_back), (layer_out, layer_back)))
        ]

    for copy in loads(0):
        copy.start()
    for copy in own_copies():
        copy.start()
    sums_hold[0] = sums[...]
    sums_exchange(0).start()

    def step(now, carry):
        @pl.when(now + 1 < chunks)
        def _():
            for copy in loads(now + 1):
                copy.start()

        @pl.when(now < chunks)
        def _():
            produce(now)

        for stage in range(1, 9):
            lag = LAGS[stage]

            @pl.when(jnp.logical_and(now >= lag, now < chunks + lag))
            def _(stage=stage, lag=lag):
                take(stage, now - lag)

        for turn in range(5):

            @pl.when(now == 2 * turn + 4)
            def _(turn=turn):
                sums_exchange(turn).wait_recv()
                summed = sums_hold[turn] + sums_got[turn]
                if turn < 4:
                    sums_hold[turn + 1] = summed
                    sums_exchange(turn + 1).start()
                else:
                    sums_out[...] = summed

        @pl.when(now == chunks + 1)
        def _():
            for copy in back_copies():
                copy.start()

        return carry

    lax.fori_loop(0, chunks + LAGS[8], step, 0)

    def settle(chunk, carry):
        for stage in range(8):
            exchange(stage, chunk).wait_send()
        out_copy(chunk).wait()
        return carry

    lax.fori_loop(0, chunks, settle, 0)
    for turn in range(5):
        sums_exchange(turn).wait_send()
    for copy in own_copies():
        copy.wait()
    for copy in back_copies():
        copy.wait()


SETTLED = (2, 3, 4, 5, 6, 7, 8)
LAG = 2
DEPTH = 3
MIXED = 0


class Network:
    def __init__(self, owners, part, got, whole, merged, send_sem, recv_sem, out_sem):
        self.owners, self.part, self.got, self.whole = owners, part, got, whole
        self.merged, self.send_sem, self.recv_sem, self.out_sem = merged, send_sem, recv_sem, out_sem
        self.chunks, self.rows = whole.shape[0], whole.shape[1]
        self.ring = part.shape[0]
        win, var = lax.axis_index("win"), lax.axis_index("var")
        self.win, self.var = win, var
        self.core = half_of(var, 1)
        self.along = {
            "core": (self.core, (win, flip(var, 1))),
            "x": (half_of(var, 2), (win, flip(var, 2))),
            "y": (half_of(win, 1), (flip(win, 1), var)),
            "z": (half_of(win, 2), (flip(win, 2), var)),
            "w": (half_of(win, 4), (flip(win, 4), var)),
        }
        unit, at, self.places = self.rows // 8, 0, {}
        for stage, name in ((7, "y"), (6, "z"), (5, "w")):
            size = (1 << (stage - 5)) * unit
            at = pl.multiple_of(at + self.along[name][0] * size, size)
            self.places[stage] = (at, size)

    @staticmethod
    def way(chunk):
        return (chunk % 4 + 3) // 4 * ((4 - chunk % 4) // 3) * MIXED

    def hop(self, stage, chunk):
        name = ("core", "x", "y", "z", "w", "w", "z", "y")[stage]
        if stage not in (1, 2):
            return self.along[name]
        swap = self.way(chunk)
        if isinstance(swap, int):
            return self.along[name if swap == 0 else {"x": "y", "y": "x"}[name]]
        (half, (win, var)), (other_half, (other_win, other_var)) = (
            self.along["x"], self.along["y"]
        ) if name == "x" else (self.along["y"], self.along["x"])
        return half + swap * (other_half - half), (
            win + swap * (other_win - win), var + swap * (other_var - var)
        )

    def part_of(self, stage, half):
        size = self.got[stage].shape[1]
        return pl.ds(pl.multiple_of(half * size, 16), size)

    def exchange(self, stage, chunk):
        half, beyond = self.hop(stage, chunk)
        if stage == 0:
            source, target = self.part.at[chunk % self.ring, 1 - half], self.got[0].at[chunk]
        elif stage < 5:
            source, target = self.got[stage - 1].at[chunk, self.part_of(stage, 1 - half), :], self.got[stage].at[chunk]
        else:
            at, size = self.places[stage]
            source = target = self.whole.at[chunk, pl.ds(at, size), :]
        return pltpu.make_async_remote_copy(
            src_ref=source,
            dst_ref=target,
            send_sem=self.send_sem.at[stage, chunk],
            recv_sem=self.recv_sem.at[stage, chunk],
            device_id=beyond,
            device_id_type=MESH,
        )

    def out_copy(self, chunk):
        return pltpu.make_async_copy(self.whole.at[chunk], self.merged.at[chunk], self.out_sem.at[chunk])

    def emit(self, chunk, place, left, right):
        product = dot(left, right, 0, 0).astype(LOW)
        slot = place % self.ring

        @pl.when(chunk >= self.ring)
        def _():
            self.exchange(0, chunk - self.ring).wait_send()

        rows = self.rows
        for shard in range(self.owners):
            core, x = shard % 2, shard // 2
            mine = product[shard * rows : (shard + 1) * rows]
            if self.way(place):
                for y in range(2):
                    at = y * rows + x * (rows // 2)
                    self.part[slot, core, at : at + rows // 2] = mine[y * (rows // 2) : (y + 1) * (rows // 2)]
            else:
                self.part[slot, core, x * rows : (x + 1) * rows] = mine
        self.exchange(0, chunk).start()

    def take(self, stage, chunk):
        def add(mine, target):
            return (mine.astype(F32) + target[chunk].astype(F32)).astype(LOW)

        self.exchange(stage - 1, chunk).wait_recv()
        if stage == 1:
            target = self.got[0]
            target[chunk] = add(self.part[chunk % self.ring, self.core], target)
        elif stage <= 4:
            half, _ = self.hop(stage - 1, chunk)
            target = self.got[stage - 1]
            target[chunk] = add(self.got[stage - 2][chunk, self.part_of(stage - 1, half), :], target)
        elif stage == 5:
            half, _ = self.hop(4, chunk)
            at, unit = self.places[5]
            self.whole[chunk, pl.ds(at, unit), :] = add(self.got[3][chunk, self.part_of(4, half), :], self.got[4])
        if stage == 1:

            @pl.when(chunk < DEPTH)
            def _():
                self.exchange(1, chunk).start()
        elif stage < 8:
            self.exchange(stage, chunk).start()
        else:
            self.out_copy(chunk).start()

    def pump(self, turn):
        for place, stage in enumerate(SETTLED):
            chunk = turn - LAG * place

            @pl.when(jnp.logical_and(chunk >= 0, chunk < self.chunks))
            def _(stage=stage, chunk=chunk):
                self.take(stage, chunk)

            if place == 0:

                @pl.when(turn + DEPTH < self.chunks)
                def _():
                    self.exchange(1, turn + DEPTH).start()

    def settle(self):
        def one(chunk, carry):
            for stage in range(1, 8):
                self.exchange(stage, chunk).wait_send()
            self.out_copy(chunk).wait()
            return carry

        lax.fori_loop(0, self.chunks, one, 0)
        for chunk in range(self.chunks - self.ring, self.chunks):
            self.exchange(0, chunk).wait_send()


def packed_kernel(
    owners, size,
    meta, row_index, x, cotangent, w_qkv, w_attn, w_in, w_out, bias_qv, out_bias, bias_in, gain, shift,
    merged, sums_out, layer_back, grad_back,
    wv_qkv, wv_attn, wv_in, wv_out, g_stage, g, layer_out, grad_out, spots, state, lefts, rights, qkv, slope,
    normal, inverse, top, mixed_grad, sums, part, got_core, got_one, got_two, got_three, got_four, whole,
    sums_hold, sums_got,
    weight_sem, send_sem, recv_sem, out_sem, sums_send, sums_recv, far_send, far_recv, own_sem,
):
    each, length, width = x.shape
    wins, rows = cotangent.shape[0], cotangent.shape[1]
    layers = w_qkv.shape[0]
    hidden_width = w_in.shape[2]
    pieces = hidden_width // width
    strip = width // pieces
    pairs = width // 128
    got = (got_core, got_one, got_two, got_three, got_four)
    net = Network(owners, part, got, whole, merged, send_sem, recv_sem, out_sem)
    win, var = net.win, net.var
    others = [flip(var, 1), flip(var, 2), flip(flip(var, 1), 2)]
    weights = ((w_qkv, wv_qkv), (w_attn, wv_attn), (w_in, wv_in), (w_out, wv_out))

    def fetch(layer, which):
        source, target = weights[which]
        return pltpu.make_async_copy(source.at[layer], target.at[layer], weight_sem.at[layer, which])

    fetch(0, 0).start()
    fetch(0, 1).start()

    barrier = pltpu.get_barrier_semaphore()
    friends = [(win, other) for other in others] + [(flip(win, bit), var) for bit in (1, 2, 4)]
    for friend in friends:
        pl.semaphore_signal(barrier, inc=1, device_id=friend, device_id_type=MESH)
    for place in range(wins):
        g_stage[place] = cotangent[meta[place]]
    pl.semaphore_wait(barrier, len(friends))
    mine = pl.ds(pl.multiple_of(var * rows, rows), rows)

    def remote(source, target, which, place, other):
        return pltpu.make_async_remote_copy(
            src_ref=source,
            dst_ref=target,
            send_sem=far_send.at[which, place],
            recv_sem=far_recv.at[which, place],
            device_id=(win, other),
            device_id_type=MESH,
        )

    def to_owners():
        return [
            remote(g_stage.at[pl.ds(other * each, each)], g.at[:, mine, :], 0, place, other)
            for place, other in enumerate(others)
        ] + [pltpu.make_async_copy(g_stage.at[pl.ds(var * each, each)], g.at[:, mine, :], own_sem.at[0])]

    def to_slots(source, target, which):
        home = target.at[pl.ds(var * each, each)]
        return [
            remote(source.at[:, pl.ds(pl.multiple_of(other * rows, rows), rows), :], home, which, place, other)
            for place, other in enumerate(others)
        ] + [pltpu.make_async_copy(source.at[:, mine, :], home, own_sem.at[which])]

    for copy in to_owners():
        copy.start()

    counts = [meta[wins + each + place] for place in range(each)]
    starts = [jnp.int32(0)]
    for count in counts:
        starts.append(starts[-1] + count)
    for place in range(each):
        hits = marks(row_index, meta[wins + place], counts[place], length)
        along = lax.broadcasted_iota(jnp.int32, (length, size), 0) + starts[place]
        moved = jnp.where(lax.broadcasted_iota(jnp.int32, (length, size), 1) == along, 1.0, 0.0).astype(LOW)
        spots[place * length : (place + 1) * length] = dot(hits, moved, 1, 0).astype(LOW)

    row = lax.broadcasted_iota(jnp.int32, (size, 128), 0)
    lane = lax.broadcasted_iota(jnp.int32, (size, 128), 1)
    owner = jnp.zeros((size, 128), jnp.int32)
    for start in starts[1:]:
        owner = owner + jnp.where(row >= start, 1, 0)
    key_mark = jnp.where(lane == owner, 1.0, 0.0).astype(LOW)
    query_mark = jnp.where(lane == owner, jnp.where(lane < each, 0.0, -1e30), -1e30).astype(LOW)
    query_mark = jnp.concatenate([query_mark, query_mark], axis=0)
    lane_low, lane_high = lane_masks(128)

    state[...] = dot(spots[...], x[...].reshape(each * length, width), 0, 0)
    fetch(0, 0).wait()
    for layer, which in ((0, 2), (0, 3), (1, 0), (1, 1), (1, 2), (1, 3)):
        fetch(layer, which).start()

    def masked_scores(layer, at):
        query = two_heads(qkv[layer, :, pl.ds(at, 128)], lane_low, lane_high)
        key = qkv[layer, :, pl.ds(at + width, 128)]
        value = qkv[layer, :, pl.ds(at + 2 * width, 128)]
        scores = dot(
            jnp.concatenate([key, key_mark], axis=1), jnp.concatenate([query, query_mark], axis=1), 1, 1
        )
        return query, key, value, scores

    def forward_layer(layer, carry):
        @pl.when(layer > 0)
        def _():
            fetch(layer, 0).wait()

        tokens = state[...].astype(LOW)
        lefts[layer, 0] = tokens
        for which in range(3):
            columns = slice(which * width, (which + 1) * width)
            joint = dot(tokens, wv_qkv[layer, :, columns], 1, 0)
            if which == 0:
                joint = (joint + bias_qv[pl.ds(layer, 1), :width]).astype(LOW) * LOW(0.125)
            elif which == 2:
                joint = (joint + bias_qv[pl.ds(layer, 1), width:]).astype(LOW)
            else:
                joint = joint.astype(LOW)
            qkv[layer, :, columns] = joint
        for pair in range(pairs):
            at = pair * 128
            _, _, value, scores = masked_scores(layer, at)
            peak = jnp.max(scores, axis=0, keepdims=True)
            expo = jnp.exp(scores - peak)
            total = jnp.sum(expo, axis=0, keepdims=True)
            probs = (expo * (1.0 / total)).astype(LOW)
            lefts[layer, 1, :, pl.ds(at, 128)] = join_heads(dot(probs, value, 0, 0)).astype(LOW)
            top[layer, pair] = peak + jnp.log(total)
        for which in range(1, 4):
            fetch(layer, which).wait()
        first = dot(lefts[layer, 1], wv_attn[layer], 1, 0) + out_bias[layer, 0:1, :]
        one, inverse_one = normalize(state[...] + first)
        normal[layer, 0] = one
        after = one * gain[layer, 0:1, :] + shift[layer, 0:1, :]
        after_low = after.astype(LOW)
        lefts[layer, 2] = after_low
        second = jnp.zeros((size, width), F32)
        for piece in range(pieces):
            columns = slice(piece * width, (piece + 1) * width)
            hidden = dot(after_low, wv_in[layer, :, columns], 1, 0) + bias_in[pl.ds(layer, 1), columns]
            squared = hidden * hidden
            bend = jnp.tanh(hidden * (SMOOTH + SMOOTH * CUBIC * squared))
            half = 0.5 + 0.5 * bend
            active = (hidden * half).astype(LOW)
            rise = half + (hidden * half) * (1.0 - bend) * (SMOOTH + SMOOTH * 3.0 * CUBIC * squared)
            slope[layer, :, columns] = rise.astype(LOW)
            for sub in range(pieces):
                lefts[layer, 3 + sub, :, piece * strip : (piece + 1) * strip] = active[
                    :, sub * strip : (sub + 1) * strip
                ]
            second = second + dot(active, wv_out[layer, columns, :], 1, 0)
        two, inverse_two = normalize(after + second + out_bias[layer, 1:2, :])
        normal[layer, 1] = two
        state[...] = two * gain[layer, 1:2, :] + shift[layer, 1:2, :]
        lanes = lax.broadcasted_iota(jnp.int32, (size, 128), 1)
        inverse[layer] = jnp.where(lanes < 64, inverse_one, inverse_two)
        return carry

    lax.fori_loop(0, layers, forward_layer, 0)
    layer_out[...] = dot(spots[...], state[...].astype(LOW), 1, 0).astype(LOW).reshape(layer_out.shape)
    for copy in to_owners():
        copy.wait()
    state[...] = dot(spots[...], g[...].reshape(each * length, width), 0, 0)
    sums[...] = jnp.zeros_like(sums)

    def add_rows(layer, place, values):
        sums[layer, place : place + 1, :] += jnp.sum(values, axis=0, keepdims=True)

    per_layer = net.chunks // layers

    def backward_layer(step, carry):
        layer = layers - 1 - step
        first = step * per_layer
        turn = step * 7

        def emit(place, left, right):
            net.emit(first + place, place, left, right)

        def take(place):
            net.take(1, first + place)

        grad = state[...]
        two = normal[layer, 1]
        back = normalize_back(grad, gain[layer, 1:2, :], two, inverse[layer, :, 64:65])
        back_low = back.astype(LOW)
        for piece in range(pieces):
            emit(piece, lefts[layer, 3 + piece], back_low)
            if piece > 0:
                take(piece - 1)
        add_rows(layer, 9, grad * two)
        add_rows(layer, 11, grad)
        add_rows(layer, 3, back_low.astype(F32))
        for piece in range(pieces):
            columns = slice(piece * width, (piece + 1) * width)
            active = dot(back_low, wv_out[layer, columns, :], 1, 1)
            hidden = (active * slope[layer, :, columns].astype(F32)).astype(LOW)
            add_rows(layer, 4 + piece, hidden.astype(F32))
            back = back + dot(hidden, wv_in[layer, :, columns], 1, 1)
            emit(pieces + piece, lefts[layer, 2], hidden)
            take(pieces + piece - 1)
            net.pump(turn + piece)
        one = normal[layer, 0]
        add_rows(layer, 8, back * one)
        add_rows(layer, 10, back)
        back = normalize_back(back, gain[layer, 0:1, :], one, inverse[layer, :, 0:1])
        back_low = back.astype(LOW)
        emit(8, lefts[layer, 1], back_low)
        take(7)
        add_rows(layer, 2, back_low.astype(F32))
        mixed_grad[...] = dot(back_low, wv_attn[layer], 1, 1).astype(LOW)
        state[...] = back
        net.pump(turn + 4)
        for pair in range(pairs):
            at = pair * 128
            query, key, value, scores = masked_scores(layer, at)
            grads = two_heads(mixed_grad[:, pl.ds(at, 128)], lane_low, lane_high)
            probs = jnp.exp(scores - top[layer, pair])
            d_probs = dot(value, grads, 1, 1)
            centre = jnp.sum(probs * d_probs, axis=0, keepdims=True)
            d_scores = (probs * (d_probs - centre)).astype(LOW)
            d_query = join_heads(dot(d_scores, key, 0, 0)) * 0.125
            rights[0, :, pl.ds(at, 128)] = d_query.astype(LOW)
            rights[1, :, pl.ds(at, 128)] = dot(d_scores, query, 1, 0).astype(LOW)
            rights[2, :, pl.ds(at, 128)] = dot(probs.astype(LOW), grads, 1, 0).astype(LOW)
        take(8)
        net.pump(turn + 5)
        for which in range(3):
            emit(9 + which, lefts[layer, 0], rights[which])
            if which > 0:
                take(8 + which)
        grad = state[...]
        for which in range(3):
            piece = rights[which]
            grad = grad + dot(piece, wv_qkv[layer, :, which * width : (which + 1) * width], 1, 1)
            if which != 1:
                add_rows(layer, which // 2, piece.astype(F32))
        state[...] = grad
        take(11)
        net.pump(turn + 6)
        return carry

    lax.fori_loop(0, layers, backward_layer, 0)
    first_turn = 7 * layers
    grad_out[...] = dot(spots[...], state[...].astype(LOW), 1, 0).astype(LOW).reshape(grad_out.shape)

    route = [partner(axis, bit) for axis, bit in ROUTE]

    def sums_exchange(step):
        return pltpu.make_async_remote_copy(
            src_ref=sums_hold.at[step],
            dst_ref=sums_got.at[step],
            send_sem=sums_send.at[step],
            recv_sem=sums_recv.at[step],
            device_id=route[step],
            device_id_type=MESH,
        )

    sums_hold[0] = sums[...]
    sums_exchange(0).start()

    def step(now, carry):
        net.pump(now)

        @pl.when(now == net.chunks - 1)
        def _():
            for copy in to_slots(grad_out, grad_back, 2) + to_slots(layer_out, layer_back, 1):
                copy.start()

        for place in range(5):

            @pl.when(now == first_turn + 1 + 2 * place)
            def _(place=place):
                sums_exchange(place).wait_recv()
                summed = sums_hold[place] + sums_got[place]
                if place < 4:
                    sums_hold[place + 1] = summed
                    sums_exchange(place + 1).start()
                else:
                    sums_out[...] = summed

        return carry

    lax.fori_loop(first_turn, net.chunks + LAG * (len(SETTLED) - 1), step, 0)
    net.settle()
    for place in range(5):
        sums_exchange(place).wait_send()
    for copy in to_slots(layer_out, layer_back, 1) + to_slots(grad_out, grad_back, 2):
        copy.wait()


def finish_kernel(
    mixed, meta, merged, sums, layer_back, grad_back,
    layer_out, grad_inputs, qkv, bias_qv, attn, out_bias, in_, bias_in, out, gain, shift,
):
    wins = layer_back.shape[0]
    layers, width = qkv.shape[0], merged.shape[2]
    part_rows = merged.shape[1]
    per_layer = merged.shape[0] // layers
    def take(chunk):
        values = merged[chunk].astype(F32)
        return values

    var = meta[meta.shape[0] - 3]
    for place in range(wins):
        window = meta[place]
        layer_out[window] = layer_back[place]
        grad_inputs[window] = grad_back[place].astype(F32)
    narrow = out_bias.shape[2]
    at = pl.multiple_of(var * narrow, narrow)
    wide = bias_qv.shape[1]
    for layer in range(layers):
        base = (layers - 1 - layer) * per_layer
        at_out, at_in, at_attn, at_qkv = (0, 4, 8, 9) if mixed else (8, 4, 3, 0)
        for which in range(3):
            qkv[layer, :, which * width : (which + 1) * width] = take(base + at_qkv + which)
        attn[layer] = take(base + at_attn)
        for which in range(4):
            in_[layer, :, which * width : (which + 1) * width] = take(base + at_in + which)
            out[layer, which * part_rows : (which + 1) * part_rows, :] = take(base + at_out + which)
        half = width // wide
        bias_qv[layer : layer + 1, :] = sums[
            layer, pl.ds(var // half, 1), pl.ds(pl.multiple_of(lax.rem(var, half) * wide, wide), wide)
        ]
        bias_in[layer : layer + 1, :] = sums[layer, pl.ds(4 + var, 1), :]
        out_bias[layer] = sums[layer, 2:4, pl.ds(at, narrow)]
        gain[layer] = sums[layer, 8:10, pl.ds(at, narrow)]
        shift[layer] = sums[layer, 10:12, pl.ds(at, narrow)]


def gather_kernel(owners, meta, x, x_out, x_stage, x_send, x_recv, own_sem):
    wins, rows = x.shape[0], x.shape[1]
    each = wins // owners
    me, win = lax.axis_index("var"), lax.axis_index("win")
    others = [(win, flip(me, 1)), (win, flip(me, 2)), (win, flip(flip(me, 1), 2))]
    for place in range(wins):
        x_stage[place] = x[meta[place]]
    greet(others)
    own = pl.ds(pl.multiple_of(me * rows, rows), rows)
    copies = [pltpu.make_async_copy(x_stage.at[pl.ds(me * each, each)], x_out.at[:, own, :], own_sem)]
    for place, other in enumerate(others):
        copies.append(
            pltpu.make_async_remote_copy(
                src_ref=x_stage.at[pl.ds(other[1] * each, each)],
                dst_ref=x_out.at[:, own, :],
                send_sem=x_send.at[place],
                recv_sem=x_recv.at[place],
                device_id=other,
                device_id_type=MESH,
            )
        )
    for copy in copies:
        copy.start()
    for copy in copies:
        copy.wait()


def in_vmem(count):
    return [pl.BlockSpec(memory_space=pltpu.VMEM)] * count


def anywhere(count):
    return [pl.BlockSpec(memory_space=pl.ANY)] * count


def in_smem():
    return [pl.BlockSpec(memory_space=pltpu.SMEM)]


def shaped(shape, kind=LOW):
    return jax.ShapeDtypeStruct(shape, kind)


def whole_windows(
    inputs, counts, row_index, w_qkv, bias_qv, w_attn_out, out_bias, w_in, bias_in, w_ffn_out,
    norm_gain, norm_bias, cotangent,
):
    wins, rows, width = inputs.shape
    owners, groups = lax.axis_size("var"), lax.axis_size("win")
    each, length = wins // owners, rows * owners
    packed = each * length
    layers, hidden_width = w_in.shape[0], w_in.shape[2]
    dma = pltpu.SemaphoreType.DMA

    def params(**more):
        return pltpu.CompilerParams(vmem_limit_bytes=VMEM_BYTES, **more)

    x, meta = pl.pallas_call(
        functools.partial(spread_kernel, owners),
        name="spread",
        out_shape=[shaped((each, length, width)), shaped((wins + 2 * each + 3,), jnp.int32)],
        in_specs=in_smem() + in_vmem(1),
        out_specs=anywhere(1) + in_smem(),
        scratch_shapes=[
            pltpu.VMEM((wins, rows, width), LOW),
            pltpu.VMEM((4, 8, 128), jnp.int32),
            pltpu.VMEM((3, 8, 128), jnp.int32),
        ]
        + [dma((owners - 1,))] * 2
        + [dma((3,))] * 2
        + [dma],
        compiler_params=params(collective_id=0, has_side_effects=True),
    )(counts, inputs)

    weights = (w_qkv, w_attn_out, w_in, w_ffn_out)
    weight_space = [pltpu.VMEM(weight.shape, LOW) for weight in weights]
    narrow = width // owners
    chunks = layers * 12
    part_rows = width // owners
    half, quarter, eighth = part_rows // 2, part_rows // 4, part_rows // 8
    sums_shape = (layers, 16, width)

    def space(*shape):
        return pltpu.VMEM((chunks,) + shape + (width,), LOW)

    def finish(mixed, merged, sums, layer_back, grad_back):
        return pl.pallas_call(
            functools.partial(finish_kernel, mixed),
            name="finish",
            out_shape=[
                shaped((wins, rows, width)),
                shaped((wins, rows, width), F32),
                shaped((layers, narrow, 3 * width), F32),
                shaped((layers, 2 * narrow), F32),
                shaped((layers, narrow, width), F32),
                shaped((layers, 2, narrow), F32),
                shaped((layers, narrow, hidden_width), F32),
                shaped((layers, hidden_width // owners), F32),
                shaped((layers, hidden_width // owners, width), F32),
                shaped((layers, 2, narrow), F32),
                shaped((layers, 2, narrow), F32),
            ],
            in_specs=in_smem() + in_vmem(4),
            out_specs=in_vmem(11),
            compiler_params=params(),
        )(meta, merged, sums, layer_back, grad_back)

    def packed_way():
        size = PACKED
        merged = pl.pallas_call(
            functools.partial(packed_kernel, owners, size),
            name="packed",
            out_shape=[
                shaped((chunks, part_rows, width)),
                shaped(sums_shape, F32),
                shaped((wins, rows, width)),
                shaped((wins, rows, width)),
            ],
            in_specs=in_smem() + in_vmem(3) + anywhere(4) + in_vmem(5),
            out_specs=anywhere(1) + in_vmem(1) + anywhere(2),
            scratch_shapes=weight_space
            + [
                pltpu.VMEM((wins, rows, width), LOW),
                pltpu.VMEM((each, length, width), LOW),
                pltpu.VMEM((each, length, width), LOW),
                pltpu.VMEM((each, length, width), LOW),
                pltpu.VMEM((each * length, size), LOW),
                pltpu.VMEM((size, width), F32),
                pltpu.VMEM((layers, 7, size, width), LOW),
                pltpu.VMEM((3, size, width), LOW),
                pltpu.VMEM((layers, size, 3 * width), LOW),
                pltpu.VMEM((layers, size, hidden_width), LOW),
                pltpu.VMEM((layers, 2, size, width), F32),
                pltpu.VMEM((layers, size, 128), F32),
                pltpu.VMEM((layers, width // 128, 1, 2 * size), F32),
                pltpu.VMEM((size, width), LOW),
                pltpu.VMEM(sums_shape, F32),
                pltpu.VMEM((4, 2, 2 * part_rows, width), LOW),
                space(2 * part_rows),
                space(part_rows),
                space(half),
                space(quarter),
                space(eighth),
                space(part_rows),
            ]
            + [pltpu.VMEM((5,) + sums_shape, F32)] * 2
            + [dma((layers, 4)), dma((8, chunks)), dma((8, chunks)), dma((chunks,))]
            + [dma((5,))] * 2
            + [dma((3, owners - 1))] * 2
            + [dma((3,))],
            compiler_params=params(collective_id=2, has_side_effects=True),
        )(
            meta, row_index, x, cotangent, *weights, bias_qv, out_bias, bias_in, norm_gain, norm_bias
        )
        return finish(True, *merged)

    def ragged_way():
        g = pl.pallas_call(
            functools.partial(gather_kernel, owners),
            name="gather",
            out_shape=shaped((each, length, width)),
            in_specs=in_smem() + in_vmem(1),
            out_specs=pl.BlockSpec(memory_space=pl.ANY),
            scratch_shapes=[pltpu.VMEM((wins, rows, width), LOW)] + [dma((owners - 1,))] * 2 + [dma],
            compiler_params=params(collective_id=3, has_side_effects=True),
        )(meta, cotangent)
        kept = [
            shaped((layers, packed, 3 * width)),
            shaped((layers, packed, hidden_width)),
            shaped((layers, 2, packed, width), F32),
            shaped((layers, packed, 128), F32),
            shaped((layers, packed, width), F32),
        ]
        kept_space = [pltpu.VMEM(entry.shape, entry.dtype) for entry in kept]
        lefts_shape = shaped((layers, 7, packed, width))
        lefts, *stash, layer_rows = pl.pallas_call(
            forward_kernel,
            name="forward",
            out_shape=[lefts_shape] + kept + [shaped((each, length, width))],
            in_specs=in_smem() + in_vmem(2) + anywhere(4) + in_vmem(5),
            out_specs=anywhere(6) + in_vmem(1),
            scratch_shapes=weight_space
            + [pltpu.VMEM(lefts_shape.shape, LOW)]
            + kept_space
            + [pltpu.VMEM((packed, width), F32), dma((layers, 4)), dma((layers, 6, 2))],
            compiler_params=params(),
        )(meta, row_index, x, *weights, bias_qv, out_bias, bias_in, norm_gain, norm_bias)

        rights_shape = shaped((layers, 9, packed, width))
        rights, grad_rows, sums = pl.pallas_call(
            backward_kernel,
            name="backward",
            out_shape=[rights_shape, shaped((each, length, width)), shaped((layers, 16, width), F32)],
            in_specs=in_smem() + in_vmem(2) + anywhere(4) + in_vmem(1) + anywhere(5),
            out_specs=anywhere(1) + in_vmem(2),
            scratch_shapes=weight_space
            + [pltpu.VMEM(rights_shape.shape, LOW)]
            + kept_space
            + [
                pltpu.VMEM((packed, width), F32),
                pltpu.VMEM((packed, width), LOW),
                dma((layers, 4)),
                dma((layers, 5, 2)),
                dma((layers, 2)),
            ],
            compiler_params=params(),
        )(meta, row_index, g, *weights, norm_gain, *stash)

        merged, sums, layer_back, grad_back = pl.pallas_call(
            functools.partial(merge_kernel, owners),
            name="merge",
            out_shape=[
                shaped((chunks, part_rows, width)),
                shaped(sums.shape, F32),
                shaped((wins, rows, width)),
                shaped((wins, rows, width)),
            ],
            in_specs=in_smem() + anywhere(2) + in_vmem(3),
            out_specs=anywhere(1) + in_vmem(1) + anywhere(2),
            scratch_shapes=[pltpu.VMEM((2, packed, width), LOW)] * 2
            + [
                space(2, 2, part_rows),
                space(2, part_rows),
                space(2, part_rows),
                space(part_rows),
                space(2, half),
                space(half),
                space(2, quarter),
                space(quarter),
                space(2, eighth),
                space(eighth),
                space(part_rows),
            ]
            + [pltpu.VMEM((5,) + sums.shape, F32)] * 2
            + [dma((2, 2)), dma((8, chunks)), dma((8, chunks)), dma((chunks,))]
            + [dma((5,))] * 2
            + [dma((2, owners - 1))] * 2
            + [dma((2,))],
            compiler_params=params(collective_id=1, has_side_effects=True),
        )(meta, lefts, rights, sums, layer_rows, grad_rows)
        return finish(False, merged, sums, layer_back, grad_back)

    return lax.cond(meta[meta.shape[0] - 1] <= PACKED, packed_way, ragged_way)


def choose(*arrays):
    wins, rows, width = arrays[0].shape
    owners, groups = lax.axis_size("var"), lax.axis_size("win")
    fits = owners == 4 and groups == 8 and wins % owners == 0 and rows % 16 == 0
    fits = fits and (wins // owners, rows * owners, width, arrays[7].shape[2]) == (3, 256, 512, 2048)
    return whole_windows(*arrays) if fits else per_device(*arrays)


def solution(mesh):
    return jax.shard_map(
        choose,
        mesh=mesh,
        in_specs=(
            P("win", "var", None),
            P("win"),
            P("win", None),
            P(),
            P(),
            P(),
            P(),
            P(),
            P(),
            P(),
            P(),
            P(),
            P("win", "var", None),
        ),
        out_specs=(
            P("win", "var", None),
            P("win", "var", None),
            P(None, "var", None),
            P(None, "var"),
            P(None, "var", None),
            P(None, None, "var"),
            P(None, "var", None),
            P(None, "var"),
            P(None, "var", None),
            P(None, None, "var"),
            P(None, None, "var"),
        ),
        check_vma=False,
    )
```

```python
import functools

import jax
import jax.numpy as jnp
from jax import lax
from jax.experimental import pallas as pl
from jax.experimental.pallas import tpu as pltpu
from jax.sharding import PartitionSpec as P

HEADS = 8
LAYERS = 2


EPS = 1e-05
LOW = jnp.bfloat16
F32 = jnp.float32
MESH = pl.DeviceIdType.MESH
VMEM_BYTES = 60 << 20
PACKED = 448
SMOOTH = 0.7978845608028654
CUBIC = 0.044715


def layer_norm(values, gain, shift):
    centre = values - jnp.mean(values, axis=-1, keepdims=True)
    spread = jnp.mean(centre * centre, axis=-1, keepdims=True)
    return centre * lax.rsqrt(spread + EPS) * gain + shift


def smooth(values):
    return jax.nn.gelu(values, approximate=True)


def scores_of(query_heads, key_heads, key_valid, scale):
    raw = (
        jnp.einsum("wqhd,wkhd->whqk", query_heads, key_heads, preferred_element_type=jnp.float32)
        * scale
    )
    return jnp.where(key_valid[:, None, None, :], raw, -1e30)


def per_device(
    inputs,
    counts,
    row_index,
    w_qkv,
    bias_qv,
    w_attn_out,
    out_bias,
    w_in,
    bias_in,
    w_ffn_out,
    norm_gain,
    norm_bias,
    cotangent,
):
    wins, rows, width = inputs.shape
    cycle_size = lax.axis_size("var")
    length = rows * cycle_size
    first_row = lax.axis_index("var") * rows
    head_count = HEADS
    head_size = width // head_count
    scale = head_size ** (-0.5)
    flat = wins * rows
    slots = jnp.arange(length, dtype=jnp.int32)
    live = (slots[None, :] < counts[:, None]).astype(jnp.float32)
    window_ids = jnp.arange(wins, dtype=jnp.int32)[:, None]
    valid = jnp.zeros((wins, length), jnp.float32).at[window_ids, row_index].add(live)
    key_valid = valid > 0.5
    own_valid = lax.dynamic_slice_in_dim(valid, first_row, rows, 1).reshape(flat, 1)
    state = inputs.astype(jnp.float32).reshape(flat, width)
    kept = []
    for which_layer in range(LAYERS):
        x_low = state.astype(jnp.bfloat16)
        joint = jnp.dot(x_low, w_qkv[which_layer], preferred_element_type=jnp.float32)
        query = (joint[:, :width] + bias_qv[which_layer, :width]).astype(jnp.bfloat16)
        keys_low = joint[:, width : 2 * width].astype(jnp.bfloat16)
        values_low = (joint[:, 2 * width :] + bias_qv[which_layer, width:]).astype(jnp.bfloat16)
        pair = jnp.concatenate([keys_low, values_low], axis=1).reshape(wins, rows, 2 * width)
        whole = lax.all_gather(pair, "var", axis=1, tiled=True)
        query_heads = query.reshape(wins, rows, head_count, head_size)
        key_heads = whole[:, :, :width].reshape(wins, length, head_count, head_size)
        value_heads = whole[:, :, width:].reshape(wins, length, head_count, head_size)
        scores = scores_of(query_heads, key_heads, key_valid, scale)
        peak = jnp.max(scores, axis=-1, keepdims=True)
        expo = jnp.exp(scores - peak)
        total = jnp.sum(expo, axis=-1, keepdims=True)
        probs = expo / total
        top = peak + jnp.log(total)
        mixed = (
            jnp.einsum(
                "whqk,wkhd->wqhd",
                probs.astype(jnp.bfloat16),
                value_heads,
                preferred_element_type=jnp.float32,
            )
            .reshape(flat, width)
            .astype(jnp.bfloat16)
        )
        attn = (
            jnp.dot(mixed, w_attn_out[which_layer], preferred_element_type=jnp.float32)
            + out_bias[which_layer, 0]
        )
        normed, norm_one = jax.vjp(
            layer_norm, state + attn, norm_gain[which_layer, 0], norm_bias[which_layer, 0]
        )
        normed_low = normed.astype(jnp.bfloat16)
        hidden = (
            jnp.dot(normed_low, w_in[which_layer], preferred_element_type=jnp.float32)
            + bias_in[which_layer]
        )
        active, gelu_back = jax.vjp(smooth, hidden)
        active_low = active.astype(jnp.bfloat16)
        ffn = (
            jnp.dot(active_low, w_ffn_out[which_layer], preferred_element_type=jnp.float32)
            + out_bias[which_layer, 1]
        )
        state, norm_two = jax.vjp(
            layer_norm, normed + ffn, norm_gain[which_layer, 1], norm_bias[which_layer, 1]
        )
        stored = whole
        kept.append(
            (
                x_low,
                query_heads,
                stored,
                top,
                mixed,
                norm_one,
                normed_low,
                gelu_back,
                active_low,
                norm_two,
            )
        )
    layer_out = (state * own_valid).astype(jnp.bfloat16).reshape(wins, rows, width)
    grad = cotangent.astype(jnp.float32).reshape(flat, width) * own_valid
    collected = []
    for which_layer in reversed(range(LAYERS)):
        (
            x_low,
            query_heads,
            stored,
            top,
            mixed,
            norm_one,
            normed_low,
            gelu_back,
            active_low,
            norm_two,
        ) = kept[which_layer]
        dz_two, gain_two, shift_two = norm_two(grad)
        d_ffn = dz_two.astype(jnp.bfloat16)
        g_ffn_out = jnp.einsum("rf,rd->fd", active_low, d_ffn, preferred_element_type=jnp.float32)
        bias_two = jnp.sum(d_ffn.astype(jnp.float32), axis=0)
        d_active = jnp.einsum(
            "rd,fd->rf", d_ffn, w_ffn_out[which_layer], preferred_element_type=jnp.float32
        )
        (d_hidden,) = gelu_back(d_active)
        d_hidden = d_hidden.astype(jnp.bfloat16)
        g_in = jnp.einsum("rd,rf->df", normed_low, d_hidden, preferred_element_type=jnp.float32)
        g_bias_in = jnp.sum(d_hidden.astype(jnp.float32), axis=0)
        d_normed = dz_two + jnp.einsum(
            "rf,df->rd", d_hidden, w_in[which_layer], preferred_element_type=jnp.float32
        )
        dz_one, gain_one, shift_one = norm_one(d_normed)
        d_attn = dz_one.astype(jnp.bfloat16)
        g_attn_out = jnp.einsum("re,rd->ed", mixed, d_attn, preferred_element_type=jnp.float32)
        bias_one = jnp.sum(d_attn.astype(jnp.float32), axis=0)
        d_mixed = jnp.einsum(
            "rd,ed->re", d_attn, w_attn_out[which_layer], preferred_element_type=jnp.float32
        ).astype(jnp.bfloat16)
        whole = stored
        key_heads = whole[:, :, :width].reshape(wins, length, head_count, head_size)
        value_heads = whole[:, :, width:].reshape(wins, length, head_count, head_size)
        scores = scores_of(query_heads, key_heads, key_valid, scale)
        probs = jnp.exp(scores - top)
        grad_heads = d_mixed.reshape(wins, rows, head_count, head_size)
        d_probs = jnp.einsum(
            "wqhd,wkhd->whqk", grad_heads, value_heads, preferred_element_type=jnp.float32
        )
        centre = jnp.sum(probs * d_probs, axis=-1, keepdims=True)
        d_scores = (probs * (d_probs - centre)).astype(jnp.bfloat16)
        probs_low = probs.astype(jnp.bfloat16)
        d_query = (
            jnp.einsum("whqk,wkhd->wqhd", d_scores, key_heads, preferred_element_type=jnp.float32)
            * scale
        )
        d_query = d_query.reshape(flat, width).astype(jnp.bfloat16)
        span_rows = lax.axis_size("var") * rows
        d_key = (
            jnp.einsum("whqk,wqhd->kwhd", d_scores, query_heads, preferred_element_type=jnp.float32)
            * scale
        )
        d_value = jnp.einsum(
            "whqk,wqhd->kwhd", probs_low, grad_heads, preferred_element_type=jnp.float32
        )
        key_grads = lax.psum_scatter(
            jnp.concatenate(
                [d_key.reshape(span_rows, wins, width), d_value.reshape(span_rows, wins, width)],
                axis=2,
            ).astype(jnp.bfloat16),
            "var",
            scatter_dimension=0,
            tiled=True,
        ).astype(jnp.float32)
        key_grads = (
            jnp.transpose(key_grads, (1, 0, 2)).reshape(flat, 2 * width).astype(jnp.bfloat16)
        )
        d_joint = jnp.concatenate([d_query, key_grads], axis=1)
        g_qkv = jnp.einsum("rd,re->de", x_low, d_joint, preferred_element_type=jnp.float32)
        g_bias_qv = jnp.concatenate(
            [
                jnp.sum(d_query.astype(jnp.float32), axis=0),
                jnp.sum(key_grads[:, width:].astype(jnp.float32), axis=0),
            ]
        )
        grad = dz_one + jnp.einsum(
            "re,de->rd", d_joint, w_qkv[which_layer], preferred_element_type=jnp.float32
        )
        g_out_bias = jnp.stack([bias_one, bias_two])
        g_gain = jnp.stack([gain_one, gain_two])
        g_shift = jnp.stack([shift_one, shift_two])
        terms = (
            g_qkv,
            g_bias_qv,
            g_attn_out,
            g_out_bias,
            g_in,
            g_bias_in,
            g_ffn_out,
            g_gain,
            g_shift,
        )
        collected.append(terms)
    collected = collected[::-1]
    stacked = tuple((jnp.stack([entry[position] for entry in collected]) for position in range(9)))
    shards = (
        lax.psum_scatter(
            stacked[0].astype(jnp.bfloat16), "var", scatter_dimension=1, tiled=True
        ).astype(jnp.float32),
        lax.psum_scatter(
            stacked[1].astype(jnp.bfloat16), "var", scatter_dimension=1, tiled=True
        ).astype(jnp.float32),
        lax.psum_scatter(
            stacked[2].astype(jnp.bfloat16), "var", scatter_dimension=1, tiled=True
        ).astype(jnp.float32),
        lax.psum_scatter(
            stacked[3].astype(jnp.bfloat16), "var", scatter_dimension=2, tiled=True
        ).astype(jnp.float32),
        lax.psum_scatter(
            stacked[4].astype(jnp.bfloat16), "var", scatter_dimension=1, tiled=True
        ).astype(jnp.float32),
        lax.psum_scatter(
            stacked[5].astype(jnp.bfloat16), "var", scatter_dimension=1, tiled=True
        ).astype(jnp.float32),
        lax.psum_scatter(
            stacked[6].astype(jnp.bfloat16), "var", scatter_dimension=1, tiled=True
        ).astype(jnp.float32),
        lax.psum_scatter(
            stacked[7].astype(jnp.bfloat16), "var", scatter_dimension=2, tiled=True
        ).astype(jnp.float32),
        lax.psum_scatter(
            stacked[8].astype(jnp.bfloat16), "var", scatter_dimension=2, tiled=True
        ).astype(jnp.float32),
    )
    stacked = (
        lax.psum(shards[0].astype(jnp.bfloat16), "win").astype(jnp.float32),
        lax.psum(shards[1].astype(jnp.bfloat16), "win").astype(jnp.float32),
        lax.psum(shards[2].astype(jnp.bfloat16), "win").astype(jnp.float32),
        lax.psum(shards[3].astype(jnp.bfloat16), "win").astype(jnp.float32),
        lax.psum(shards[4].astype(jnp.bfloat16), "win").astype(jnp.float32),
        lax.psum(shards[5].astype(jnp.bfloat16), "win").astype(jnp.float32),
        lax.psum(shards[6].astype(jnp.bfloat16), "win").astype(jnp.float32),
        lax.psum(shards[7].astype(jnp.bfloat16), "win").astype(jnp.float32),
        lax.psum(shards[8].astype(jnp.bfloat16), "win").astype(jnp.float32),
    )
    grad_inputs = grad.reshape(wins, rows, width)
    return (
        layer_out,
        grad_inputs,
        stacked[0],
        stacked[1],
        stacked[2],
        stacked[3],
        stacked[4],
        stacked[5],
        stacked[6],
        stacked[7],
        stacked[8],
    )


def dot(left, right, left_dim, right_dim):
    return lax.dot_general(
        left, right, (((left_dim,), (right_dim,)), ((), ())), preferred_element_type=F32
    )


def flip(index, bit):
    return index + bit - 2 * bit * lax.rem(index // bit, 2)


def half_of(index, bit):
    return lax.rem(index // bit, 2)


def partner(axis, bit):
    win, var = lax.axis_index("win"), lax.axis_index("var")
    if axis == "win":
        return (flip(win, bit), var)
    return (win, flip(var, bit))


def greet(partners):
    barrier = pltpu.get_barrier_semaphore()
    for other in partners:
        pl.semaphore_signal(barrier, inc=1, device_id=other, device_id_type=MESH)
    pl.semaphore_wait(barrier, len(partners))


def assign(counts, wins, owners):
    each = wins // owners
    keys = [counts[w] * wins + w for w in range(wins)]
    for stop in range(wins - 1, 0, -1):
        for low in range(stop):
            first, second = keys[low], keys[low + 1]
            keys[low], keys[low + 1] = jnp.maximum(first, second), jnp.minimum(first, second)
    load = [jnp.int32(0)] * owners
    held = [jnp.int32(0)] * owners
    slots, names = [], []
    for key in keys:
        count, name = key // wins, lax.rem(key, wins)
        best, which = load[0] + (held[0] // each) * 1000000, jnp.int32(0)
        for owner in range(1, owners):
            price = load[owner] + (held[owner] // each) * 1000000
            better = price < best
            best = jnp.where(better, price, best)
            which = jnp.where(better, owner, which)
        slot = jnp.int32(0)
        for owner in range(owners):
            mine = which == owner
            slot = jnp.where(mine, owner * each + held[owner], slot)
            load[owner] = jnp.where(mine, load[owner] + ((count + 15) // 16) * 16, load[owner])
            held[owner] = jnp.where(mine, held[owner] + 1, held[owner])
        slots.append(slot)
        names.append(name)
    order = []
    for place in range(wins):
        window = jnp.int32(0)
        for slot, name in zip(slots, names):
            window = jnp.where(slot == place, name, window)
        order.append(window)
    return order


def spread_kernel(
    owners, counts, x, x_out, meta, x_stage, x_send, x_recv, own_sem
):
    wins, rows = x.shape[0], x.shape[1]
    each = wins // owners
    me, win = lax.axis_index("var"), lax.axis_index("win")
    others = [flip(me, 1), flip(me, 2), flip(flip(me, 1), 2)]
    barrier = pltpu.get_barrier_semaphore()
    for other in others:
        pl.semaphore_signal(barrier, inc=1, device_id=(win, other), device_id_type=MESH)
    order = assign(counts, wins, owners)
    for place in range(wins):
        meta[place] = order[place]
        x_stage[place] = x[order[place]]
    pl.semaphore_wait(barrier, len(others))

    sent = []
    for place, other in enumerate(others):
        sent.append(
            pltpu.make_async_remote_copy(
                src_ref=x_stage.at[pl.ds(other * each, each)],
                dst_ref=x_out.at[:, pl.ds(pl.multiple_of(me * rows, rows), rows), :],
                send_sem=x_send.at[place],
                recv_sem=x_recv.at[place],
                device_id=(win, other),
                device_id_type=MESH,
            )
        )
    for copy in sent:
        copy.start()
    own = pl.ds(pl.multiple_of(me * rows, rows), rows)
    own_x = pltpu.make_async_copy(x_stage.at[pl.ds(me * each, each)], x_out.at[:, own, :], own_sem)
    own_x.start()
    padded = jnp.int32(0)
    for place in range(each):
        name = jnp.int32(0)
        for owner in range(owners):
            name = jnp.where(me == owner, order[owner * each + place], name)
        meta[wins + place] = name
        meta[wins + each + place] = counts[name]
        padded = padded + ((counts[name] + 15) // 16) * 16
    meta[wins + 2 * each] = me
    meta[wins + 2 * each + 1] = padded

    own_x.wait()
    for copy in sent:
        copy.wait()


class Plan:
    def __init__(self, meta, wins, each):
        self.names = [meta[wins + place] for place in range(each)]
        self.counts = [meta[wins + each + place] for place in range(each)]
        self.starts = []
        total = jnp.int32(0)
        for count in self.counts:
            self.starts.append(total)
            total = total + ((count + 15) // 16) * 16
        self.total = total
        self.blocks = (total + 127) // 128

    def each_block(self, body):
        def step(block, carry):
            body(128, block, pl.ds(pl.multiple_of(block * 128, 128), 128))
            return carry

        lax.fori_loop(0, self.blocks, step, 0)

    def pick(self, values, window):
        chosen = values[0]
        for place in range(1, len(values)):
            chosen = jnp.where(window == place, values[place], chosen)
        return chosen

    def each_window(self, body):
        def step(window, carry):
            count = self.pick(self.counts, window)
            start = pl.multiple_of(self.pick(self.starts, window), 16)
            body(256, count, pl.ds(start, 256))

            return carry

        lax.fori_loop(0, len(self.counts), step, 0)


def marks(row_index, name, count, length):
    listed = row_index[pl.ds(name, 1), :]
    slot = lax.broadcasted_iota(jnp.int32, (length, length), 0)
    place = lax.broadcasted_iota(jnp.int32, (length, length), 1)
    hit = jnp.logical_and(slot == listed, place < count)
    return jnp.where(hit, 1.0, 0.0).astype(LOW)


def mean_of(values):
    return jnp.mean(values, axis=-1, keepdims=True)


def normalize(values):
    centre = values - mean_of(values)
    inverse = lax.rsqrt(mean_of(centre * centre) + EPS)
    return centre * inverse, inverse


def normalize_back(grad, gain, normal, inverse):
    scaled = grad * gain
    return inverse * (scaled - mean_of(scaled) - normal * mean_of(scaled * normal))


def two_heads(pair, lane_low, lane_high):
    return jnp.concatenate([pair * lane_low, pair * lane_high], axis=0)


def lane_masks(lanes):
    lane = lax.broadcasted_iota(jnp.int32, (1, lanes), 1)
    low = jnp.where(lane < lanes // 2, 1.0, 0.0)
    return low.astype(LOW), (1.0 - low).astype(LOW)


def join_heads(stacked):
    size, lanes = stacked.shape[0] // 2, stacked.shape[1]
    lane = lax.broadcasted_iota(jnp.int32, (size, lanes), 1)
    return jnp.where(lane < lanes // 2, stacked[:size], stacked[size:])


def forward_kernel(
    meta, row_index, x, w_qkv, w_attn, w_in, w_out, bias_qv, out_bias, bias_in, gain, shift,
    lefts_out, qkv_out, slope_out, normal_out, inverse_out, top_out, layer_out,
    wv_qkv, wv_attn, wv_in, wv_out, lefts, qkv, slope, normal, inverse, top, state,
    weight_sem, out_sem,
):
    each, length, width = x.shape
    wins = row_index.shape[0]
    layers = w_qkv.shape[0]
    hidden_width = w_in.shape[2]
    pieces = hidden_width // width
    part = width // pieces
    plan = Plan(meta, wins, each)
    weights = ((w_qkv, wv_qkv), (w_attn, wv_attn), (w_in, wv_in), (w_out, wv_out))

    def fetch(layer, which):
        source, target = weights[which]
        return pltpu.make_async_copy(
            source.at[layer], target.at[layer], weight_sem.at[layer, which]
        )

    for layer in range(layers):
        for which in range(4):
            fetch(layer, which).start()

    state[...] = jnp.zeros_like(state)
    for layer in range(layers):
        lefts[layer, 1] = jnp.zeros(lefts.shape[2:], LOW)
        qkv[layer] = jnp.zeros(qkv.shape[1:], LOW)
    for place in range(each):
        hits = marks(row_index, plan.names[place], plan.counts[place], length)
        start = pl.multiple_of(plan.starts[place], 16)
        state[pl.ds(start, length), :] = dot(hits, x[place], 0, 0)

    kept = (
        (lefts, lefts_out, lambda ref, layer, rows: ref.at[layer, :, rows, :]),
        (qkv, qkv_out, lambda ref, layer, rows: ref.at[layer, rows, :]),
        (slope, slope_out, lambda ref, layer, rows: ref.at[layer, rows, :]),
        (normal, normal_out, lambda ref, layer, rows: ref.at[layer, :, rows, :]),
        (inverse, inverse_out, lambda ref, layer, rows: ref.at[layer, rows, :]),
        (top, top_out, lambda ref, layer, rows: ref.at[layer, rows, :]),
    )

    def stores(layer, block, rows):
        return [
            pltpu.make_async_copy(
                view(source, layer, rows), view(target, layer, rows), out_sem.at[layer, which, block]
            )
            for which, (source, target, view) in enumerate(kept)
        ]

    lane_low, lane_high = lane_masks(128)

    def one_layer(layer, carry):
        fetch(layer, 0).wait()

        def project(size, block, rows):
            tokens = state[rows, :].astype(LOW)
            lefts[layer, 0, rows, :] = tokens
            for which in range(3):
                columns = slice(which * width, (which + 1) * width)
                joint = dot(tokens, wv_qkv[layer, :, columns], 1, 0)
                if which == 0:
                    joint = (joint + bias_qv[pl.ds(layer, 1), :width]).astype(LOW) * LOW(0.125)
                elif which == 2:
                    joint = (joint + bias_qv[pl.ds(layer, 1), width:]).astype(LOW)
                else:
                    joint = joint.astype(LOW)
                qkv[layer, rows, columns] = joint

        plan.each_block(project)

        def attend(size, count, rows):
            column = lax.broadcasted_iota(jnp.int32, (2 * size, size), 1)
            live = column < count

            def pair(which, carry):
                at = pl.multiple_of(which * 128, 128)
                query = two_heads(qkv[layer, rows, pl.ds(at, 128)], lane_low, lane_high)
                key = qkv[layer, rows, pl.ds(pl.multiple_of(at + width, 128), 128)]
                value = qkv[layer, rows, pl.ds(pl.multiple_of(at + 2 * width, 128), 128)]
                scores = jnp.where(live, dot(query, key, 1, 1), -1e30)
                peak = jnp.max(scores, axis=-1, keepdims=True)
                expo = jnp.exp(scores - peak)
                total = jnp.sum(expo, axis=-1, keepdims=True)
                probs = (expo * (1.0 / total)).astype(LOW)
                lefts[layer, 1, rows, pl.ds(at, 128)] = join_heads(dot(probs, value, 1, 0)).astype(LOW)
                logs = jnp.broadcast_to(peak + jnp.log(total), (2 * size, 128))
                top[layer, rows, pl.ds(at, 128)] = join_heads(logs)
                return carry

            lax.fori_loop(0, width // 128, pair, 0)

        plan.each_window(attend)
        for which in range(1, 4):
            fetch(layer, which).wait()

        def feed(size, block, rows):
            first = dot(lefts[layer, 1, rows, :], wv_attn[layer], 1, 0) + out_bias[layer, 0:1, :]
            one, inverse_one = normalize(state[rows, :] + first)
            normal[layer, 0, rows, :] = one
            after = one * gain[layer, 0:1, :] + shift[layer, 0:1, :]
            after_low = after.astype(LOW)
            lefts[layer, 2, rows, :] = after_low
            second = jnp.zeros((size, width), F32)
            for piece in range(pieces):
                columns = slice(piece * width, (piece + 1) * width)
                hidden = dot(after_low, wv_in[layer, :, columns], 1, 0) + bias_in[pl.ds(layer, 1), columns]
                squared = hidden * hidden
                bend = jnp.tanh(SMOOTH * hidden * (1.0 + CUBIC * squared))
                half = 0.5 * (1.0 + bend)
                active = (hidden * half).astype(LOW)
                rise = half + 0.5 * hidden * (1.0 - bend * bend) * (
                    SMOOTH * (1.0 + 3.0 * CUBIC * squared)
                )
                slope[layer, rows, columns] = rise.astype(LOW)
                for sub in range(pieces):
                    lefts[layer, 3 + sub, rows, piece * part : (piece + 1) * part] = active[
                        :, sub * part : (sub + 1) * part
                    ]
                second = second + dot(active, wv_out[layer, columns, :], 1, 0)
            two, inverse_two = normalize(after + second + out_bias[layer, 1:2, :])
            normal[layer, 1, rows, :] = two
            state[rows, :] = two * gain[layer, 1:2, :] + shift[layer, 1:2, :]
            lane = lax.broadcasted_iota(jnp.int32, (size, 128), 1)
            inverse[layer, rows, :] = jnp.where(lane < 64, inverse_one, inverse_two)
            for copy in stores(layer, block, rows):
                copy.start()

        plan.each_block(feed)
        return carry

    lax.fori_loop(0, layers, one_layer, 0)
    for place in range(each):
        hits = marks(row_index, plan.names[place], plan.counts[place], length)
        start = pl.multiple_of(plan.starts[place], 16)
        layer_out[place] = dot(hits, state[pl.ds(start, length), :].astype(LOW), 1, 0).astype(LOW)

    for layer in range(layers):

        def finish(size, block, rows, layer=layer):
            for copy in stores(layer, block, rows):
                copy.wait()

        plan.each_block(finish)


def backward_kernel(
    meta, row_index, g, w_qkv, w_attn, w_in, w_out, gain,
    qkv_in, slope_in, normal_in, inverse_in, top_in,
    rights_out, grad_out, sums,
    wv_qkv, wv_attn, wv_in, wv_out, rights, qkv, slope, normal, inverse, top, state, mixed_grad,
    weight_sem, in_sem, out_sem,
):
    each, length, width = g.shape
    wins = row_index.shape[0]
    layers = w_qkv.shape[0]
    hidden_width = w_in.shape[2]
    pieces = hidden_width // width
    plan = Plan(meta, wins, each)
    weights = ((w_out, wv_out), (w_in, wv_in), (w_attn, wv_attn), (w_qkv, wv_qkv))

    def fetch(layer, which):
        source, target = weights[which]
        return pltpu.make_async_copy(
            source.at[layer], target.at[layer], weight_sem.at[layer, which]
        )

    kept = (
        (normal_in, normal, lambda ref, layer, rows: ref.at[layer, :, rows, :]),
        (inverse_in, inverse, lambda ref, layer, rows: ref.at[layer, rows, :]),
        (slope_in, slope, lambda ref, layer, rows: ref.at[layer, rows, :]),
        (qkv_in, qkv, lambda ref, layer, rows: ref.at[layer, rows, :]),
        (top_in, top, lambda ref, layer, rows: ref.at[layer, rows, :]),
    )

    def loads(layer, block, rows):
        return [
            pltpu.make_async_copy(
                view(source, layer, rows), view(target, layer, rows), in_sem.at[layer, which, block]
            )
            for which, (source, target, view) in enumerate(kept)
        ]

    for layer in range(layers):
        qkv[layer, 128:] = jnp.zeros((qkv.shape[1] - 128, qkv.shape[2]), LOW)
    for layer in reversed(range(layers)):

        def begin(size, block, rows, layer=layer):
            for copy in loads(layer, block, rows):
                copy.start()

        fetch(layer, 0).start()
        plan.each_block(begin)
        for which in range(1, 4):
            fetch(layer, which).start()

    state[...] = jnp.zeros_like(state)
    mixed_grad[...] = jnp.zeros_like(mixed_grad)
    sums[...] = jnp.zeros_like(sums)
    for layer in range(layers):
        rights[layer, 0:3] = jnp.zeros((3,) + rights.shape[2:], LOW)
    for place in range(each):
        hits = marks(row_index, plan.names[place], plan.counts[place], length)
        start = pl.multiple_of(plan.starts[place], 16)
        state[pl.ds(start, length), :] = dot(hits, g[place], 0, 0)

    lane_low, lane_high = lane_masks(128)

    def add_rows(layer, place, values):
        sums[layer, place : place + 1, :] += jnp.sum(values, axis=0, keepdims=True)

    def one_layer(step, carry):
        layer = layers - 1 - step
        for which in range(3):
            fetch(layer, which).wait()

        def feed(size, block, rows):
            for copy in loads(layer, block, rows):
                copy.wait()
            grad = state[rows, :]
            two = normal[layer, 1, rows, :]
            add_rows(layer, 9, grad * two)
            add_rows(layer, 11, grad)
            back = normalize_back(grad, gain[layer, 1:2, :], two, inverse[layer, rows, 64:65])
            back_low = back.astype(LOW)
            rights[layer, 8, rows, :] = back_low
            add_rows(layer, 3, back_low.astype(F32))
            for piece in range(pieces):
                columns = slice(piece * width, (piece + 1) * width)
                active = dot(back_low, wv_out[layer, columns, :], 1, 1)
                hidden = (active * slope[layer, rows, columns].astype(F32)).astype(LOW)
                rights[layer, 4 + piece, rows, :] = hidden
                add_rows(layer, 4 + piece, hidden.astype(F32))
                back = back + dot(hidden, wv_in[layer, :, columns], 1, 1)
            one = normal[layer, 0, rows, :]
            add_rows(layer, 8, back * one)
            add_rows(layer, 10, back)
            back = normalize_back(back, gain[layer, 0:1, :], one, inverse[layer, rows, 0:1])
            back_low = back.astype(LOW)
            rights[layer, 3, rows, :] = back_low
            add_rows(layer, 2, back_low.astype(F32))
            mixed_grad[rows, :] = dot(back_low, wv_attn[layer], 1, 1).astype(LOW)
            state[rows, :] = back

        plan.each_block(feed)

        def attend(size, count, rows):
            row = lax.broadcasted_iota(jnp.int32, (2 * size, size), 0)
            column = lax.broadcasted_iota(jnp.int32, (2 * size, size), 1)
            row = jnp.where(row < size, row, row - size)
            live = jnp.logical_and(column < count, row < count)

            def pair(which, carry):
                at = pl.multiple_of(which * 128, 128)
                query = two_heads(qkv[layer, rows, pl.ds(at, 128)], lane_low, lane_high)
                key = qkv[layer, rows, pl.ds(pl.multiple_of(at + width, 128), 128)]
                value = qkv[layer, rows, pl.ds(pl.multiple_of(at + 2 * width, 128), 128)]
                grad = two_heads(mixed_grad[rows, pl.ds(at, 128)], lane_low, lane_high)
                logs = top[layer, rows, pl.ds(at, 128)]
                logs = jnp.concatenate([logs[:, 0:1], logs[:, 64:65]], axis=0)
                probs = jnp.where(live, jnp.exp(dot(query, key, 1, 1) - logs), 0.0)
                d_probs = dot(grad, value, 1, 1)
                centre = jnp.sum(probs * d_probs, axis=-1, keepdims=True)
                d_scores = (probs * (d_probs - centre)).astype(LOW)
                d_query = join_heads(dot(d_scores, key, 1, 0)) * 0.125
                rights[layer, 0, rows, pl.ds(at, 128)] = d_query.astype(LOW)
                rights[layer, 1, rows, pl.ds(at, 128)] = dot(d_scores, query, 0, 0).astype(LOW)
                rights[layer, 2, rows, pl.ds(at, 128)] = dot(probs.astype(LOW), grad, 0, 0).astype(LOW)
                return carry

            lax.fori_loop(0, width // 128, pair, 0)

        plan.each_window(attend)
        fetch(layer, 3).wait()

        def project(size, block, rows):
            grad = state[rows, :]
            for which in range(3):
                columns = slice(which * width, (which + 1) * width)
                piece = rights[layer, which, rows, :]
                grad = grad + dot(piece, wv_qkv[layer, :, columns], 1, 1)
                if which != 1:
                    add_rows(layer, which // 2, piece.astype(F32))
            state[rows, :] = grad
            pltpu.make_async_copy(
                rights.at[layer, :, rows, :], rights_out.at[layer, :, rows, :], out_sem.at[layer, block]
            ).start()

        plan.each_block(project)
        return carry

    lax.fori_loop(0, layers, one_layer, 0)
    for place in range(each):
        hits = marks(row_index, plan.names[place], plan.counts[place], length)
        start = pl.multiple_of(plan.starts[place], 16)
        grad_out[place] = dot(hits, state[pl.ds(start, length), :].astype(LOW), 1, 0).astype(LOW)

    for layer in range(layers):

        def finish(size, block, rows, layer=layer):
            pltpu.make_async_copy(
                rights.at[layer, :, rows, :], rights_out.at[layer, :, rows, :], out_sem.at[layer, block]
            ).wait()

        plan.each_block(finish)


LAGS = (0, 1, 3, 4, 5, 6, 7, 8, 9)
ROUTE = (("var", 1), ("var", 2), ("win", 1), ("win", 2), ("win", 4))


def merge_kernel(
    owners, meta, lefts, rights, sums, layer_out, grad,
    merged, sums_out, layer_back, grad_back,
    left_in, right_in, part, got_core, hold_x, got_x, hold_y, got_y, hold_a, got_a, hold_b, got_b,
    whole, sums_hold, sums_got,
    in_sem, send_sem, recv_sem, out_sem, sums_send, sums_recv, back_send, back_recv, own_sem,
):
    chunks = merged.shape[0]
    layers = lefts.shape[0]
    per_layer = chunks // layers
    packed, width = left_in.shape[1], left_in.shape[2]
    part_rows = part.shape[3]
    each = layer_out.shape[0]
    rows = layer_back.shape[1]
    win, var = lax.axis_index("win"), lax.axis_index("var")
    core, x_half = half_of(var, 1), half_of(var, 2)
    y_half, a_half, b_half = half_of(win, 1), half_of(win, 2), half_of(win, 4)
    others = [flip(var, 1), flip(var, 2), flip(flip(var, 1), 2)]
    route = [partner(axis, bit) for axis, bit in ROUTE]
    greet(route + [(win, others[2])])
    total = meta[meta.shape[0] - 1]

    def block_of(chunk):
        layer, place = layers - 1 - chunk // per_layer, lax.rem(chunk, per_layer)
        group, member = place // 4, lax.rem(place, 4)
        first, third = (2 - group) // 2, group // 2
        second = 1 - first - third
        alone = 1 - (member + 3) // 4
        left = first * (3 + member) + second * 2 + third * alone
        right = first * 8 + second * (4 + member) + third * (member - 1 + 4 * alone)
        return layer, left, right

    def loads(chunk):
        layer, left, right = block_of(chunk)
        slot = lax.rem(chunk, 2)
        return (
            pltpu.make_async_copy(lefts.at[layer, left], left_in.at[slot], in_sem.at[0, slot]),
            pltpu.make_async_copy(rights.at[layer, right], right_in.at[slot], in_sem.at[1, slot]),
        )

    quarter = part_rows // 2
    eighth = quarter // 2
    sixteenth = eighth // 2
    at_y = pl.multiple_of(y_half * quarter, sixteenth)
    at_a = pl.multiple_of(at_y + a_half * eighth, sixteenth)
    at_b = pl.multiple_of(at_a + b_half * sixteenth, sixteenth)

    def exchange(stage, chunk):
        if stage == 0:
            source, target = part.at[chunk, 1 - core], got_core.at[chunk]
        elif stage == 1:
            source, target = hold_x.at[chunk, 1 - x_half], got_x.at[chunk]
        elif stage == 2:
            source, target = hold_y.at[chunk, 1 - y_half], got_y.at[chunk]
        elif stage == 3:
            source, target = hold_a.at[chunk, 1 - a_half], got_a.at[chunk]
        elif stage == 4:
            source, target = hold_b.at[chunk, 1 - b_half], got_b.at[chunk]
        else:
            at, size = ((at_b, sixteenth), (at_a, eighth), (at_y, quarter))[stage - 5]
            source = whole.at[chunk, pl.ds(at, size), :]
            target = source
        return pltpu.make_async_remote_copy(
            src_ref=source,
            dst_ref=target,
            send_sem=send_sem.at[stage, chunk],
            recv_sem=recv_sem.at[stage, chunk],
            device_id=route[(0, 1, 2, 3, 4, 4, 3, 2)[stage]],
            device_id_type=MESH,
        )

    def out_copy(chunk):
        return pltpu.make_async_copy(whole.at[chunk], merged.at[chunk], out_sem.at[chunk])

    def produce(chunk):
        for copy in loads(chunk):
            copy.wait()
        slot = lax.rem(chunk, 2)
        live = lax.broadcasted_iota(jnp.int32, (packed, width), 0) < total
        left = jnp.where(live, left_in[slot], LOW(0))
        right = jnp.where(live, right_in[slot], LOW(0))
        product = dot(left, right, 0, 0).astype(LOW)
        for shard in range(owners):
            part[chunk, shard % 2, shard // 2] = product[shard * part_rows : (shard + 1) * part_rows]
        exchange(0, chunk).start()

    def add(mine, theirs):
        return (mine.astype(F32) + theirs.astype(F32)).astype(LOW)

    def take(stage, chunk):
        exchange(stage - 1, chunk).wait_recv()
        if stage == 1:
            hold_x[chunk] = add(part[chunk, core], got_core[chunk])
        elif stage == 2:
            hold_y[chunk] = add(hold_x[chunk, x_half], got_x[chunk]).reshape(hold_y.shape[1:])
        elif stage == 3:
            hold_a[chunk] = add(hold_y[chunk, y_half], got_y[chunk]).reshape(hold_a.shape[1:])
        elif stage == 4:
            hold_b[chunk] = add(hold_a[chunk, a_half], got_a[chunk]).reshape(hold_b.shape[1:])
        elif stage == 5:
            whole[chunk, pl.ds(at_b, sixteenth), :] = add(hold_b[chunk, b_half], got_b[chunk])
        if stage < 8:
            exchange(stage, chunk).start()
        else:
            out_copy(chunk).start()

    def sums_exchange(turn):
        return pltpu.make_async_remote_copy(
            src_ref=sums_hold.at[turn],
            dst_ref=sums_got.at[turn],
            send_sem=sums_send.at[turn],
            recv_sem=sums_recv.at[turn],
            device_id=route[turn],
            device_id_type=MESH,
        )

    def back_copies():
        sent = []
        for which, (source, target) in enumerate(((grad, grad_back), (layer_out, layer_back))):
            for place, other in enumerate(others):
                sent.append(
                    pltpu.make_async_remote_copy(
                        src_ref=source.at[:, pl.ds(pl.multiple_of(other * rows, rows), rows), :],
                        dst_ref=target.at[pl.ds(var * each, each)],
                        send_sem=back_send.at[which, place],
                        recv_sem=back_recv.at[which, place],
                        device_id=(win, other),
                        device_id_type=MESH,
                    )
                )
        return sent

    def own_copies():
        return [
            pltpu.make_async_copy(
                source.at[:, pl.ds(pl.multiple_of(var * rows, rows), rows), :],
                target.at[pl.ds(var * each, each)],
                own_sem.at[which],
            )
            for which, (source, target) in enumerate(((grad, grad_back), (layer_out, layer_back)))
        ]

    for copy in loads(0):
        copy.start()
    for copy in own_copies():
        copy.start()
    sums_hold[0] = sums[...]
    sums_exchange(0).start()

    def step(now, carry):
        @pl.when(now + 1 < chunks)
        def _():
            for copy in loads(now + 1):
                copy.start()

        @pl.when(now < chunks)
        def _():
            produce(now)

        for stage in range(1, 9):
            lag = LAGS[stage]

            @pl.when(jnp.logical_and(now >= lag, now < chunks + lag))
            def _(stage=stage, lag=lag):
                take(stage, now - lag)

        for turn in range(5):

            @pl.when(now == 2 * turn + 4)
            def _(turn=turn):
                sums_exchange(turn).wait_recv()
                summed = sums_hold[turn] + sums_got[turn]
                if turn < 4:
                    sums_hold[turn + 1] = summed
                    sums_exchange(turn + 1).start()
                else:
                    sums_out[...] = summed

        @pl.when(now == chunks + 1)
        def _():
            for copy in back_copies():
                copy.start()

        return carry

    lax.fori_loop(0, chunks + LAGS[8], step, 0)

    def settle(chunk, carry):
        for stage in range(8):
            exchange(stage, chunk).wait_send()
        out_copy(chunk).wait()
        return carry

    lax.fori_loop(0, chunks, settle, 0)
    for turn in range(5):
        sums_exchange(turn).wait_send()
    for copy in own_copies():
        copy.wait()
    for copy in back_copies():
        copy.wait()


SETTLED = (2, 3, 4, 5, 6, 7, 8)
LAG = 2
DEPTH = 4
Y_FIRST = (1, 7)
Z_FIRST = (4, 10)


class Network:
    def __init__(self, owners, part, got, whole, merged, send_sem, recv_sem, out_sem):
        self.owners, self.part, self.got, self.whole = owners, part, got, whole
        self.merged, self.send_sem, self.recv_sem, self.out_sem = merged, send_sem, recv_sem, out_sem
        self.chunks, self.rows = whole.shape[0], whole.shape[1]
        self.ring = part.shape[0]
        win, var = lax.axis_index("win"), lax.axis_index("var")
        self.win, self.var = win, var
        self.core = half_of(var, 1)
        self.along = {
            "core": (self.core, (win, flip(var, 1))),
            "x": (half_of(var, 2), (win, flip(var, 2))),
            "y": (half_of(win, 1), (flip(win, 1), var)),
            "z": (half_of(win, 2), (flip(win, 2), var)),
            "w": (half_of(win, 4), (flip(win, 4), var)),
        }
        unit, at, self.places = self.rows // 8, 0, {}
        for stage, name in ((7, "y"), (6, "z"), (5, "w")):
            size = (1 << (stage - 5)) * unit
            at = pl.multiple_of(at + self.along[name][0] * size, size)
            self.places[stage] = (at, size)

    @staticmethod
    def way(chunk):
        place = chunk % 12

        def among(chosen):
            return sum(1 - ((place - one) * (place - one) + 143) // 144 for one in chosen)

        return among(Y_FIRST), among(Z_FIRST)

    def hop(self, stage, chunk):
        name = ("core", "x", "y", "z", "w", "w", "z", "y")[stage]
        if stage not in (1, 2, 3):
            return self.along[name]
        y_first, z_first = self.way(chunk)
        shares = {
            1: ((1 - y_first - z_first, "x"), (y_first, "y"), (z_first, "z")),
            2: ((1 - y_first - z_first, "y"), (y_first + z_first, "x")),
            3: ((1 - z_first, "z"), (z_first, "y")),
        }[stage]
        half, win, var = 0, 0, 0
        for share, name in shares:
            bit, (to_win, to_var) = self.along[name]
            half, win, var = half + share * bit, win + share * to_win, var + share * to_var
        return half, (win, var)

    def part_of(self, stage, half):
        size = self.got[stage].shape[1]
        return pl.ds(pl.multiple_of(half * size, 16), size)

    def exchange(self, stage, chunk):
        half, beyond = self.hop(stage, chunk)
        if stage == 0:
            source, target = self.part.at[chunk % self.ring, 1 - half], self.got[0].at[chunk]
        elif stage < 5:
            source, target = self.got[stage - 1].at[chunk, self.part_of(stage, 1 - half), :], self.got[stage].at[chunk]
        else:
            at, size = self.places[stage]
            source = target = self.whole.at[chunk, pl.ds(at, size), :]
        return pltpu.make_async_remote_copy(
            src_ref=source,
            dst_ref=target,
            send_sem=self.send_sem.at[stage, chunk],
            recv_sem=self.recv_sem.at[stage, chunk],
            device_id=beyond,
            device_id_type=MESH,
        )

    def out_copy(self, chunk):
        return pltpu.make_async_copy(self.whole.at[chunk], self.merged.at[chunk], self.out_sem.at[chunk])

    def emit(self, chunk, place, left, right):
        product = dot(left, right, 0, 0).astype(LOW)
        slot = chunk % self.ring

        @pl.when(chunk >= self.ring)
        def _():
            self.exchange(0, chunk - self.ring).wait_send()

        rows, quarter = self.rows, self.rows // 4
        y_first, z_first = self.way(place)
        for shard in range(self.owners):
            core, x = shard % 2, shard // 2
            for y in range(2):
                for z in range(2):
                    straight, over_y, over_z = 4 * x + 2 * y + z, 4 * y + 2 * x + z, 4 * z + 2 * x + y
                    at = straight + y_first * (over_y - straight) + z_first * (over_z - straight)
                    here = shard * rows + (2 * y + z) * quarter
                    self.part[slot, core, pl.ds(at * quarter, quarter), :] = product[here : here + quarter]
        self.exchange(0, chunk).start()

    def take(self, stage, chunk):
        def add(mine, target):
            return (mine.astype(F32) + target[chunk].astype(F32)).astype(LOW)

        self.exchange(stage - 1, chunk).wait_recv()
        if stage == 1:
            target = self.got[0]
            target[chunk] = add(self.part[chunk % self.ring, self.core], target)
        elif stage <= 4:
            half, _ = self.hop(stage - 1, chunk)
            target = self.got[stage - 1]
            target[chunk] = add(self.got[stage - 2][chunk, self.part_of(stage - 1, half), :], target)
        elif stage == 5:
            half, _ = self.hop(4, chunk)
            at, unit = self.places[5]
            self.whole[chunk, pl.ds(at, unit), :] = add(self.got[3][chunk, self.part_of(4, half), :], self.got[4])
        if stage == 1:

            @pl.when(chunk < DEPTH)
            def _():
                self.exchange(1, chunk).start()
        elif stage < 8:
            self.exchange(stage, chunk).start()
        else:
            self.out_copy(chunk).start()

    def pump(self, turn):
        for place, stage in enumerate(SETTLED):
            chunk = turn - LAG * place

            @pl.when(jnp.logical_and(chunk >= 0, chunk < self.chunks))
            def _(stage=stage, chunk=chunk):
                self.take(stage, chunk)

            if place == 0:

                @pl.when(turn + DEPTH < self.chunks)
                def _():
                    self.exchange(1, turn + DEPTH).start()

    def settle(self):
        def one(chunk, carry):
            for stage in range(1, 8):
                self.exchange(stage, chunk).wait_send()
            self.out_copy(chunk).wait()
            return carry

        lax.fori_loop(0, self.chunks, one, 0)
        for chunk in range(self.chunks - self.ring, self.chunks):
            self.exchange(0, chunk).wait_send()


def packed_kernel(
    owners, size,
    windows, row_index, inputs, cotangent, w_qkv, w_attn, w_in, w_out, bias_qv, out_bias, bias_in, gain, shift,
    merged, sums_out, layer_back, grad_back, meta,
    x_stage, x, most, most_got, wv_qkv, wv_attn, wv_in, wv_out, g_stage, g, spots, state, lefts, rights, qkv, slope,
    normal, inverse, top, mixed_grad, last_right, sums, part, got_core, got_one, got_two, got_three, got_four, whole,
    sums_hold, sums_got,
    weight_sem, send_sem, recv_sem, out_sem, sums_send, sums_recv, far_send, far_recv, own_sem, most_send, most_recv,
):
    each, length, width = x.shape
    wins, rows = cotangent.shape[0], cotangent.shape[1]
    layers = w_qkv.shape[0]
    hidden_width = w_in.shape[2]
    pieces = hidden_width // width
    strip = width // pieces
    pairs = width // 128
    got = (got_core, got_one, got_two, got_three, got_four)
    layer_out, grad_out = x, g
    net = Network(owners, part, got, whole, merged, send_sem, recv_sem, out_sem)
    win, var = net.win, net.var
    others = [flip(var, 1), flip(var, 2), flip(flip(var, 1), 2)]
    weights = ((w_qkv, wv_qkv), (w_attn, wv_attn), (w_in, wv_in), (w_out, wv_out))

    def fetch(layer, which):
        source, target = weights[which]
        return pltpu.make_async_copy(source.at[layer], target.at[layer], weight_sem.at[layer, which])

    for layer in range(layers):
        for which in range(4):
            fetch(layer, which).start()

    barrier = pltpu.get_barrier_semaphore()
    across = [(flip(win, bit), var) for bit in (1, 2, 4)]
    friends = [(win, other) for other in others] + across
    for friend in friends:
        pl.semaphore_signal(barrier, inc=1, device_id=friend, device_id_type=MESH)
    order = assign(windows, wins, owners)
    for place in range(wins):
        meta[place] = order[place]
        x_stage[place] = inputs[order[place]]
    meta[wins] = var
    pl.semaphore_wait(barrier, len(friends))
    mine = pl.ds(pl.multiple_of(var * rows, rows), rows)

    def remote(source, target, which, place, other):
        return pltpu.make_async_remote_copy(
            src_ref=source,
            dst_ref=target,
            send_sem=far_send.at[which, place],
            recv_sem=far_recv.at[which, place],
            device_id=(win, other),
            device_id_type=MESH,
        )

    def to_owners(stage, target, which):
        return [
            remote(stage.at[pl.ds(other * each, each)], target.at[:, mine, :], which, place, other)
            for place, other in enumerate(others)
        ] + [pltpu.make_async_copy(stage.at[pl.ds(var * each, each)], target.at[:, mine, :], own_sem.at[which])]

    def to_slots(source, target, which):
        home = target.at[pl.ds(var * each, each)]
        return [
            remote(source.at[:, pl.ds(pl.multiple_of(other * rows, rows), rows), :], home, which, place, other)
            for place, other in enumerate(others)
        ] + [pltpu.make_async_copy(source.at[:, mine, :], home, own_sem.at[which])]

    for copy in to_owners(x_stage, x, 3):
        copy.start()
    for place in range(wins):
        g_stage[place] = cotangent[order[place]]

    names, counts = [], []
    for place in range(each):
        name = order[place]
        for owner in range(1, owners):
            name = jnp.where(var == owner, order[owner * each + place], name)
        names.append(name)
        counts.append(windows[name])

    starts = [jnp.int32(0)]
    for count in counts:
        starts.append(starts[-1] + count)
    for place in range(each):
        hits = marks(row_index, names[place], counts[place], length)
        along = lax.broadcasted_iota(jnp.int32, (length, size), 0) + starts[place]
        moved = jnp.where(lax.broadcasted_iota(jnp.int32, (length, size), 1) == along, 1.0, 0.0).astype(LOW)
        spots[place * length : (place + 1) * length] = dot(hits, moved, 1, 0).astype(LOW)

    row = lax.broadcasted_iota(jnp.int32, (size, 128), 0)
    lane = lax.broadcasted_iota(jnp.int32, (size, 128), 1)
    owner = jnp.zeros((size, 128), jnp.int32)
    for start in starts[1:]:
        owner = owner + jnp.where(row >= start, 1, 0)
    key_mark = jnp.where(lane == owner, 1.0, 0.0).astype(LOW)
    query_mark = jnp.where(lane == owner, jnp.where(lane < each, 0.0, -1e30), -1e30).astype(LOW)
    query_mark = jnp.concatenate([query_mark, query_mark], axis=0)
    lane_low, lane_high = lane_masks(128)

    largest = jnp.int32(0)
    for owner in range(owners):
        total = jnp.int32(0)
        for place in range(each):
            total = total + windows[order[owner * each + place]]
        largest = jnp.maximum(largest, total)
    most[0] = jnp.full(most.shape[1:], largest, jnp.int32)
    for turn, friend in enumerate(across):
        copy = pltpu.make_async_remote_copy(
            src_ref=most.at[turn],
            dst_ref=most_got.at[turn],
            send_sem=most_send.at[turn],
            recv_sem=most_recv.at[turn],
            device_id=friend,
            device_id_type=MESH,
        )
        copy.start()
        copy.wait()
        most[turn + 1] = jnp.maximum(most[turn], most_got[turn])
    meta[wins + 1] = jnp.max(most[len(across)])
    for copy in to_owners(x_stage, x, 3):
        copy.wait()
    for copy in to_owners(g_stage, g, 0):
        copy.start()
    state[...] = dot(spots[...], x[...].reshape(each * length, width), 0, 0)
    fetch(0, 0).wait()

    def masked_scores(layer, at):
        query = two_heads(qkv[layer, :, pl.ds(at, 128)], lane_low, lane_high)
        key = qkv[layer, :, pl.ds(at + width, 128)]
        value = qkv[layer, :, pl.ds(at + 2 * width, 128)]
        scores = dot(
            jnp.concatenate([key, key_mark], axis=1), jnp.concatenate([query, query_mark], axis=1), 1, 1
        )
        return query, key, value, scores

    def forward_layer(layer, carry):
        @pl.when(layer > 0)
        def _():
            fetch(layer, 0).wait()

        tokens = state[...].astype(LOW)
        lefts[layer, 0] = tokens
        for which in range(3):
            columns = slice(which * width, (which + 1) * width)
            joint = dot(tokens, wv_qkv[layer, :, columns], 1, 0)
            if which == 0:
                joint = (joint + bias_qv[pl.ds(layer, 1), :width]).astype(LOW) * LOW(0.125)
            elif which == 2:
                joint = (joint + bias_qv[pl.ds(layer, 1), width:]).astype(LOW)
            else:
                joint = joint.astype(LOW)
            qkv[layer, :, columns] = joint
        for pair in range(pairs):
            at = pair * 128
            _, _, value, scores = masked_scores(layer, at)
            peak = jnp.max(scores, axis=0, keepdims=True)
            expo = jnp.exp(scores - peak)
            total = jnp.sum(expo, axis=0, keepdims=True)
            probs = (expo * (1.0 / total)).astype(LOW)
            lefts[layer, 1, :, pl.ds(at, 128)] = join_heads(dot(probs, value, 0, 0)).astype(LOW)
            top[layer, pair] = peak + jnp.log(total)
        for which in range(1, 4):
            fetch(layer, which).wait()
        first = dot(lefts[layer, 1], wv_attn[layer], 1, 0) + out_bias[layer, 0:1, :]
        one, inverse_one = normalize(state[...] + first)
        normal[layer, 0] = one
        after = one * gain[layer, 0:1, :] + shift[layer, 0:1, :]
        after_low = after.astype(LOW)
        lefts[layer, 2] = after_low
        second = jnp.zeros((size, width), F32)
        for piece in range(pieces):
            columns = slice(piece * width, (piece + 1) * width)
            hidden = dot(after_low, wv_in[layer, :, columns], 1, 0) + bias_in[pl.ds(layer, 1), columns]
            squared = hidden * hidden
            bend = jnp.tanh(hidden * (SMOOTH + SMOOTH * CUBIC * squared))
            half = 0.5 + 0.5 * bend
            active = (hidden * half).astype(LOW)
            rise = half + (hidden * half) * (1.0 - bend) * (SMOOTH + SMOOTH * 3.0 * CUBIC * squared)
            slope[layer, :, columns] = rise.astype(LOW)
            for sub in range(pieces):
                lefts[layer, 3 + sub, :, piece * strip : (piece + 1) * strip] = active[
                    :, sub * strip : (sub + 1) * strip
                ]
            second = second + dot(active, wv_out[layer, columns, :], 1, 0)
        two, inverse_two = normalize(after + second + out_bias[layer, 1:2, :])
        normal[layer, 1] = two
        state[...] = two * gain[layer, 1:2, :] + shift[layer, 1:2, :]
        lanes = lax.broadcasted_iota(jnp.int32, (size, 128), 1)
        inverse[layer] = jnp.where(lanes < 64, inverse_one, inverse_two)
        return carry

    lax.fori_loop(0, layers, forward_layer, 0)
    layer_out[...] = dot(spots[...], state[...].astype(LOW), 1, 0).astype(LOW).reshape(layer_out.shape)
    for copy in to_owners(g_stage, g, 0):
        copy.wait()
    state[...] = dot(spots[...], g[...].reshape(each * length, width), 0, 0)
    sums[...] = jnp.zeros_like(sums)

    def add_rows(layer, place, values):
        sums[layer, place : place + 1, :] += jnp.sum(values, axis=0, keepdims=True)

    per_layer = net.chunks // layers

    def backward_layer(step, carry):
        layer = layers - 1 - step
        first = step * per_layer
        turn = step * 7

        def emit(place, left, right):
            net.emit(first + place, place, left, right)

        def take(place):
            net.take(1, first + place)

        grad = state[...]
        two = normal[layer, 1]
        back = normalize_back(grad, gain[layer, 1:2, :], two, inverse[layer, :, 64:65])
        back_low = back.astype(LOW)
        last_right[...] = back_low

        def outer(piece, carry):
            emit(piece, lefts[layer, 3 + piece], last_right[...])

            @pl.when(piece > 0)
            def _():
                take(piece - 1)

            return carry

        lax.fori_loop(0, pieces, outer, 0)
        add_rows(layer, 9, grad * two)
        add_rows(layer, 11, grad)
        add_rows(layer, 3, back_low.astype(F32))
        state[...] = back

        def inner(piece, carry):
            columns = pl.ds(pl.multiple_of(piece * width, width), width)
            active = dot(last_right[...], wv_out[layer, columns, :], 1, 1)
            hidden = (active * slope[layer, :, columns].astype(F32)).astype(LOW)
            sums[layer, pl.ds(4 + piece, 1), :] = jnp.sum(hidden.astype(F32), axis=0, keepdims=True)
            rights[0] = hidden
            emit(pieces + piece, lefts[layer, 2], rights[0])
            state[...] += dot(rights[0], wv_in[layer, :, columns], 1, 1)
            take(pieces + piece - 1)

            @pl.when(piece > 0)
            def _():
                net.pump(turn + piece - 1)

            return carry

        lax.fori_loop(0, pieces, inner, 0)
        back = state[...]
        one = normal[layer, 0]
        add_rows(layer, 8, back * one)
        add_rows(layer, 10, back)
        back = normalize_back(back, gain[layer, 0:1, :], one, inverse[layer, :, 0:1])
        back_low = back.astype(LOW)
        emit(8, lefts[layer, 1], back_low)
        take(7)
        add_rows(layer, 2, back_low.astype(F32))
        mixed_grad[...] = dot(back_low, wv_attn[layer], 1, 1).astype(LOW)
        state[...] = back
        net.pump(turn + 3)
        for pair in range(pairs):
            at = pair * 128
            query, key, value, scores = masked_scores(layer, at)
            grads = two_heads(mixed_grad[:, pl.ds(at, 128)], lane_low, lane_high)
            probs = jnp.exp(scores - top[layer, pair])
            d_probs = dot(value, grads, 1, 1)
            centre = jnp.sum(probs * d_probs, axis=0, keepdims=True)
            d_scores = (probs * (d_probs - centre)).astype(LOW)
            d_query = join_heads(dot(d_scores, key, 0, 0)) * 0.125
            rights[0, :, pl.ds(at, 128)] = d_query.astype(LOW)
            rights[1, :, pl.ds(at, 128)] = dot(d_scores, query, 1, 0).astype(LOW)
            rights[2, :, pl.ds(at, 128)] = dot(probs.astype(LOW), grads, 1, 0).astype(LOW)
        take(8)
        net.pump(turn + 4)

        def last(which, carry):
            emit(9 + which, lefts[layer, 0], rights[which])

            @pl.when(which > 0)
            def _():
                take(8 + which)

            return carry

        lax.fori_loop(0, 3, last, 0)
        net.pump(turn + 5)
        grad = state[...]
        for which in range(3):
            piece = rights[which]
            grad = grad + dot(piece, wv_qkv[layer, :, which * width : (which + 1) * width], 1, 1)
            if which != 1:
                add_rows(layer, which // 2, piece.astype(F32))
        state[...] = grad
        take(11)
        net.pump(turn + 6)
        return carry

    lax.fori_loop(0, layers, backward_layer, 0)
    first_turn = 7 * layers
    grad_out[...] = dot(spots[...], state[...].astype(LOW), 1, 0).astype(LOW).reshape(grad_out.shape)

    route = [partner(axis, bit) for axis, bit in ROUTE]

    def sums_exchange(step):
        return pltpu.make_async_remote_copy(
            src_ref=sums_hold.at[step],
            dst_ref=sums_got.at[step],
            send_sem=sums_send.at[step],
            recv_sem=sums_recv.at[step],
            device_id=route[step],
            device_id_type=MESH,
        )

    sums_hold[0] = sums[...]
    sums_exchange(0).start()

    def step(now, carry):
        net.pump(now)

        @pl.when(now == net.chunks - 1)
        def _():
            for copy in to_slots(grad_out, grad_back, 2) + to_slots(layer_out, layer_back, 1):
                copy.start()

        for place in range(5):

            @pl.when(now == first_turn + 1 + 2 * place)
            def _(place=place):
                sums_exchange(place).wait_recv()
                summed = sums_hold[place] + sums_got[place]
                if place < 4:
                    sums_hold[place + 1] = summed
                    sums_exchange(place + 1).start()
                else:
                    sums_out[...] = summed

        return carry

    lax.fori_loop(first_turn, net.chunks + LAG * (len(SETTLED) - 1), step, 0)
    net.settle()
    for place in range(5):
        sums_exchange(place).wait_send()
    for copy in to_slots(layer_out, layer_back, 1) + to_slots(grad_out, grad_back, 2):
        copy.wait()


def finish_kernel(
    at_var, meta, sums, merged, layer_back, grad_back,
    layer_out, grad_inputs, qkv, attn, in_, out, bias_qv, out_bias, bias_in, gain, shift,
    chunks, layer_in, grad_in, grad_wide, qkv_wide, attn_wide, in_wide, out_wide, in_sem, out_sem,
):
    wins, rows = layer_back.shape[0], layer_back.shape[1]
    layers, width = qkv.shape[0], merged.shape[2]
    part_rows = merged.shape[1]
    per_layer = merged.shape[0] // layers
    loads = [
        pltpu.make_async_copy(grad_back, grad_in, in_sem.at[0]),
        pltpu.make_async_copy(layer_back, layer_in, in_sem.at[1]),
    ] + [
        pltpu.make_async_copy(
            merged.at[pl.ds(half * per_layer, per_layer)], chunks.at[pl.ds(half * per_layer, per_layer)], in_sem.at[2 + half]
        )
        for half in range(layers)
    ]
    for load in loads:
        load.start()

    def home(place):
        window = meta[place]
        return (
            pltpu.make_async_copy(grad_wide.at[place], grad_inputs.at[window], out_sem.at[0, place]),
            pltpu.make_async_copy(layer_in.at[place], layer_out.at[window], out_sem.at[1, place]),
        )

    def outs(layer):
        return [
            pltpu.make_async_copy(source.at[layer], target.at[layer], out_sem.at[2 + layer, which])
            for which, (source, target) in enumerate(
                ((qkv_wide, qkv), (attn_wide, attn), (in_wide, in_), (out_wide, out))
            )
        ]

    loads[0].wait()
    loads[1].wait()

    def send(place, carry):
        grad_wide[place] = grad_in[place].astype(F32)
        for copy in home(place):
            copy.start()
        return carry

    lax.fori_loop(0, wins, send, 0)
    for half in range(layers):
        loads[2 + half].wait()
        layer, base = layers - 1 - half, half * per_layer

        def widen(block, carry, layer=layer, base=base):
            at = pl.multiple_of(block * 32, 32)
            here = pl.ds(at, 32)
            for which in range(4):
                columns = slice(which * width, (which + 1) * width)
                there = pl.ds(pl.multiple_of(at + which * part_rows, 32), 32)
                out_wide[layer, there, :] = chunks[base + which, here, :].astype(F32)
                in_wide[layer, here, columns] = chunks[base + 4 + which, here, :].astype(F32)
                if which < 3:
                    qkv_wide[layer, here, columns] = chunks[base + 9 + which, here, :].astype(F32)
            attn_wide[layer, here, :] = chunks[base + 8, here, :].astype(F32)
            return carry

        lax.fori_loop(0, part_rows // 32, widen, 0)
        for copy in outs(layer):
            copy.start()

    var = meta[at_var]
    narrow = out_bias.shape[2]
    at = pl.multiple_of(var * narrow, narrow)
    wide = bias_qv.shape[1]
    for layer in range(layers):
        half = width // wide
        bias_qv[layer : layer + 1, :] = sums[
            layer, pl.ds(var // half, 1), pl.ds(pl.multiple_of(lax.rem(var, half) * wide, wide), wide)
        ]
        bias_in[layer : layer + 1, :] = sums[layer, pl.ds(4 + var, 1), :]
        out_bias[layer] = sums[layer, 2:4, pl.ds(at, narrow)]
        gain[layer] = sums[layer, 8:10, pl.ds(at, narrow)]
        shift[layer] = sums[layer, 10:12, pl.ds(at, narrow)]

    def settle(place, carry):
        for copy in home(place):
            copy.wait()
        return carry

    lax.fori_loop(0, wins, settle, 0)
    for layer in range(layers):
        for copy in outs(layer):
            copy.wait()


def gather_kernel(owners, meta, x, x_out, x_stage, x_send, x_recv, own_sem):
    wins, rows = x.shape[0], x.shape[1]
    each = wins // owners
    me, win = lax.axis_index("var"), lax.axis_index("win")
    others = [(win, flip(me, 1)), (win, flip(me, 2)), (win, flip(flip(me, 1), 2))]
    for place in range(wins):
        x_stage[place] = x[meta[place]]
    greet(others)
    own = pl.ds(pl.multiple_of(me * rows, rows), rows)
    copies = [pltpu.make_async_copy(x_stage.at[pl.ds(me * each, each)], x_out.at[:, own, :], own_sem)]
    for place, other in enumerate(others):
        copies.append(
            pltpu.make_async_remote_copy(
                src_ref=x_stage.at[pl.ds(other[1] * each, each)],
                dst_ref=x_out.at[:, own, :],
                send_sem=x_send.at[place],
                recv_sem=x_recv.at[place],
                device_id=other,
                device_id_type=MESH,
            )
        )
    for copy in copies:
        copy.start()
    for copy in copies:
        copy.wait()


def in_vmem(count):
    return [pl.BlockSpec(memory_space=pltpu.VMEM)] * count


def anywhere(count):
    return [pl.BlockSpec(memory_space=pl.ANY)] * count


def in_smem():
    return [pl.BlockSpec(memory_space=pltpu.SMEM)]


def shaped(shape, kind=LOW):
    return jax.ShapeDtypeStruct(shape, kind)


def whole_windows(
    inputs, counts, row_index, w_qkv, bias_qv, w_attn_out, out_bias, w_in, bias_in, w_ffn_out,
    norm_gain, norm_bias, cotangent,
):
    wins, rows, width = inputs.shape
    owners, groups = lax.axis_size("var"), lax.axis_size("win")
    each, length = wins // owners, rows * owners
    packed = each * length
    layers, hidden_width = w_in.shape[0], w_in.shape[2]
    dma = pltpu.SemaphoreType.DMA

    def params(**more):
        return pltpu.CompilerParams(vmem_limit_bytes=VMEM_BYTES, **more)

    weights = (w_qkv, w_attn_out, w_in, w_ffn_out)
    weight_space = [pltpu.VMEM(weight.shape, LOW) for weight in weights]
    narrow = width // owners
    chunks = layers * 12
    part_rows = width // owners
    half, quarter, eighth = part_rows // 2, part_rows // 4, part_rows // 8
    sums_shape = (layers, 16, width)

    def space(*shape):
        return pltpu.VMEM((chunks,) + shape + (width,), LOW)

    def finish(at_var, meta, merged, sums, layer_back, grad_back):
        rows_shape = (wins, rows, width)
        large = [
            shaped((layers, narrow, 3 * width), F32),
            shaped((layers, narrow, width), F32),
            shaped((layers, narrow, hidden_width), F32),
            shaped((layers, hidden_width // owners, width), F32),
        ]
        layer_out, grad_inputs, *rest = pl.pallas_call(
            functools.partial(finish_kernel, at_var),
            name="finish",
            out_shape=[shaped(rows_shape), shaped(rows_shape, F32)]
            + large
            + [
                shaped((layers, 2 * narrow), F32),
                shaped((layers, 2, narrow), F32),
                shaped((layers, hidden_width // owners), F32),
                shaped((layers, 2, narrow), F32),
                shaped((layers, 2, narrow), F32),
            ],
            in_specs=in_smem() + in_vmem(1) + anywhere(3),
            out_specs=anywhere(6) + in_vmem(5),
            scratch_shapes=[pltpu.VMEM(merged.shape, LOW)]
            + [pltpu.VMEM(rows_shape, LOW)] * 2
            + [pltpu.VMEM(rows_shape, F32)]
            + [pltpu.VMEM(entry.shape, F32) for entry in large]
            + [dma((2 + layers,)), dma((2 + layers, wins))],
            compiler_params=params(),
        )(meta, sums, merged, layer_back, grad_back)
        qkv, attn, in_, out, qv, biases, hidden, gain, shift = rest
        return layer_out, grad_inputs, qkv, qv, attn, biases, in_, hidden, out, gain, shift

    def packed_way():
        size = PACKED
        return pl.pallas_call(
            functools.partial(packed_kernel, owners, size),
            name="packed",
            out_shape=[
                shaped((chunks, part_rows, width)),
                shaped(sums_shape, F32),
                shaped((wins, rows, width)),
                shaped((wins, rows, width)),
                shaped((wins + 2,), jnp.int32),
            ],
            in_specs=in_smem() + in_vmem(3) + anywhere(4) + in_vmem(5),
            out_specs=anywhere(1) + in_vmem(1) + anywhere(2) + in_smem(),
            scratch_shapes=[
                pltpu.VMEM((wins, rows, width), LOW),
                pltpu.VMEM((each, length, width), LOW),
                pltpu.VMEM((4, 8, 128), jnp.int32),
                pltpu.VMEM((3, 8, 128), jnp.int32),
            ]
            + weight_space
            + [
                pltpu.VMEM((wins, rows, width), LOW),
                pltpu.VMEM((each, length, width), LOW),
                pltpu.VMEM((each * length, size), LOW),
                pltpu.VMEM((size, width), F32),
                pltpu.VMEM((layers, 7, size, width), LOW),
                pltpu.VMEM((3, size, width), LOW),
                pltpu.VMEM((layers, size, 3 * width), LOW),
                pltpu.VMEM((layers, size, hidden_width), LOW),
                pltpu.VMEM((layers, 2, size, width), F32),
                pltpu.VMEM((layers, size, 128), F32),
                pltpu.VMEM((layers, width // 128, 1, 2 * size), F32),
                pltpu.VMEM((size, width), LOW),
                pltpu.VMEM((size, width), LOW),
                pltpu.VMEM(sums_shape, F32),
                pltpu.VMEM((4, 2, 2 * part_rows, width), LOW),
                space(2 * part_rows),
                space(part_rows),
                space(half),
                space(quarter),
                space(eighth),
                space(part_rows),
            ]
            + [pltpu.VMEM((5,) + sums_shape, F32)] * 2
            + [dma((layers, 4)), dma((8, chunks)), dma((8, chunks)), dma((chunks,))]
            + [dma((5,))] * 2
            + [dma((4, owners - 1))] * 2
            + [dma((4,))]
            + [dma((3,))] * 2,
            compiler_params=params(collective_id=2, has_side_effects=True),
        )(
            counts, row_index, inputs, cotangent, *weights, bias_qv, out_bias, bias_in, norm_gain, norm_bias
        )

    def ragged_way():
        x, meta = pl.pallas_call(
            functools.partial(spread_kernel, owners),
            name="spread",
            out_shape=[shaped((each, length, width)), shaped((wins + 2 * each + 2,), jnp.int32)],
            in_specs=in_smem() + in_vmem(1),
            out_specs=anywhere(1) + in_smem(),
            scratch_shapes=[
                pltpu.VMEM((wins, rows, width), LOW),
            ]
            + [dma((owners - 1,))] * 2
            + [dma],
            compiler_params=params(collective_id=0, has_side_effects=True),
        )(counts, inputs)
        g = pl.pallas_call(
            functools.partial(gather_kernel, owners),
            name="gather",
            out_shape=shaped((each, length, width)),
            in_specs=in_smem() + in_vmem(1),
            out_specs=pl.BlockSpec(memory_space=pl.ANY),
            scratch_shapes=[pltpu.VMEM((wins, rows, width), LOW)] + [dma((owners - 1,))] * 2 + [dma],
            compiler_params=params(collective_id=3, has_side_effects=True),
        )(meta, cotangent)
        kept = [
            shaped((layers, packed, 3 * width)),
            shaped((layers, packed, hidden_width)),
            shaped((layers, 2, packed, width), F32),
            shaped((layers, packed, 128), F32),
            shaped((layers, packed, width), F32),
        ]
        kept_space = [pltpu.VMEM(entry.shape, entry.dtype) for entry in kept]
        lefts_shape = shaped((layers, 7, packed, width))
        lefts, *stash, layer_rows = pl.pallas_call(
            forward_kernel,
            name="forward",
            out_shape=[lefts_shape] + kept + [shaped((each, length, width))],
            in_specs=in_smem() + in_vmem(2) + anywhere(4) + in_vmem(5),
            out_specs=anywhere(6) + in_vmem(1),
            scratch_shapes=weight_space
            + [pltpu.VMEM(lefts_shape.shape, LOW)]
            + kept_space
            + [pltpu.VMEM((packed, width), F32), dma((layers, 4)), dma((layers, 6, 6))],
            compiler_params=params(),
        )(meta, row_index, x, *weights, bias_qv, out_bias, bias_in, norm_gain, norm_bias)

        rights_shape = shaped((layers, 9, packed, width))
        rights, grad_rows, sums = pl.pallas_call(
            backward_kernel,
            name="backward",
            out_shape=[rights_shape, shaped((each, length, width)), shaped((layers, 16, width), F32)],
            in_specs=in_smem() + in_vmem(2) + anywhere(4) + in_vmem(1) + anywhere(5),
            out_specs=anywhere(1) + in_vmem(2),
            scratch_shapes=weight_space
            + [pltpu.VMEM(rights_shape.shape, LOW)]
            + kept_space
            + [
                pltpu.VMEM((packed, width), F32),
                pltpu.VMEM((packed, width), LOW),
                dma((layers, 4)),
                dma((layers, 5, 6)),
                dma((layers, 6)),
            ],
            compiler_params=params(),
        )(meta, row_index, g, *weights, norm_gain, *stash)

        merged, sums, layer_back, grad_back = pl.pallas_call(
            functools.partial(merge_kernel, owners),
            name="merge",
            out_shape=[
                shaped((chunks, part_rows, width)),
                shaped(sums.shape, F32),
                shaped((wins, rows, width)),
                shaped((wins, rows, width)),
            ],
            in_specs=in_smem() + anywhere(2) + in_vmem(3),
            out_specs=anywhere(1) + in_vmem(1) + anywhere(2),
            scratch_shapes=[pltpu.VMEM((2, packed, width), LOW)] * 2
            + [
                space(2, 2, part_rows),
                space(2, part_rows),
                space(2, part_rows),
                space(part_rows),
                space(2, half),
                space(half),
                space(2, quarter),
                space(quarter),
                space(2, eighth),
                space(eighth),
                space(part_rows),
            ]
            + [pltpu.VMEM((5,) + sums.shape, F32)] * 2
            + [dma((2, 2)), dma((8, chunks)), dma((8, chunks)), dma((chunks,))]
            + [dma((5,))] * 2
            + [dma((2, owners - 1))] * 2
            + [dma((2,))],
            compiler_params=params(collective_id=1, has_side_effects=True),
        )(meta, lefts, rights, sums, layer_rows, grad_rows)
        return finish(wins + 2 * each, meta, merged, sums, layer_back, grad_back)

    *sums_up, order = packed_way()
    return lax.cond(order[wins + 1] <= PACKED, lambda: finish(wins, order, *sums_up), ragged_way)


def choose(*arrays):
    wins, rows, width = arrays[0].shape
    owners, groups = lax.axis_size("var"), lax.axis_size("win")
    fits = owners == 4 and groups == 8 and wins % owners == 0 and rows % 16 == 0
    fits = fits and (wins // owners, rows * owners, width, arrays[7].shape[2]) == (3, 256, 512, 2048)
    return whole_windows(*arrays) if fits else per_device(*arrays)


def solution(mesh):
    return jax.shard_map(
        choose,
        mesh=mesh,
        in_specs=(
            P("win", "var", None),
            P("win"),
            P("win", None),
            P(),
            P(),
            P(),
            P(),
            P(),
            P(),
            P(),
            P(),
            P(),
            P("win", "var", None),
        ),
        out_specs=(
            P("win", "var", None),
            P("win", "var", None),
            P(None, "var", None),
            P(None, "var"),
            P(None, "var", None),
            P(None, None, "var"),
            P(None, "var", None),
            P(None, "var"),
            P(None, "var", None),
            P(None, None, "var"),
            P(None, None, "var"),
        ),
        check_vma=False,
    )
```

```python
import functools

import jax
import jax.numpy as jnp
from jax import lax
from jax.experimental import pallas as pl
from jax.experimental.pallas import tpu as pltpu
from jax.sharding import PartitionSpec as P

HEADS = 8
LAYERS = 2


EPS = 1e-05
LOW = jnp.bfloat16
F32 = jnp.float32
MESH = pl.DeviceIdType.MESH
VMEM_BYTES = 60 << 20
BLOCKS = (256, 224)
PACKED = sum(BLOCKS)
SMOOTH = 0.7978845608028654
CUBIC = 0.044715


def layer_norm(values, gain, shift):
    centre = values - jnp.mean(values, axis=-1, keepdims=True)
    spread = jnp.mean(centre * centre, axis=-1, keepdims=True)
    return centre * lax.rsqrt(spread + EPS) * gain + shift


def smooth(values):
    return jax.nn.gelu(values, approximate=True)


def scores_of(query_heads, key_heads, key_valid, scale):
    raw = (
        jnp.einsum("wqhd,wkhd->whqk", query_heads, key_heads, preferred_element_type=jnp.float32)
        * scale
    )
    return jnp.where(key_valid[:, None, None, :], raw, -1e30)


def per_device(
    inputs,
    counts,
    row_index,
    w_qkv,
    bias_qv,
    w_attn_out,
    out_bias,
    w_in,
    bias_in,
    w_ffn_out,
    norm_gain,
    norm_bias,
    cotangent,
):
    wins, rows, width = inputs.shape
    cycle_size = lax.axis_size("var")
    length = rows * cycle_size
    first_row = lax.axis_index("var") * rows
    head_count = HEADS
    head_size = width // head_count
    scale = head_size ** (-0.5)
    flat = wins * rows
    slots = jnp.arange(length, dtype=jnp.int32)
    live = (slots[None, :] < counts[:, None]).astype(jnp.float32)
    window_ids = jnp.arange(wins, dtype=jnp.int32)[:, None]
    valid = jnp.zeros((wins, length), jnp.float32).at[window_ids, row_index].add(live)
    key_valid = valid > 0.5
    own_valid = lax.dynamic_slice_in_dim(valid, first_row, rows, 1).reshape(flat, 1)
    state = inputs.astype(jnp.float32).reshape(flat, width)
    kept = []
    for which_layer in range(LAYERS):
        x_low = state.astype(jnp.bfloat16)
        joint = jnp.dot(x_low, w_qkv[which_layer], preferred_element_type=jnp.float32)
        query = (joint[:, :width] + bias_qv[which_layer, :width]).astype(jnp.bfloat16)
        keys_low = joint[:, width : 2 * width].astype(jnp.bfloat16)
        values_low = (joint[:, 2 * width :] + bias_qv[which_layer, width:]).astype(jnp.bfloat16)
        pair = jnp.concatenate([keys_low, values_low], axis=1).reshape(wins, rows, 2 * width)
        whole = lax.all_gather(pair, "var", axis=1, tiled=True)
        query_heads = query.reshape(wins, rows, head_count, head_size)
        key_heads = whole[:, :, :width].reshape(wins, length, head_count, head_size)
        value_heads = whole[:, :, width:].reshape(wins, length, head_count, head_size)
        scores = scores_of(query_heads, key_heads, key_valid, scale)
        peak = jnp.max(scores, axis=-1, keepdims=True)
        expo = jnp.exp(scores - peak)
        total = jnp.sum(expo, axis=-1, keepdims=True)
        probs = expo / total
        top = peak + jnp.log(total)
        mixed = (
            jnp.einsum(
                "whqk,wkhd->wqhd",
                probs.astype(jnp.bfloat16),
                value_heads,
                preferred_element_type=jnp.float32,
            )
            .reshape(flat, width)
            .astype(jnp.bfloat16)
        )
        attn = (
            jnp.dot(mixed, w_attn_out[which_layer], preferred_element_type=jnp.float32)
            + out_bias[which_layer, 0]
        )
        normed, norm_one = jax.vjp(
            layer_norm, state + attn, norm_gain[which_layer, 0], norm_bias[which_layer, 0]
        )
        normed_low = normed.astype(jnp.bfloat16)
        hidden = (
            jnp.dot(normed_low, w_in[which_layer], preferred_element_type=jnp.float32)
            + bias_in[which_layer]
        )
        active, gelu_back = jax.vjp(smooth, hidden)
        active_low = active.astype(jnp.bfloat16)
        ffn = (
            jnp.dot(active_low, w_ffn_out[which_layer], preferred_element_type=jnp.float32)
            + out_bias[which_layer, 1]
        )
        state, norm_two = jax.vjp(
            layer_norm, normed + ffn, norm_gain[which_layer, 1], norm_bias[which_layer, 1]
        )
        stored = whole
        kept.append(
            (
                x_low,
                query_heads,
                stored,
                top,
                mixed,
                norm_one,
                normed_low,
                gelu_back,
                active_low,
                norm_two,
            )
        )
    layer_out = (state * own_valid).astype(jnp.bfloat16).reshape(wins, rows, width)
    grad = cotangent.astype(jnp.float32).reshape(flat, width) * own_valid
    collected = []
    for which_layer in reversed(range(LAYERS)):
        (
            x_low,
            query_heads,
            stored,
            top,
            mixed,
            norm_one,
            normed_low,
            gelu_back,
            active_low,
            norm_two,
        ) = kept[which_layer]
        dz_two, gain_two, shift_two = norm_two(grad)
        d_ffn = dz_two.astype(jnp.bfloat16)
        g_ffn_out = jnp.einsum("rf,rd->fd", active_low, d_ffn, preferred_element_type=jnp.float32)
        bias_two = jnp.sum(d_ffn.astype(jnp.float32), axis=0)
        d_active = jnp.einsum(
            "rd,fd->rf", d_ffn, w_ffn_out[which_layer], preferred_element_type=jnp.float32
        )
        (d_hidden,) = gelu_back(d_active)
        d_hidden = d_hidden.astype(jnp.bfloat16)
        g_in = jnp.einsum("rd,rf->df", normed_low, d_hidden, preferred_element_type=jnp.float32)
        g_bias_in = jnp.sum(d_hidden.astype(jnp.float32), axis=0)
        d_normed = dz_two + jnp.einsum(
            "rf,df->rd", d_hidden, w_in[which_layer], preferred_element_type=jnp.float32
        )
        dz_one, gain_one, shift_one = norm_one(d_normed)
        d_attn = dz_one.astype(jnp.bfloat16)
        g_attn_out = jnp.einsum("re,rd->ed", mixed, d_attn, preferred_element_type=jnp.float32)
        bias_one = jnp.sum(d_attn.astype(jnp.float32), axis=0)
        d_mixed = jnp.einsum(
            "rd,ed->re", d_attn, w_attn_out[which_layer], preferred_element_type=jnp.float32
        ).astype(jnp.bfloat16)
        whole = stored
        key_heads = whole[:, :, :width].reshape(wins, length, head_count, head_size)
        value_heads = whole[:, :, width:].reshape(wins, length, head_count, head_size)
        scores = scores_of(query_heads, key_heads, key_valid, scale)
        probs = jnp.exp(scores - top)
        grad_heads = d_mixed.reshape(wins, rows, head_count, head_size)
        d_probs = jnp.einsum(
            "wqhd,wkhd->whqk", grad_heads, value_heads, preferred_element_type=jnp.float32
        )
        centre = jnp.sum(probs * d_probs, axis=-1, keepdims=True)
        d_scores = (probs * (d_probs - centre)).astype(jnp.bfloat16)
        probs_low = probs.astype(jnp.bfloat16)
        d_query = (
            jnp.einsum("whqk,wkhd->wqhd", d_scores, key_heads, preferred_element_type=jnp.float32)
            * scale
        )
        d_query = d_query.reshape(flat, width).astype(jnp.bfloat16)
        span_rows = lax.axis_size("var") * rows
        d_key = (
            jnp.einsum("whqk,wqhd->kwhd", d_scores, query_heads, preferred_element_type=jnp.float32)
            * scale
        )
        d_value = jnp.einsum(
            "whqk,wqhd->kwhd", probs_low, grad_heads, preferred_element_type=jnp.float32
        )
        key_grads = lax.psum_scatter(
            jnp.concatenate(
                [d_key.reshape(span_rows, wins, width), d_value.reshape(span_rows, wins, width)],
                axis=2,
            ).astype(jnp.bfloat16),
            "var",
            scatter_dimension=0,
            tiled=True,
        ).astype(jnp.float32)
        key_grads = (
            jnp.transpose(key_grads, (1, 0, 2)).reshape(flat, 2 * width).astype(jnp.bfloat16)
        )
        d_joint = jnp.concatenate([d_query, key_grads], axis=1)
        g_qkv = jnp.einsum("rd,re->de", x_low, d_joint, preferred_element_type=jnp.float32)
        g_bias_qv = jnp.concatenate(
            [
                jnp.sum(d_query.astype(jnp.float32), axis=0),
                jnp.sum(key_grads[:, width:].astype(jnp.float32), axis=0),
            ]
        )
        grad = dz_one + jnp.einsum(
            "re,de->rd", d_joint, w_qkv[which_layer], preferred_element_type=jnp.float32
        )
        g_out_bias = jnp.stack([bias_one, bias_two])
        g_gain = jnp.stack([gain_one, gain_two])
        g_shift = jnp.stack([shift_one, shift_two])
        terms = (
            g_qkv,
            g_bias_qv,
            g_attn_out,
            g_out_bias,
            g_in,
            g_bias_in,
            g_ffn_out,
            g_gain,
            g_shift,
        )
        collected.append(terms)
    collected = collected[::-1]
    stacked = tuple((jnp.stack([entry[position] for entry in collected]) for position in range(9)))
    shards = (
        lax.psum_scatter(
            stacked[0].astype(jnp.bfloat16), "var", scatter_dimension=1, tiled=True
        ).astype(jnp.float32),
        lax.psum_scatter(
            stacked[1].astype(jnp.bfloat16), "var", scatter_dimension=1, tiled=True
        ).astype(jnp.float32),
        lax.psum_scatter(
            stacked[2].astype(jnp.bfloat16), "var", scatter_dimension=1, tiled=True
        ).astype(jnp.float32),
        lax.psum_scatter(
            stacked[3].astype(jnp.bfloat16), "var", scatter_dimension=2, tiled=True
        ).astype(jnp.float32),
        lax.psum_scatter(
            stacked[4].astype(jnp.bfloat16), "var", scatter_dimension=1, tiled=True
        ).astype(jnp.float32),
        lax.psum_scatter(
            stacked[5].astype(jnp.bfloat16), "var", scatter_dimension=1, tiled=True
        ).astype(jnp.float32),
        lax.psum_scatter(
            stacked[6].astype(jnp.bfloat16), "var", scatter_dimension=1, tiled=True
        ).astype(jnp.float32),
        lax.psum_scatter(
            stacked[7].astype(jnp.bfloat16), "var", scatter_dimension=2, tiled=True
        ).astype(jnp.float32),
        lax.psum_scatter(
            stacked[8].astype(jnp.bfloat16), "var", scatter_dimension=2, tiled=True
        ).astype(jnp.float32),
    )
    stacked = (
        lax.psum(shards[0].astype(jnp.bfloat16), "win").astype(jnp.float32),
        lax.psum(shards[1].astype(jnp.bfloat16), "win").astype(jnp.float32),
        lax.psum(shards[2].astype(jnp.bfloat16), "win").astype(jnp.float32),
        lax.psum(shards[3].astype(jnp.bfloat16), "win").astype(jnp.float32),
        lax.psum(shards[4].astype(jnp.bfloat16), "win").astype(jnp.float32),
        lax.psum(shards[5].astype(jnp.bfloat16), "win").astype(jnp.float32),
        lax.psum(shards[6].astype(jnp.bfloat16), "win").astype(jnp.float32),
        lax.psum(shards[7].astype(jnp.bfloat16), "win").astype(jnp.float32),
        lax.psum(shards[8].astype(jnp.bfloat16), "win").astype(jnp.float32),
    )
    grad_inputs = grad.reshape(wins, rows, width)
    return (
        layer_out,
        grad_inputs,
        stacked[0],
        stacked[1],
        stacked[2],
        stacked[3],
        stacked[4],
        stacked[5],
        stacked[6],
        stacked[7],
        stacked[8],
    )


def dot(left, right, left_dim, right_dim):
    return lax.dot_general(
        left, right, (((left_dim,), (right_dim,)), ((), ())), preferred_element_type=F32
    )


def flip(index, bit):
    return index + bit - 2 * bit * lax.rem(index // bit, 2)


def half_of(index, bit):
    return lax.rem(index // bit, 2)


def partner(axis, bit):
    win, var = lax.axis_index("win"), lax.axis_index("var")
    if axis == "win":
        return (flip(win, bit), var)
    return (win, flip(var, bit))


def greet(partners):
    barrier = pltpu.get_barrier_semaphore()
    for other in partners:
        pl.semaphore_signal(barrier, inc=1, device_id=other, device_id_type=MESH)
    pl.semaphore_wait(barrier, len(partners))


def assign(counts, wins, owners):
    each = wins // owners
    keys = [counts[w] * wins + w for w in range(wins)]
    for stop in range(wins - 1, 0, -1):
        for low in range(stop):
            first, second = keys[low], keys[low + 1]
            keys[low], keys[low + 1] = jnp.maximum(first, second), jnp.minimum(first, second)
    names = [lax.rem(key, wins) for key in keys]
    order = []
    for owner in range(owners):
        order += [names[owner], names[2 * owners - 1 - owner], names[2 * owners + owner]]
    return order


def spread_kernel(
    owners, counts, x, x_out, meta, x_stage, x_send, x_recv, own_sem
):
    wins, rows = x.shape[0], x.shape[1]
    each = wins // owners
    me, win = lax.axis_index("var"), lax.axis_index("win")
    others = [flip(me, 1), flip(me, 2), flip(flip(me, 1), 2)]
    barrier = pltpu.get_barrier_semaphore()
    for other in others:
        pl.semaphore_signal(barrier, inc=1, device_id=(win, other), device_id_type=MESH)
    order = assign(counts, wins, owners)
    for place in range(wins):
        meta[place] = order[place]
        x_stage[place] = x[order[place]]
    pl.semaphore_wait(barrier, len(others))

    sent = []
    for place, other in enumerate(others):
        sent.append(
            pltpu.make_async_remote_copy(
                src_ref=x_stage.at[pl.ds(other * each, each)],
                dst_ref=x_out.at[:, pl.ds(pl.multiple_of(me * rows, rows), rows), :],
                send_sem=x_send.at[place],
                recv_sem=x_recv.at[place],
                device_id=(win, other),
                device_id_type=MESH,
            )
        )
    for copy in sent:
        copy.start()
    own = pl.ds(pl.multiple_of(me * rows, rows), rows)
    own_x = pltpu.make_async_copy(x_stage.at[pl.ds(me * each, each)], x_out.at[:, own, :], own_sem)
    own_x.start()
    padded = jnp.int32(0)
    for place in range(each):
        name = jnp.int32(0)
        for owner in range(owners):
            name = jnp.where(me == owner, order[owner * each + place], name)
        meta[wins + place] = name
        meta[wins + each + place] = counts[name]
        padded = padded + ((counts[name] + 15) // 16) * 16
    meta[wins + 2 * each] = me
    meta[wins + 2 * each + 1] = padded

    own_x.wait()
    for copy in sent:
        copy.wait()


class Plan:
    def __init__(self, meta, wins, each):
        self.names = [meta[wins + place] for place in range(each)]
        self.counts = [meta[wins + each + place] for place in range(each)]
        self.starts = []
        total = jnp.int32(0)
        for count in self.counts:
            self.starts.append(total)
            total = total + ((count + 15) // 16) * 16
        self.total = total
        self.blocks = (total + 127) // 128

    def each_block(self, body):
        def step(block, carry):
            body(128, block, pl.ds(pl.multiple_of(block * 128, 128), 128))
            return carry

        lax.fori_loop(0, self.blocks, step, 0)

    def pick(self, values, window):
        chosen = values[0]
        for place in range(1, len(values)):
            chosen = jnp.where(window == place, values[place], chosen)
        return chosen

    def each_window(self, body):
        def step(window, carry):
            count = self.pick(self.counts, window)
            start = pl.multiple_of(self.pick(self.starts, window), 16)
            body(256, count, pl.ds(start, 256))

            return carry

        lax.fori_loop(0, len(self.counts), step, 0)


def marks(row_index, name, count, length):
    listed = row_index[pl.ds(name, 1), :]
    slot = lax.broadcasted_iota(jnp.int32, (length, length), 0)
    place = lax.broadcasted_iota(jnp.int32, (length, length), 1)
    hit = jnp.logical_and(slot == listed, place < count)
    return jnp.where(hit, 1.0, 0.0).astype(LOW)


def mean_of(values):
    return jnp.mean(values, axis=-1, keepdims=True)


def normalize(values):
    centre = values - mean_of(values)
    inverse = lax.rsqrt(mean_of(centre * centre) + EPS)
    return centre * inverse, inverse


def normalize_back(grad, gain, normal, inverse):
    scaled = grad * gain
    return inverse * (scaled - mean_of(scaled) - normal * mean_of(scaled * normal))


def two_heads(pair, lane_low, lane_high):
    return jnp.concatenate([pair * lane_low, pair * lane_high], axis=0)


def lane_masks(lanes):
    lane = lax.broadcasted_iota(jnp.int32, (1, lanes), 1)
    low = jnp.where(lane < lanes // 2, 1.0, 0.0)
    return low.astype(LOW), (1.0 - low).astype(LOW)


def join_heads(stacked):
    size, lanes = stacked.shape[0] // 2, stacked.shape[1]
    lane = lax.broadcasted_iota(jnp.int32, (size, lanes), 1)
    return jnp.where(lane < lanes // 2, stacked[:size], stacked[size:])


def forward_kernel(
    meta, row_index, x, w_qkv, w_attn, w_in, w_out, bias_qv, out_bias, bias_in, gain, shift,
    lefts_out, qkv_out, slope_out, normal_out, inverse_out, top_out, layer_out,
    wv_qkv, wv_attn, wv_in, wv_out, lefts, qkv, slope, normal, inverse, top, state,
    weight_sem, out_sem,
):
    each, length, width = x.shape
    wins = row_index.shape[0]
    layers = w_qkv.shape[0]
    hidden_width = w_in.shape[2]
    pieces = hidden_width // width
    part = width // pieces
    plan = Plan(meta, wins, each)
    weights = ((w_qkv, wv_qkv), (w_attn, wv_attn), (w_in, wv_in), (w_out, wv_out))

    def fetch(layer, which):
        source, target = weights[which]
        return pltpu.make_async_copy(
            source.at[layer], target.at[layer], weight_sem.at[layer, which]
        )

    for layer in range(layers):
        for which in range(4):
            fetch(layer, which).start()

    state[...] = jnp.zeros_like(state)
    for layer in range(layers):
        lefts[layer, 1] = jnp.zeros(lefts.shape[2:], LOW)
        qkv[layer] = jnp.zeros(qkv.shape[1:], LOW)
    for place in range(each):
        hits = marks(row_index, plan.names[place], plan.counts[place], length)
        start = pl.multiple_of(plan.starts[place], 16)
        state[pl.ds(start, length), :] = dot(hits, x[place], 0, 0)

    kept = (
        (lefts, lefts_out, lambda ref, layer, rows: ref.at[layer, :, rows, :]),
        (qkv, qkv_out, lambda ref, layer, rows: ref.at[layer, rows, :]),
        (slope, slope_out, lambda ref, layer, rows: ref.at[layer, rows, :]),
        (normal, normal_out, lambda ref, layer, rows: ref.at[layer, :, rows, :]),
        (inverse, inverse_out, lambda ref, layer, rows: ref.at[layer, rows, :]),
        (top, top_out, lambda ref, layer, rows: ref.at[layer, rows, :]),
    )

    def stores(layer, block, rows):
        return [
            pltpu.make_async_copy(
                view(source, layer, rows), view(target, layer, rows), out_sem.at[layer, which, block]
            )
            for which, (source, target, view) in enumerate(kept)
        ]

    lane_low, lane_high = lane_masks(128)

    def one_layer(layer, carry):
        fetch(layer, 0).wait()

        def project(size, block, rows):
            tokens = state[rows, :].astype(LOW)
            lefts[layer, 0, rows, :] = tokens
            for which in range(3):
                columns = slice(which * width, (which + 1) * width)
                joint = dot(tokens, wv_qkv[layer, :, columns], 1, 0)
                if which == 0:
                    joint = (joint + bias_qv[pl.ds(layer, 1), :width]).astype(LOW) * LOW(0.125)
                elif which == 2:
                    joint = (joint + bias_qv[pl.ds(layer, 1), width:]).astype(LOW)
                else:
                    joint = joint.astype(LOW)
                qkv[layer, rows, columns] = joint

        plan.each_block(project)

        def attend(size, count, rows):
            column = lax.broadcasted_iota(jnp.int32, (2 * size, size), 1)
            live = column < count

            def pair(which, carry):
                at = pl.multiple_of(which * 128, 128)
                query = two_heads(qkv[layer, rows, pl.ds(at, 128)], lane_low, lane_high)
                key = qkv[layer, rows, pl.ds(pl.multiple_of(at + width, 128), 128)]
                value = qkv[layer, rows, pl.ds(pl.multiple_of(at + 2 * width, 128), 128)]
                scores = jnp.where(live, dot(query, key, 1, 1), -1e30)
                peak = jnp.max(scores, axis=-1, keepdims=True)
                expo = jnp.exp(scores - peak)
                total = jnp.sum(expo, axis=-1, keepdims=True)
                probs = (expo * (1.0 / total)).astype(LOW)
                lefts[layer, 1, rows, pl.ds(at, 128)] = join_heads(dot(probs, value, 1, 0)).astype(LOW)
                logs = jnp.broadcast_to(peak + jnp.log(total), (2 * size, 128))
                top[layer, rows, pl.ds(at, 128)] = join_heads(logs)
                return carry

            lax.fori_loop(0, width // 128, pair, 0)

        plan.each_window(attend)
        for which in range(1, 4):
            fetch(layer, which).wait()

        def feed(size, block, rows):
            first = dot(lefts[layer, 1, rows, :], wv_attn[layer], 1, 0) + out_bias[layer, 0:1, :]
            one, inverse_one = normalize(state[rows, :] + first)
            normal[layer, 0, rows, :] = one
            after = one * gain[layer, 0:1, :] + shift[layer, 0:1, :]
            after_low = after.astype(LOW)
            lefts[layer, 2, rows, :] = after_low
            second = jnp.zeros((size, width), F32)
            for piece in range(pieces):
                columns = slice(piece * width, (piece + 1) * width)
                hidden = dot(after_low, wv_in[layer, :, columns], 1, 0) + bias_in[pl.ds(layer, 1), columns]
                squared = hidden * hidden
                bend = jnp.tanh(SMOOTH * hidden * (1.0 + CUBIC * squared))
                half = 0.5 * (1.0 + bend)
                active = (hidden * half).astype(LOW)
                rise = half + 0.5 * hidden * (1.0 - bend * bend) * (
                    SMOOTH * (1.0 + 3.0 * CUBIC * squared)
                )
                slope[layer, rows, columns] = rise.astype(LOW)
                for sub in range(pieces):
                    lefts[layer, 3 + sub, rows, piece * part : (piece + 1) * part] = active[
                        :, sub * part : (sub + 1) * part
                    ]
                second = second + dot(active, wv_out[layer, columns, :], 1, 0)
            two, inverse_two = normalize(after + second + out_bias[layer, 1:2, :])
            normal[layer, 1, rows, :] = two
            state[rows, :] = two * gain[layer, 1:2, :] + shift[layer, 1:2, :]
            lane = lax.broadcasted_iota(jnp.int32, (size, 128), 1)
            inverse[layer, rows, :] = jnp.where(lane < 64, inverse_one, inverse_two)
            for copy in stores(layer, block, rows):
                copy.start()

        plan.each_block(feed)
        return carry

    lax.fori_loop(0, layers, one_layer, 0)
    for place in range(each):
        hits = marks(row_index, plan.names[place], plan.counts[place], length)
        start = pl.multiple_of(plan.starts[place], 16)
        layer_out[place] = dot(hits, state[pl.ds(start, length), :].astype(LOW), 1, 0).astype(LOW)

    for layer in range(layers):

        def finish(size, block, rows, layer=layer):
            for copy in stores(layer, block, rows):
                copy.wait()

        plan.each_block(finish)


def backward_kernel(
    meta, row_index, g, w_qkv, w_attn, w_in, w_out, gain,
    qkv_in, slope_in, normal_in, inverse_in, top_in,
    rights_out, grad_out, sums,
    wv_qkv, wv_attn, wv_in, wv_out, rights, qkv, slope, normal, inverse, top, state, mixed_grad,
    weight_sem, in_sem, out_sem,
):
    each, length, width = g.shape
    wins = row_index.shape[0]
    layers = w_qkv.shape[0]
    hidden_width = w_in.shape[2]
    pieces = hidden_width // width
    plan = Plan(meta, wins, each)
    weights = ((w_out, wv_out), (w_in, wv_in), (w_attn, wv_attn), (w_qkv, wv_qkv))

    def fetch(layer, which):
        source, target = weights[which]
        return pltpu.make_async_copy(
            source.at[layer], target.at[layer], weight_sem.at[layer, which]
        )

    kept = (
        (normal_in, normal, lambda ref, layer, rows: ref.at[layer, :, rows, :]),
        (inverse_in, inverse, lambda ref, layer, rows: ref.at[layer, rows, :]),
        (slope_in, slope, lambda ref, layer, rows: ref.at[layer, rows, :]),
        (qkv_in, qkv, lambda ref, layer, rows: ref.at[layer, rows, :]),
        (top_in, top, lambda ref, layer, rows: ref.at[layer, rows, :]),
    )

    def loads(layer, block, rows):
        return [
            pltpu.make_async_copy(
                view(source, layer, rows), view(target, layer, rows), in_sem.at[layer, which, block]
            )
            for which, (source, target, view) in enumerate(kept)
        ]

    for layer in range(layers):
        qkv[layer, 128:] = jnp.zeros((qkv.shape[1] - 128, qkv.shape[2]), LOW)
    for layer in reversed(range(layers)):

        def begin(size, block, rows, layer=layer):
            for copy in loads(layer, block, rows):
                copy.start()

        fetch(layer, 0).start()
        plan.each_block(begin)
        for which in range(1, 4):
            fetch(layer, which).start()

    state[...] = jnp.zeros_like(state)
    mixed_grad[...] = jnp.zeros_like(mixed_grad)
    sums[...] = jnp.zeros_like(sums)
    for layer in range(layers):
        rights[layer, 0:3] = jnp.zeros((3,) + rights.shape[2:], LOW)
    for place in range(each):
        hits = marks(row_index, plan.names[place], plan.counts[place], length)
        start = pl.multiple_of(plan.starts[place], 16)
        state[pl.ds(start, length), :] = dot(hits, g[place], 0, 0)

    lane_low, lane_high = lane_masks(128)

    def add_rows(layer, place, values):
        sums[layer, place : place + 1, :] += jnp.sum(values, axis=0, keepdims=True)

    def one_layer(step, carry):
        layer = layers - 1 - step
        for which in range(3):
            fetch(layer, which).wait()

        def feed(size, block, rows):
            for copy in loads(layer, block, rows):
                copy.wait()
            grad = state[rows, :]
            two = normal[layer, 1, rows, :]
            add_rows(layer, 9, grad * two)
            add_rows(layer, 11, grad)
            back = normalize_back(grad, gain[layer, 1:2, :], two, inverse[layer, rows, 64:65])
            back_low = back.astype(LOW)
            rights[layer, 8, rows, :] = back_low
            add_rows(layer, 3, back_low.astype(F32))
            for piece in range(pieces):
                columns = slice(piece * width, (piece + 1) * width)
                active = dot(back_low, wv_out[layer, columns, :], 1, 1)
                hidden = (active * slope[layer, rows, columns].astype(F32)).astype(LOW)
                rights[layer, 4 + piece, rows, :] = hidden
                add_rows(layer, 4 + piece, hidden.astype(F32))
                back = back + dot(hidden, wv_in[layer, :, columns], 1, 1)
            one = normal[layer, 0, rows, :]
            add_rows(layer, 8, back * one)
            add_rows(layer, 10, back)
            back = normalize_back(back, gain[layer, 0:1, :], one, inverse[layer, rows, 0:1])
            back_low = back.astype(LOW)
            rights[layer, 3, rows, :] = back_low
            add_rows(layer, 2, back_low.astype(F32))
            mixed_grad[rows, :] = dot(back_low, wv_attn[layer], 1, 1).astype(LOW)
            state[rows, :] = back

        plan.each_block(feed)

        def attend(size, count, rows):
            row = lax.broadcasted_iota(jnp.int32, (2 * size, size), 0)
            column = lax.broadcasted_iota(jnp.int32, (2 * size, size), 1)
            row = jnp.where(row < size, row, row - size)
            live = jnp.logical_and(column < count, row < count)

            def pair(which, carry):
                at = pl.multiple_of(which * 128, 128)
                query = two_heads(qkv[layer, rows, pl.ds(at, 128)], lane_low, lane_high)
                key = qkv[layer, rows, pl.ds(pl.multiple_of(at + width, 128), 128)]
                value = qkv[layer, rows, pl.ds(pl.multiple_of(at + 2 * width, 128), 128)]
                grad = two_heads(mixed_grad[rows, pl.ds(at, 128)], lane_low, lane_high)
                logs = top[layer, rows, pl.ds(at, 128)]
                logs = jnp.concatenate([logs[:, 0:1], logs[:, 64:65]], axis=0)
                probs = jnp.where(live, jnp.exp(dot(query, key, 1, 1) - logs), 0.0)
                d_probs = dot(grad, value, 1, 1)
                centre = jnp.sum(probs * d_probs, axis=-1, keepdims=True)
                d_scores = (probs * (d_probs - centre)).astype(LOW)
                d_query = join_heads(dot(d_scores, key, 1, 0)) * 0.125
                rights[layer, 0, rows, pl.ds(at, 128)] = d_query.astype(LOW)
                rights[layer, 1, rows, pl.ds(at, 128)] = dot(d_scores, query, 0, 0).astype(LOW)
                rights[layer, 2, rows, pl.ds(at, 128)] = dot(probs.astype(LOW), grad, 0, 0).astype(LOW)
                return carry

            lax.fori_loop(0, width // 128, pair, 0)

        plan.each_window(attend)
        fetch(layer, 3).wait()

        def project(size, block, rows):
            grad = state[rows, :]
            for which in range(3):
                columns = slice(which * width, (which + 1) * width)
                piece = rights[layer, which, rows, :]
                grad = grad + dot(piece, wv_qkv[layer, :, columns], 1, 1)
                if which != 1:
                    add_rows(layer, which // 2, piece.astype(F32))
            state[rows, :] = grad
            pltpu.make_async_copy(
                rights.at[layer, :, rows, :], rights_out.at[layer, :, rows, :], out_sem.at[layer, block]
            ).start()

        plan.each_block(project)
        return carry

    lax.fori_loop(0, layers, one_layer, 0)
    for place in range(each):
        hits = marks(row_index, plan.names[place], plan.counts[place], length)
        start = pl.multiple_of(plan.starts[place], 16)
        grad_out[place] = dot(hits, state[pl.ds(start, length), :].astype(LOW), 1, 0).astype(LOW)

    for layer in range(layers):

        def finish(size, block, rows, layer=layer):
            pltpu.make_async_copy(
                rights.at[layer, :, rows, :], rights_out.at[layer, :, rows, :], out_sem.at[layer, block]
            ).wait()

        plan.each_block(finish)


LAGS = (0, 1, 3, 4, 5, 6, 7, 8, 9)
ROUTE = (("var", 1), ("var", 2), ("win", 1), ("win", 2), ("win", 4))


def merge_kernel(
    owners, meta, lefts, rights, sums, layer_out, grad,
    merged, sums_out, layer_back, grad_back,
    left_in, right_in, part, got_core, hold_x, got_x, hold_y, got_y, hold_a, got_a, hold_b, got_b,
    whole, sums_hold, sums_got,
    in_sem, send_sem, recv_sem, out_sem, sums_send, sums_recv, back_send, back_recv, own_sem,
):
    chunks = merged.shape[0]
    layers = lefts.shape[0]
    per_layer = chunks // layers
    packed, width = left_in.shape[1], left_in.shape[2]
    part_rows = part.shape[3]
    each = layer_out.shape[0]
    rows = layer_back.shape[1]
    win, var = lax.axis_index("win"), lax.axis_index("var")
    core, x_half = half_of(var, 1), half_of(var, 2)
    y_half, a_half, b_half = half_of(win, 1), half_of(win, 2), half_of(win, 4)
    others = [flip(var, 1), flip(var, 2), flip(flip(var, 1), 2)]
    route = [partner(axis, bit) for axis, bit in ROUTE]
    greet(route + [(win, others[2])])
    total = meta[meta.shape[0] - 1]

    def block_of(chunk):
        layer, place = layers - 1 - chunk // per_layer, lax.rem(chunk, per_layer)
        group, member = place // 4, lax.rem(place, 4)
        first, third = (2 - group) // 2, group // 2
        second = 1 - first - third
        alone = 1 - (member + 3) // 4
        left = first * (3 + member) + second * 2 + third * alone
        right = first * 8 + second * (4 + member) + third * (member - 1 + 4 * alone)
        return layer, left, right

    def loads(chunk):
        layer, left, right = block_of(chunk)
        slot = lax.rem(chunk, 2)
        return (
            pltpu.make_async_copy(lefts.at[layer, left], left_in.at[slot], in_sem.at[0, slot]),
            pltpu.make_async_copy(rights.at[layer, right], right_in.at[slot], in_sem.at[1, slot]),
        )

    quarter = part_rows // 2
    eighth = quarter // 2
    sixteenth = eighth // 2
    at_y = pl.multiple_of(y_half * quarter, sixteenth)
    at_a = pl.multiple_of(at_y + a_half * eighth, sixteenth)
    at_b = pl.multiple_of(at_a + b_half * sixteenth, sixteenth)

    def exchange(stage, chunk):
        if stage == 0:
            source, target = part.at[chunk, 1 - core], got_core.at[chunk]
        elif stage == 1:
            source, target = hold_x.at[chunk, 1 - x_half], got_x.at[chunk]
        elif stage == 2:
            source, target = hold_y.at[chunk, 1 - y_half], got_y.at[chunk]
        elif stage == 3:
            source, target = hold_a.at[chunk, 1 - a_half], got_a.at[chunk]
        elif stage == 4:
            source, target = hold_b.at[chunk, 1 - b_half], got_b.at[chunk]
        else:
            at, size = ((at_b, sixteenth), (at_a, eighth), (at_y, quarter))[stage - 5]
            source = whole.at[chunk, pl.ds(at, size), :]
            target = source
        return pltpu.make_async_remote_copy(
            src_ref=source,
            dst_ref=target,
            send_sem=send_sem.at[stage, chunk],
            recv_sem=recv_sem.at[stage, chunk],
            device_id=route[(0, 1, 2, 3, 4, 4, 3, 2)[stage]],
            device_id_type=MESH,
        )

    def out_copy(chunk):
        return pltpu.make_async_copy(whole.at[chunk], merged.at[chunk], out_sem.at[chunk])

    def produce(chunk):
        for copy in loads(chunk):
            copy.wait()
        slot = lax.rem(chunk, 2)
        live = lax.broadcasted_iota(jnp.int32, (packed, width), 0) < total
        left = jnp.where(live, left_in[slot], LOW(0))
        right = jnp.where(live, right_in[slot], LOW(0))
        product = dot(left, right, 0, 0).astype(LOW)
        for shard in range(owners):
            part[chunk, shard % 2, shard // 2] = product[shard * part_rows : (shard + 1) * part_rows]
        exchange(0, chunk).start()

    def add(mine, theirs):
        return (mine.astype(F32) + theirs.astype(F32)).astype(LOW)

    def take(stage, chunk):
        exchange(stage - 1, chunk).wait_recv()
        if stage == 1:
            hold_x[chunk] = add(part[chunk, core], got_core[chunk])
        elif stage == 2:
            hold_y[chunk] = add(hold_x[chunk, x_half], got_x[chunk]).reshape(hold_y.shape[1:])
        elif stage == 3:
            hold_a[chunk] = add(hold_y[chunk, y_half], got_y[chunk]).reshape(hold_a.shape[1:])
        elif stage == 4:
            hold_b[chunk] = add(hold_a[chunk, a_half], got_a[chunk]).reshape(hold_b.shape[1:])
        elif stage == 5:
            whole[chunk, pl.ds(at_b, sixteenth), :] = add(hold_b[chunk, b_half], got_b[chunk])
        if stage < 8:
            exchange(stage, chunk).start()
        else:
            out_copy(chunk).start()

    def sums_exchange(turn):
        return pltpu.make_async_remote_copy(
            src_ref=sums_hold.at[turn],
            dst_ref=sums_got.at[turn],
            send_sem=sums_send.at[turn],
            recv_sem=sums_recv.at[turn],
            device_id=route[turn],
            device_id_type=MESH,
        )

    def back_copies():
        sent = []
        for which, (source, target) in enumerate(((grad, grad_back), (layer_out, layer_back))):
            for place, other in enumerate(others):
                sent.append(
                    pltpu.make_async_remote_copy(
                        src_ref=source.at[:, pl.ds(pl.multiple_of(other * rows, rows), rows), :],
                        dst_ref=target.at[pl.ds(var * each, each)],
                        send_sem=back_send.at[which, place],
                        recv_sem=back_recv.at[which, place],
                        device_id=(win, other),
                        device_id_type=MESH,
                    )
                )
        return sent

    def own_copies():
        return [
            pltpu.make_async_copy(
                source.at[:, pl.ds(pl.multiple_of(var * rows, rows), rows), :],
                target.at[pl.ds(var * each, each)],
                own_sem.at[which],
            )
            for which, (source, target) in enumerate(((grad, grad_back), (layer_out, layer_back)))
        ]

    for copy in loads(0):
        copy.start()
    for copy in own_copies():
        copy.start()
    sums_hold[0] = sums[...]
    sums_exchange(0).start()

    def step(now, carry):
        @pl.when(now + 1 < chunks)
        def _():
            for copy in loads(now + 1):
                copy.start()

        @pl.when(now < chunks)
        def _():
            produce(now)

        for stage in range(1, 9):
            lag = LAGS[stage]

            @pl.when(jnp.logical_and(now >= lag, now < chunks + lag))
            def _(stage=stage, lag=lag):
                take(stage, now - lag)

        for turn in range(5):

            @pl.when(now == 2 * turn + 4)
            def _(turn=turn):
                sums_exchange(turn).wait_recv()
                summed = sums_hold[turn] + sums_got[turn]
                if turn < 4:
                    sums_hold[turn + 1] = summed
                    sums_exchange(turn + 1).start()
                else:
                    sums_out[...] = summed

        @pl.when(now == chunks + 1)
        def _():
            for copy in back_copies():
                copy.start()

        return carry

    lax.fori_loop(0, chunks + LAGS[8], step, 0)

    def settle(chunk, carry):
        for stage in range(8):
            exchange(stage, chunk).wait_send()
        out_copy(chunk).wait()
        return carry

    lax.fori_loop(0, chunks, settle, 0)
    for turn in range(5):
        sums_exchange(turn).wait_send()
    for copy in own_copies():
        copy.wait()
    for copy in back_copies():
        copy.wait()


SETTLED = (2, 3, 4, 5, 6, 7, 8)
LAG = 2
DEPTH = 4
Y_FIRST = (1, 7)
Z_FIRST = (4, 10)


class Network:
    def __init__(self, owners, part, got, whole, merged, send_sem, recv_sem, out_sem):
        self.owners, self.part, self.got, self.whole = owners, part, got, whole
        self.merged, self.send_sem, self.recv_sem, self.out_sem = merged, send_sem, recv_sem, out_sem
        self.chunks, self.rows = whole.shape[0], whole.shape[1]
        self.ring = part.shape[0]
        win, var = lax.axis_index("win"), lax.axis_index("var")
        self.win, self.var = win, var
        self.core = half_of(var, 1)
        self.along = {
            "core": (self.core, (win, flip(var, 1))),
            "x": (half_of(var, 2), (win, flip(var, 2))),
            "y": (half_of(win, 1), (flip(win, 1), var)),
            "z": (half_of(win, 2), (flip(win, 2), var)),
            "w": (half_of(win, 4), (flip(win, 4), var)),
        }
        unit, at, self.places = self.rows // 8, 0, {}
        for stage, name in ((7, "y"), (6, "z"), (5, "w")):
            size = (1 << (stage - 5)) * unit
            at = pl.multiple_of(at + self.along[name][0] * size, size)
            self.places[stage] = (at, size)

    @staticmethod
    def way(chunk):
        place = chunk % 12

        def among(chosen):
            return sum(1 - ((place - one) * (place - one) + 143) // 144 for one in chosen)

        return among(Y_FIRST), among(Z_FIRST)

    def hop(self, stage, chunk):
        name = ("core", "x", "y", "z", "w", "w", "z", "y")[stage]
        if stage not in (1, 2, 3):
            return self.along[name]
        y_first, z_first = self.way(chunk)
        shares = {
            1: ((1 - y_first - z_first, "x"), (y_first, "y"), (z_first, "z")),
            2: ((1 - y_first - z_first, "y"), (y_first + z_first, "x")),
            3: ((1 - z_first, "z"), (z_first, "y")),
        }[stage]
        half, win, var = 0, 0, 0
        for share, name in shares:
            bit, (to_win, to_var) = self.along[name]
            half, win, var = half + share * bit, win + share * to_win, var + share * to_var
        return half, (win, var)

    def part_of(self, stage, half):
        size = self.got[stage].shape[1]
        return pl.ds(pl.multiple_of(half * size, 16), size)

    def exchange(self, stage, chunk):
        half, beyond = self.hop(stage, chunk)
        if stage == 0:
            source, target = self.part.at[chunk % self.ring, 1 - half], self.got[0].at[chunk]
        elif stage < 5:
            source, target = self.got[stage - 1].at[chunk, self.part_of(stage, 1 - half), :], self.got[stage].at[chunk]
        else:
            at, size = self.places[stage]
            source = target = self.whole.at[chunk, pl.ds(at, size), :]
        return pltpu.make_async_remote_copy(
            src_ref=source,
            dst_ref=target,
            send_sem=self.send_sem.at[stage, chunk],
            recv_sem=self.recv_sem.at[stage, chunk],
            device_id=beyond,
            device_id_type=MESH,
        )

    def out_copy(self, chunk):
        return pltpu.make_async_copy(self.whole.at[chunk], self.merged.at[chunk], self.out_sem.at[chunk])

    def emit(self, chunk, place, left, right):
        product = dot(left, right, 0, 0).astype(LOW)
        slot = chunk % self.ring

        @pl.when(chunk >= self.ring)
        def _():
            self.exchange(0, chunk - self.ring).wait_send()

        rows, quarter = self.rows, self.rows // 4
        y_first, z_first = self.way(place)
        for shard in range(self.owners):
            core, x = shard % 2, shard // 2
            for y in range(2):
                for z in range(2):
                    straight, over_y, over_z = 4 * x + 2 * y + z, 4 * y + 2 * x + z, 4 * z + 2 * x + y
                    at = straight + y_first * (over_y - straight) + z_first * (over_z - straight)
                    here = shard * rows + (2 * y + z) * quarter
                    self.part[slot, core, pl.ds(at * quarter, quarter), :] = product[here : here + quarter]
        self.exchange(0, chunk).start()

    def take(self, stage, chunk):
        def add(mine, target):
            return (mine.astype(F32) + target[chunk].astype(F32)).astype(LOW)

        self.exchange(stage - 1, chunk).wait_recv()
        if stage == 1:
            target = self.got[0]
            target[chunk] = add(self.part[chunk % self.ring, self.core], target)
        elif stage <= 4:
            half, _ = self.hop(stage - 1, chunk)
            target = self.got[stage - 1]
            target[chunk] = add(self.got[stage - 2][chunk, self.part_of(stage - 1, half), :], target)
        elif stage == 5:
            half, _ = self.hop(4, chunk)
            at, unit = self.places[5]
            self.whole[chunk, pl.ds(at, unit), :] = add(self.got[3][chunk, self.part_of(4, half), :], self.got[4])
        if stage == 1:

            @pl.when(chunk < DEPTH)
            def _():
                self.exchange(1, chunk).start()
        elif stage < 8:
            self.exchange(stage, chunk).start()
        else:
            self.out_copy(chunk).start()

    def pump(self, turn):
        for place, stage in enumerate(SETTLED):
            chunk = turn - LAG * place

            @pl.when(jnp.logical_and(chunk >= 0, chunk < self.chunks))
            def _(stage=stage, chunk=chunk):
                self.take(stage, chunk)

            if place == 0:

                @pl.when(turn + DEPTH < self.chunks)
                def _():
                    self.exchange(1, turn + DEPTH).start()

    def settle(self):
        def one(chunk, carry):
            for stage in range(1, 8):
                self.exchange(stage, chunk).wait_send()
            self.out_copy(chunk).wait()
            return carry

        lax.fori_loop(0, self.chunks, one, 0)
        for chunk in range(self.chunks - self.ring, self.chunks):
            self.exchange(0, chunk).wait_send()


def packed_kernel(
    owners, size,
    windows, row_index, inputs, cotangent, w_qkv, w_attn, w_in, w_out, bias_qv, out_bias, bias_in, gain, shift,
    merged, sums_out, layer_back, grad_back, meta,
    x_stage, x, most, most_got, wv_qkv, wv_attn, wv_in, wv_out, g_stage, g, spots, state, lefts, rights, qkv, slope,
    normal, inverse, top, mixed_grad, last_right, sums, part, got_core, got_one, got_two, got_three, got_four, whole,
    sums_hold, sums_got,
    weight_sem, send_sem, recv_sem, out_sem, sums_send, sums_recv, far_send, far_recv, own_sem, most_send, most_recv,
):
    each, length, width = x.shape
    wins, rows = cotangent.shape[0], cotangent.shape[1]
    layers = w_qkv.shape[0]
    hidden_width = w_in.shape[2]
    pieces = hidden_width // width
    strip = width // pieces
    pairs = width // 128
    got = (got_core, got_one, got_two, got_three, got_four)
    layer_out, grad_out = x, g
    net = Network(owners, part, got, whole, merged, send_sem, recv_sem, out_sem)
    win, var = net.win, net.var
    others = [flip(var, 1), flip(var, 2), flip(flip(var, 1), 2)]
    weights = ((w_qkv, wv_qkv), (w_attn, wv_attn), (w_in, wv_in), (w_out, wv_out))

    def fetch(layer, which):
        source, target = weights[which]
        return pltpu.make_async_copy(source.at[layer], target.at[layer], weight_sem.at[layer, which])

    for layer in range(layers):
        for which in range(4):
            fetch(layer, which).start()

    barrier = pltpu.get_barrier_semaphore()
    across = [(flip(win, bit), var) for bit in (1, 2, 4)]
    friends = [(win, other) for other in others] + across
    for friend in friends:
        pl.semaphore_signal(barrier, inc=1, device_id=friend, device_id_type=MESH)
    order = assign(windows, wins, owners)
    for place in range(wins):
        meta[place] = order[place]
        x_stage[place] = inputs[order[place]]
    meta[wins] = var
    pl.semaphore_wait(barrier, len(friends))
    mine = pl.ds(pl.multiple_of(var * rows, rows), rows)

    def remote(source, target, which, place, other):
        return pltpu.make_async_remote_copy(
            src_ref=source,
            dst_ref=target,
            send_sem=far_send.at[which, place],
            recv_sem=far_recv.at[which, place],
            device_id=(win, other),
            device_id_type=MESH,
        )

    def to_owners(stage, target, which):
        return [
            remote(stage.at[pl.ds(other * each, each)], target.at[:, mine, :], which, place, other)
            for place, other in enumerate(others)
        ] + [pltpu.make_async_copy(stage.at[pl.ds(var * each, each)], target.at[:, mine, :], own_sem.at[which])]

    def to_slots(source, target, which):
        home = target.at[pl.ds(var * each, each)]
        return [
            remote(source.at[:, pl.ds(pl.multiple_of(other * rows, rows), rows), :], home, which, place, other)
            for place, other in enumerate(others)
        ] + [pltpu.make_async_copy(source.at[:, mine, :], home, own_sem.at[which])]

    for copy in to_owners(x_stage, x, 3):
        copy.start()
    for place in range(wins):
        g_stage[place] = cotangent[order[place]]

    names, counts = [], []
    for place in range(each):
        name = order[place]
        for owner in range(1, owners):
            name = jnp.where(var == owner, order[owner * each + place], name)
        names.append(name)
        counts.append(windows[name])

    shares = counts[0] + counts[2] <= BLOCKS[0]
    starts = [jnp.int32(0), jnp.int32(BLOCKS[0]), jnp.where(shares, counts[0], BLOCKS[0] + counts[1])]
    for place in range(each):
        hits = marks(row_index, names[place], counts[place], length)
        along = lax.broadcasted_iota(jnp.int32, (length, size), 0) + starts[place]
        moved = jnp.where(lax.broadcasted_iota(jnp.int32, (length, size), 1) == along, 1.0, 0.0).astype(LOW)
        spots[place * length : (place + 1) * length] = dot(hits, moved, 1, 0).astype(LOW)

    row = lax.broadcasted_iota(jnp.int32, (size, 128), 0)
    lane = lax.broadcasted_iota(jnp.int32, (size, 128), 1)
    owner = jnp.full((size, 128), each, jnp.int32)
    for place in range(each):
        inside = jnp.logical_and(row >= starts[place], row < starts[place] + counts[place])
        owner = jnp.where(inside, place, owner)
    key_mark = jnp.where(lane == owner, 1.0, 0.0).astype(LOW)
    query_mark = jnp.where(lane == owner, jnp.where(lane < each, 0.0, -1e30), -1e30).astype(LOW)
    lane_low, lane_high = lane_masks(128)

    largest = jnp.int32(0)
    for owner in range(owners):
        held = [windows[order[owner * each + place]] for place in range(each)]
        second = jnp.where(held[0] + held[2] <= BLOCKS[0], held[1], held[1] + held[2])
        largest = jnp.maximum(largest, second)
    most[0] = jnp.full(most.shape[1:], largest, jnp.int32)
    for turn, friend in enumerate(across):
        copy = pltpu.make_async_remote_copy(
            src_ref=most.at[turn],
            dst_ref=most_got.at[turn],
            send_sem=most_send.at[turn],
            recv_sem=most_recv.at[turn],
            device_id=friend,
            device_id_type=MESH,
        )
        copy.start()
        copy.wait()
        most[turn + 1] = jnp.maximum(most[turn], most_got[turn])
    meta[wins + 1] = jnp.max(most[len(across)])
    for copy in to_owners(x_stage, x, 3):
        copy.wait()
    for copy in to_owners(g_stage, g, 0):
        copy.start()
    state[...] = dot(spots[...], x[...].reshape(each * length, width), 0, 0)
    fetch(0, 0).wait()

    spans = []
    for block in BLOCKS:
        first = spans[-1].stop if spans else 0
        spans.append(slice(first, first + block))

    def masked_scores(layer, at, span):
        query = two_heads(qkv[layer, span, pl.ds(at, 128)], lane_low, lane_high)
        key = qkv[layer, span, pl.ds(at + width, 128)]
        value = qkv[layer, span, pl.ds(at + 2 * width, 128)]
        allowed = jnp.concatenate([query_mark[span], query_mark[span]], axis=0)
        scores = dot(
            jnp.concatenate([key, key_mark[span]], axis=1), jnp.concatenate([query, allowed], axis=1), 1, 1
        )
        return query, key, value, scores

    def forward_layer(layer, carry):
        @pl.when(layer > 0)
        def _():
            fetch(layer, 0).wait()

        tokens = state[...].astype(LOW)
        lefts[layer, 0] = tokens
        for which in range(3):
            columns = slice(which * width, (which + 1) * width)
            joint = dot(tokens, wv_qkv[layer, :, columns], 1, 0)
            if which == 0:
                joint = (joint + bias_qv[pl.ds(layer, 1), :width]).astype(LOW) * LOW(0.125)
            elif which == 2:
                joint = (joint + bias_qv[pl.ds(layer, 1), width:]).astype(LOW)
            else:
                joint = joint.astype(LOW)
            qkv[layer, :, columns] = joint
        for pair, span in [(pair, span) for pair in range(pairs) for span in spans]:
            at = pair * 128
            _, _, value, scores = masked_scores(layer, at, span)
            peak = jnp.max(scores, axis=0, keepdims=True)
            expo = jnp.exp(scores - peak)
            total = jnp.sum(expo, axis=0, keepdims=True)
            probs = (expo * (1.0 / total)).astype(LOW)
            lefts[layer, 1, span, pl.ds(at, 128)] = join_heads(dot(probs, value, 0, 0)).astype(LOW)
            top[layer, pair, :, 2 * span.start : 2 * span.stop] = peak + jnp.log(total)
        for which in range(1, 4):
            fetch(layer, which).wait()
        first = dot(lefts[layer, 1], wv_attn[layer], 1, 0) + out_bias[layer, 0:1, :]
        one, inverse_one = normalize(state[...] + first)
        normal[layer, 0] = one.astype(LOW)
        after = one * gain[layer, 0:1, :] + shift[layer, 0:1, :]
        after_low = after.astype(LOW)
        lefts[layer, 2] = after_low
        second = jnp.zeros((size, width), F32)
        for piece in range(pieces):
            columns = slice(piece * width, (piece + 1) * width)
            hidden = dot(after_low, wv_in[layer, :, columns], 1, 0) + bias_in[pl.ds(layer, 1), columns]
            squared = hidden * hidden
            bend = jnp.tanh(hidden * (SMOOTH + SMOOTH * CUBIC * squared))
            half = 0.5 + 0.5 * bend
            active = (hidden * half).astype(LOW)
            rise = half + (hidden * half) * (1.0 - bend) * (SMOOTH + SMOOTH * 3.0 * CUBIC * squared)
            slope[layer, :, columns] = rise.astype(LOW)
            for sub in range(pieces):
                lefts[layer, 3 + sub, :, piece * strip : (piece + 1) * strip] = active[
                    :, sub * strip : (sub + 1) * strip
                ]
            second = second + dot(active, wv_out[layer, columns, :], 1, 0)
        two, inverse_two = normalize(after + second + out_bias[layer, 1:2, :])
        normal[layer, 1] = two.astype(LOW)
        state[...] = two * gain[layer, 1:2, :] + shift[layer, 1:2, :]
        lanes = lax.broadcasted_iota(jnp.int32, (size, 128), 1)
        inverse[layer] = jnp.where(lanes < 64, inverse_one, inverse_two)
        return carry

    lax.fori_loop(0, layers, forward_layer, 0)
    layer_out[...] = dot(spots[...], state[...].astype(LOW), 1, 0).astype(LOW).reshape(layer_out.shape)
    for copy in to_owners(g_stage, g, 0):
        copy.wait()
    state[...] = dot(spots[...], g[...].reshape(each * length, width), 0, 0)
    sums[...] = jnp.zeros_like(sums)

    def add_rows(layer, place, values):
        sums[layer, place : place + 1, :] += jnp.sum(values, axis=0, keepdims=True)

    per_layer = net.chunks // layers

    def backward_layer(step, carry):
        layer = layers - 1 - step
        first = step * per_layer
        turn = step * 7

        def emit(place, left, right):
            net.emit(first + place, place, left, right)

        def take(place):
            net.take(1, first + place)

        grad = state[...]
        two = normal[layer, 1].astype(F32)
        back = normalize_back(grad, gain[layer, 1:2, :], two, inverse[layer, :, 64:65])
        back_low = back.astype(LOW)
        last_right[...] = back_low

        def outer(piece, carry):
            emit(piece, lefts[layer, 3 + piece], last_right[...])

            @pl.when(piece > 0)
            def _():
                take(piece - 1)

            return carry

        lax.fori_loop(0, pieces, outer, 0, unroll=4)
        add_rows(layer, 9, grad * two)
        add_rows(layer, 11, grad)
        add_rows(layer, 3, back_low.astype(F32))
        state[...] = back

        def inner(piece, carry):
            columns = pl.ds(pl.multiple_of(piece * width, width), width)
            active = dot(last_right[...], wv_out[layer, columns, :], 1, 1)
            hidden = (active * slope[layer, :, columns].astype(F32)).astype(LOW)
            sums[layer, pl.ds(4 + piece, 1), :] = jnp.sum(hidden.astype(F32), axis=0, keepdims=True)
            rights[0] = hidden
            emit(pieces + piece, lefts[layer, 2], rights[0])
            state[...] += dot(rights[0], wv_in[layer, :, columns], 1, 1)
            take(pieces + piece - 1)

            @pl.when(piece > 0)
            def _():
                net.pump(turn + piece - 1)

            return carry

        lax.fori_loop(0, pieces, inner, 0)
        back = state[...]
        one = normal[layer, 0].astype(F32)
        add_rows(layer, 8, back * one)
        add_rows(layer, 10, back)
        back = normalize_back(back, gain[layer, 0:1, :], one, inverse[layer, :, 0:1])
        back_low = back.astype(LOW)
        emit(8, lefts[layer, 1], back_low)
        take(7)
        add_rows(layer, 2, back_low.astype(F32))
        mixed_grad[...] = dot(back_low, wv_attn[layer], 1, 1).astype(LOW)
        state[...] = back
        net.pump(turn + 3)
        for pair, span in [(pair, span) for pair in range(pairs) for span in spans]:
            at = pair * 128
            query, key, value, scores = masked_scores(layer, at, span)
            grads = two_heads(mixed_grad[span, pl.ds(at, 128)], lane_low, lane_high)
            probs = jnp.exp(scores - top[layer, pair, :, 2 * span.start : 2 * span.stop])
            d_probs = dot(value, grads, 1, 1)
            centre = jnp.sum(probs * d_probs, axis=0, keepdims=True)
            d_scores = (probs * (d_probs - centre)).astype(LOW)
            d_query = join_heads(dot(d_scores, key, 0, 0)) * 0.125
            rights[0, span, pl.ds(at, 128)] = d_query.astype(LOW)
            rights[1, span, pl.ds(at, 128)] = dot(d_scores, query, 1, 0).astype(LOW)
            rights[2, span, pl.ds(at, 128)] = dot(probs.astype(LOW), grads, 1, 0).astype(LOW)
        take(8)
        net.pump(turn + 4)

        def last(which, carry):
            emit(9 + which, lefts[layer, 0], rights[which])

            @pl.when(which > 0)
            def _():
                take(8 + which)

            return carry

        lax.fori_loop(0, 3, last, 0, unroll=3)
        net.pump(turn + 5)
        grad = state[...]
        for which in range(3):
            piece = rights[which]
            grad = grad + dot(piece, wv_qkv[layer, :, which * width : (which + 1) * width], 1, 1)
            if which != 1:
                add_rows(layer, which // 2, piece.astype(F32))
        state[...] = grad
        take(11)
        net.pump(turn + 6)
        return carry

    lax.fori_loop(0, layers, backward_layer, 0)
    first_turn = 7 * layers
    grad_out[...] = dot(spots[...], state[...].astype(LOW), 1, 0).astype(LOW).reshape(grad_out.shape)

    route = [partner(axis, bit) for axis, bit in ROUTE]

    def sums_exchange(step):
        return pltpu.make_async_remote_copy(
            src_ref=sums_hold.at[step],
            dst_ref=sums_got.at[step],
            send_sem=sums_send.at[step],
            recv_sem=sums_recv.at[step],
            device_id=route[step],
            device_id_type=MESH,
        )

    sums_hold[0] = sums[...]
    sums_exchange(0).start()

    def step(now, carry):
        net.pump(now)

        @pl.when(now == net.chunks - 1)
        def _():
            for copy in to_slots(grad_out, grad_back, 2) + to_slots(layer_out, layer_back, 1):
                copy.start()

        for place in range(5):

            @pl.when(now == first_turn + 1 + 2 * place)
            def _(place=place):
                sums_exchange(place).wait_recv()
                summed = sums_hold[place] + sums_got[place]
                if place < 4:
                    sums_hold[place + 1] = summed
                    sums_exchange(place + 1).start()
                else:
                    sums_out[...] = summed

        return carry

    lax.fori_loop(first_turn, net.chunks + LAG * (len(SETTLED) - 1), step, 0)
    net.settle()
    for place in range(5):
        sums_exchange(place).wait_send()
    for copy in to_slots(layer_out, layer_back, 1) + to_slots(grad_out, grad_back, 2):
        copy.wait()


def finish_kernel(
    at_var, meta, sums, merged, layer_back, grad_back,
    layer_out, grad_inputs, qkv, attn, in_, out, bias_qv, out_bias, bias_in, gain, shift,
    chunks, layer_in, grad_in, grad_wide, qkv_wide, attn_wide, in_wide, out_wide, in_sem, out_sem,
):
    wins, rows = layer_back.shape[0], layer_back.shape[1]
    layers, width = qkv.shape[0], merged.shape[2]
    part_rows = merged.shape[1]
    per_layer = merged.shape[0] // layers
    loads = [
        pltpu.make_async_copy(grad_back, grad_in, in_sem.at[0]),
        pltpu.make_async_copy(layer_back, layer_in, in_sem.at[1]),
    ] + [
        pltpu.make_async_copy(
            merged.at[pl.ds(half * per_layer, per_layer)], chunks.at[pl.ds(half * per_layer, per_layer)], in_sem.at[2 + half]
        )
        for half in range(layers)
    ]
    for load in loads:
        load.start()

    def home(place):
        window = meta[place]
        return (
            pltpu.make_async_copy(grad_wide.at[place], grad_inputs.at[window], out_sem.at[0, place]),
            pltpu.make_async_copy(layer_in.at[place], layer_out.at[window], out_sem.at[1, place]),
        )

    def outs(layer):
        return [
            pltpu.make_async_copy(source.at[layer], target.at[layer], out_sem.at[2 + layer, which])
            for which, (source, target) in enumerate(
                ((qkv_wide, qkv), (attn_wide, attn), (in_wide, in_), (out_wide, out))
            )
        ]

    loads[0].wait()
    loads[1].wait()

    def send(place, carry):
        grad_wide[place] = grad_in[place].astype(F32)
        for copy in home(place):
            copy.start()
        return carry

    lax.fori_loop(0, wins, send, 0)
    for half in range(layers):
        loads[2 + half].wait()
        layer, base = layers - 1 - half, half * per_layer

        def widen(block, carry, layer=layer, base=base):
            at = pl.multiple_of(block * 32, 32)
            here = pl.ds(at, 32)
            for which in range(4):
                columns = slice(which * width, (which + 1) * width)
                there = pl.ds(pl.multiple_of(at + which * part_rows, 32), 32)
                out_wide[layer, there, :] = chunks[base + which, here, :].astype(F32)
                in_wide[layer, here, columns] = chunks[base + 4 + which, here, :].astype(F32)
                if which < 3:
                    qkv_wide[layer, here, columns] = chunks[base + 9 + which, here, :].astype(F32)
            attn_wide[layer, here, :] = chunks[base + 8, here, :].astype(F32)
            return carry

        lax.fori_loop(0, part_rows // 32, widen, 0)
        for copy in outs(layer):
            copy.start()

    var = meta[at_var]
    narrow = out_bias.shape[2]
    at = pl.multiple_of(var * narrow, narrow)
    wide = bias_qv.shape[1]
    for layer in range(layers):
        half = width // wide
        bias_qv[layer : layer + 1, :] = sums[
            layer, pl.ds(var // half, 1), pl.ds(pl.multiple_of(lax.rem(var, half) * wide, wide), wide)
        ]
        bias_in[layer : layer + 1, :] = sums[layer, pl.ds(4 + var, 1), :]
        out_bias[layer] = sums[layer, 2:4, pl.ds(at, narrow)]
        gain[layer] = sums[layer, 8:10, pl.ds(at, narrow)]
        shift[layer] = sums[layer, 10:12, pl.ds(at, narrow)]

    def settle(place, carry):
        for copy in home(place):
            copy.wait()
        return carry

    lax.fori_loop(0, wins, settle, 0)
    for layer in range(layers):
        for copy in outs(layer):
            copy.wait()


def gather_kernel(owners, meta, x, x_out, x_stage, x_send, x_recv, own_sem):
    wins, rows = x.shape[0], x.shape[1]
    each = wins // owners
    me, win = lax.axis_index("var"), lax.axis_index("win")
    others = [(win, flip(me, 1)), (win, flip(me, 2)), (win, flip(flip(me, 1), 2))]
    for place in range(wins):
        x_stage[place] = x[meta[place]]
    greet(others)
    own = pl.ds(pl.multiple_of(me * rows, rows), rows)
    copies = [pltpu.make_async_copy(x_stage.at[pl.ds(me * each, each)], x_out.at[:, own, :], own_sem)]
    for place, other in enumerate(others):
        copies.append(
            pltpu.make_async_remote_copy(
                src_ref=x_stage.at[pl.ds(other[1] * each, each)],
                dst_ref=x_out.at[:, own, :],
                send_sem=x_send.at[place],
                recv_sem=x_recv.at[place],
                device_id=other,
                device_id_type=MESH,
            )
        )
    for copy in copies:
        copy.start()
    for copy in copies:
        copy.wait()


def in_vmem(count):
    return [pl.BlockSpec(memory_space=pltpu.VMEM)] * count


def anywhere(count):
    return [pl.BlockSpec(memory_space=pl.ANY)] * count


def in_smem():
    return [pl.BlockSpec(memory_space=pltpu.SMEM)]


def shaped(shape, kind=LOW):
    return jax.ShapeDtypeStruct(shape, kind)


def whole_windows(
    inputs, counts, row_index, w_qkv, bias_qv, w_attn_out, out_bias, w_in, bias_in, w_ffn_out,
    norm_gain, norm_bias, cotangent,
):
    wins, rows, width = inputs.shape
    owners, groups = lax.axis_size("var"), lax.axis_size("win")
    each, length = wins // owners, rows * owners
    packed = each * length
    layers, hidden_width = w_in.shape[0], w_in.shape[2]
    dma = pltpu.SemaphoreType.DMA

    def params(**more):
        return pltpu.CompilerParams(vmem_limit_bytes=VMEM_BYTES, **more)

    weights = (w_qkv, w_attn_out, w_in, w_ffn_out)
    weight_space = [pltpu.VMEM(weight.shape, LOW) for weight in weights]
    narrow = width // owners
    chunks = layers * 12
    part_rows = width // owners
    half, quarter, eighth = part_rows // 2, part_rows // 4, part_rows // 8
    sums_shape = (layers, 16, width)

    def space(*shape):
        return pltpu.VMEM((chunks,) + shape + (width,), LOW)

    def finish(at_var, meta, merged, sums, layer_back, grad_back):
        rows_shape = (wins, rows, width)
        large = [
            shaped((layers, narrow, 3 * width), F32),
            shaped((layers, narrow, width), F32),
            shaped((layers, narrow, hidden_width), F32),
            shaped((layers, hidden_width // owners, width), F32),
        ]
        layer_out, grad_inputs, *rest = pl.pallas_call(
            functools.partial(finish_kernel, at_var),
            name="finish",
            out_shape=[shaped(rows_shape), shaped(rows_shape, F32)]
            + large
            + [
                shaped((layers, 2 * narrow), F32),
                shaped((layers, 2, narrow), F32),
                shaped((layers, hidden_width // owners), F32),
                shaped((layers, 2, narrow), F32),
                shaped((layers, 2, narrow), F32),
            ],
            in_specs=in_smem() + in_vmem(1) + anywhere(3),
            out_specs=anywhere(6) + in_vmem(5),
            scratch_shapes=[pltpu.VMEM(merged.shape, LOW)]
            + [pltpu.VMEM(rows_shape, LOW)] * 2
            + [pltpu.VMEM(rows_shape, F32)]
            + [pltpu.VMEM(entry.shape, F32) for entry in large]
            + [dma((2 + layers,)), dma((2 + layers, wins))],
            compiler_params=params(),
        )(meta, sums, merged, layer_back, grad_back)
        qkv, attn, in_, out, qv, biases, hidden, gain, shift = rest
        return layer_out, grad_inputs, qkv, qv, attn, biases, in_, hidden, out, gain, shift

    def packed_way():
        size = PACKED
        return pl.pallas_call(
            functools.partial(packed_kernel, owners, size),
            name="packed",
            out_shape=[
                shaped((chunks, part_rows, width)),
                shaped(sums_shape, F32),
                shaped((wins, rows, width)),
                shaped((wins, rows, width)),
                shaped((wins + 2,), jnp.int32),
            ],
            in_specs=in_smem() + in_vmem(3) + anywhere(4) + in_vmem(5),
            out_specs=anywhere(1) + in_vmem(1) + anywhere(2) + in_smem(),
            scratch_shapes=[
                pltpu.VMEM((wins, rows, width), LOW),
                pltpu.VMEM((each, length, width), LOW),
                pltpu.VMEM((4, 8, 128), jnp.int32),
                pltpu.VMEM((3, 8, 128), jnp.int32),
            ]
            + weight_space
            + [
                pltpu.VMEM((wins, rows, width), LOW),
                pltpu.VMEM((each, length, width), LOW),
                pltpu.VMEM((each * length, size), LOW),
                pltpu.VMEM((size, width), F32),
                pltpu.VMEM((layers, 7, size, width), LOW),
                pltpu.VMEM((3, size, width), LOW),
                pltpu.VMEM((layers, size, 3 * width), LOW),
                pltpu.VMEM((layers, size, hidden_width), LOW),
                pltpu.VMEM((layers, 2, size, width), LOW),
                pltpu.VMEM((layers, size, 128), F32),
                pltpu.VMEM((layers, width // 128, 1, 2 * size), F32),
                pltpu.VMEM((size, width), LOW),
                pltpu.VMEM((size, width), LOW),
                pltpu.VMEM(sums_shape, F32),
                pltpu.VMEM((4, 2, 2 * part_rows, width), LOW),
                space(2 * part_rows),
                space(part_rows),
                space(half),
                space(quarter),
                space(eighth),
                space(part_rows),
            ]
            + [pltpu.VMEM((5,) + sums_shape, F32)] * 2
            + [dma((layers, 4)), dma((8, chunks)), dma((8, chunks)), dma((chunks,))]
            + [dma((5,))] * 2
            + [dma((4, owners - 1))] * 2
            + [dma((4,))]
            + [dma((3,))] * 2,
            compiler_params=params(collective_id=2, has_side_effects=True),
        )(
            counts, row_index, inputs, cotangent, *weights, bias_qv, out_bias, bias_in, norm_gain, norm_bias
        )

    def ragged_way():
        x, meta = pl.pallas_call(
            functools.partial(spread_kernel, owners),
            name="spread",
            out_shape=[shaped((each, length, width)), shaped((wins + 2 * each + 2,), jnp.int32)],
            in_specs=in_smem() + in_vmem(1),
            out_specs=anywhere(1) + in_smem(),
            scratch_shapes=[
                pltpu.VMEM((wins, rows, width), LOW),
            ]
            + [dma((owners - 1,))] * 2
            + [dma],
            compiler_params=params(collective_id=0, has_side_effects=True),
        )(counts, inputs)
        g = pl.pallas_call(
            functools.partial(gather_kernel, owners),
            name="gather",
            out_shape=shaped((each, length, width)),
            in_specs=in_smem() + in_vmem(1),
            out_specs=pl.BlockSpec(memory_space=pl.ANY),
            scratch_shapes=[pltpu.VMEM((wins, rows, width), LOW)] + [dma((owners - 1,))] * 2 + [dma],
            compiler_params=params(collective_id=3, has_side_effects=True),
        )(meta, cotangent)
        kept = [
            shaped((layers, packed, 3 * width)),
            shaped((layers, packed, hidden_width)),
            shaped((layers, 2, packed, width), F32),
            shaped((layers, packed, 128), F32),
            shaped((layers, packed, width), F32),
        ]
        kept_space = [pltpu.VMEM(entry.shape, entry.dtype) for entry in kept]
        lefts_shape = shaped((layers, 7, packed, width))
        lefts, *stash, layer_rows = pl.pallas_call(
            forward_kernel,
            name="forward",
            out_shape=[lefts_shape] + kept + [shaped((each, length, width))],
            in_specs=in_smem() + in_vmem(2) + anywhere(4) + in_vmem(5),
            out_specs=anywhere(6) + in_vmem(1),
            scratch_shapes=weight_space
            + [pltpu.VMEM(lefts_shape.shape, LOW)]
            + kept_space
            + [pltpu.VMEM((packed, width), F32), dma((layers, 4)), dma((layers, 6, 6))],
            compiler_params=params(),
        )(meta, row_index, x, *weights, bias_qv, out_bias, bias_in, norm_gain, norm_bias)

        rights_shape = shaped((layers, 9, packed, width))
        rights, grad_rows, sums = pl.pallas_call(
            backward_kernel,
            name="backward",
            out_shape=[rights_shape, shaped((each, length, width)), shaped((layers, 16, width), F32)],
            in_specs=in_smem() + in_vmem(2) + anywhere(4) + in_vmem(1) + anywhere(5),
            out_specs=anywhere(1) + in_vmem(2),
            scratch_shapes=weight_space
            + [pltpu.VMEM(rights_shape.shape, LOW)]
            + kept_space
            + [
                pltpu.VMEM((packed, width), F32),
                pltpu.VMEM((packed, width), LOW),
                dma((layers, 4)),
                dma((layers, 5, 6)),
                dma((layers, 6)),
            ],
            compiler_params=params(),
        )(meta, row_index, g, *weights, norm_gain, *stash)

        merged, sums, layer_back, grad_back = pl.pallas_call(
            functools.partial(merge_kernel, owners),
            name="merge",
            out_shape=[
                shaped((chunks, part_rows, width)),
                shaped(sums.shape, F32),
                shaped((wins, rows, width)),
                shaped((wins, rows, width)),
            ],
            in_specs=in_smem() + anywhere(2) + in_vmem(3),
            out_specs=anywhere(1) + in_vmem(1) + anywhere(2),
            scratch_shapes=[pltpu.VMEM((2, packed, width), LOW)] * 2
            + [
                space(2, 2, part_rows),
                space(2, part_rows),
                space(2, part_rows),
                space(part_rows),
                space(2, half),
                space(half),
                space(2, quarter),
                space(quarter),
                space(2, eighth),
                space(eighth),
                space(part_rows),
            ]
            + [pltpu.VMEM((5,) + sums.shape, F32)] * 2
            + [dma((2, 2)), dma((8, chunks)), dma((8, chunks)), dma((chunks,))]
            + [dma((5,))] * 2
            + [dma((2, owners - 1))] * 2
            + [dma((2,))],
            compiler_params=params(collective_id=1, has_side_effects=True),
        )(meta, lefts, rights, sums, layer_rows, grad_rows)
        return finish(wins + 2 * each, meta, merged, sums, layer_back, grad_back)

    *sums_up, order = packed_way()
    return lax.cond(order[wins + 1] <= BLOCKS[1], lambda: finish(wins, order, *sums_up), ragged_way)


def choose(*arrays):
    wins, rows, width = arrays[0].shape
    owners, groups = lax.axis_size("var"), lax.axis_size("win")
    fits = owners == 4 and groups == 8 and wins % owners == 0 and rows % 16 == 0
    fits = fits and (wins // owners, rows * owners, width, arrays[7].shape[2]) == (3, 256, 512, 2048)
    return whole_windows(*arrays) if fits else per_device(*arrays)


def solution(mesh):
    return jax.shard_map(
        choose,
        mesh=mesh,
        in_specs=(
            P("win", "var", None),
            P("win"),
            P("win", None),
            P(),
            P(),
            P(),
            P(),
            P(),
            P(),
            P(),
            P(),
            P(),
            P("win", "var", None),
        ),
        out_specs=(
            P("win", "var", None),
            P("win", "var", None),
            P(None, "var", None),
            P(None, "var"),
            P(None, "var", None),
            P(None, None, "var"),
            P(None, "var", None),
            P(None, "var"),
            P(None, "var", None),
            P(None, None, "var"),
            P(None, None, "var"),
        ),
        check_vma=False,
    )
```

```python
import functools

import jax
import jax.numpy as jnp
from jax import lax
from jax.experimental import pallas as pl
from jax.experimental.pallas import tpu as pltpu
from jax.sharding import PartitionSpec as P

HEADS = 8
LAYERS = 2


EPS = 1e-05
LOW = jnp.bfloat16
F32 = jnp.float32
MESH = pl.DeviceIdType.MESH
VMEM_BYTES = 60 << 20
BLOCKS = (256, 224)
PACKED = sum(BLOCKS)
SMOOTH = 0.7978845608028654
CUBIC = 0.044715


def layer_norm(values, gain, shift):
    centre = values - jnp.mean(values, axis=-1, keepdims=True)
    spread = jnp.mean(centre * centre, axis=-1, keepdims=True)
    return centre * lax.rsqrt(spread + EPS) * gain + shift


def smooth(values):
    return jax.nn.gelu(values, approximate=True)


def scores_of(query_heads, key_heads, key_valid, scale):
    raw = (
        jnp.einsum("wqhd,wkhd->whqk", query_heads, key_heads, preferred_element_type=jnp.float32)
        * scale
    )
    return jnp.where(key_valid[:, None, None, :], raw, -1e30)


def per_device(
    inputs,
    counts,
    row_index,
    w_qkv,
    bias_qv,
    w_attn_out,
    out_bias,
    w_in,
    bias_in,
    w_ffn_out,
    norm_gain,
    norm_bias,
    cotangent,
):
    wins, rows, width = inputs.shape
    cycle_size = lax.axis_size("var")
    length = rows * cycle_size
    first_row = lax.axis_index("var") * rows
    head_count = HEADS
    head_size = width // head_count
    scale = head_size ** (-0.5)
    flat = wins * rows
    slots = jnp.arange(length, dtype=jnp.int32)
    live = (slots[None, :] < counts[:, None]).astype(jnp.float32)
    window_ids = jnp.arange(wins, dtype=jnp.int32)[:, None]
    valid = jnp.zeros((wins, length), jnp.float32).at[window_ids, row_index].add(live)
    key_valid = valid > 0.5
    own_valid = lax.dynamic_slice_in_dim(valid, first_row, rows, 1).reshape(flat, 1)
    state = inputs.astype(jnp.float32).reshape(flat, width)
    kept = []
    for which_layer in range(LAYERS):
        x_low = state.astype(jnp.bfloat16)
        joint = jnp.dot(x_low, w_qkv[which_layer], preferred_element_type=jnp.float32)
        query = (joint[:, :width] + bias_qv[which_layer, :width]).astype(jnp.bfloat16)
        keys_low = joint[:, width : 2 * width].astype(jnp.bfloat16)
        values_low = (joint[:, 2 * width :] + bias_qv[which_layer, width:]).astype(jnp.bfloat16)
        pair = jnp.concatenate([keys_low, values_low], axis=1).reshape(wins, rows, 2 * width)
        whole = lax.all_gather(pair, "var", axis=1, tiled=True)
        query_heads = query.reshape(wins, rows, head_count, head_size)
        key_heads = whole[:, :, :width].reshape(wins, length, head_count, head_size)
        value_heads = whole[:, :, width:].reshape(wins, length, head_count, head_size)
        scores = scores_of(query_heads, key_heads, key_valid, scale)
        peak = jnp.max(scores, axis=-1, keepdims=True)
        expo = jnp.exp(scores - peak)
        total = jnp.sum(expo, axis=-1, keepdims=True)
        probs = expo / total
        top = peak + jnp.log(total)
        mixed = (
            jnp.einsum(
                "whqk,wkhd->wqhd",
                probs.astype(jnp.bfloat16),
                value_heads,
                preferred_element_type=jnp.float32,
            )
            .reshape(flat, width)
            .astype(jnp.bfloat16)
        )
        attn = (
            jnp.dot(mixed, w_attn_out[which_layer], preferred_element_type=jnp.float32)
            + out_bias[which_layer, 0]
        )
        normed, norm_one = jax.vjp(
            layer_norm, state + attn, norm_gain[which_layer, 0], norm_bias[which_layer, 0]
        )
        normed_low = normed.astype(jnp.bfloat16)
        hidden = (
            jnp.dot(normed_low, w_in[which_layer], preferred_element_type=jnp.float32)
            + bias_in[which_layer]
        )
        active, gelu_back = jax.vjp(smooth, hidden)
        active_low = active.astype(jnp.bfloat16)
        ffn = (
            jnp.dot(active_low, w_ffn_out[which_layer], preferred_element_type=jnp.float32)
            + out_bias[which_layer, 1]
        )
        state, norm_two = jax.vjp(
            layer_norm, normed + ffn, norm_gain[which_layer, 1], norm_bias[which_layer, 1]
        )
        stored = whole
        kept.append(
            (
                x_low,
                query_heads,
                stored,
                top,
                mixed,
                norm_one,
                normed_low,
                gelu_back,
                active_low,
                norm_two,
            )
        )
    layer_out = (state * own_valid).astype(jnp.bfloat16).reshape(wins, rows, width)
    grad = cotangent.astype(jnp.float32).reshape(flat, width) * own_valid
    collected = []
    for which_layer in reversed(range(LAYERS)):
        (
            x_low,
            query_heads,
            stored,
            top,
            mixed,
            norm_one,
            normed_low,
            gelu_back,
            active_low,
            norm_two,
        ) = kept[which_layer]
        dz_two, gain_two, shift_two = norm_two(grad)
        d_ffn = dz_two.astype(jnp.bfloat16)
        g_ffn_out = jnp.einsum("rf,rd->fd", active_low, d_ffn, preferred_element_type=jnp.float32)
        bias_two = jnp.sum(d_ffn.astype(jnp.float32), axis=0)
        d_active = jnp.einsum(
            "rd,fd->rf", d_ffn, w_ffn_out[which_layer], preferred_element_type=jnp.float32
        )
        (d_hidden,) = gelu_back(d_active)
        d_hidden = d_hidden.astype(jnp.bfloat16)
        g_in = jnp.einsum("rd,rf->df", normed_low, d_hidden, preferred_element_type=jnp.float32)
        g_bias_in = jnp.sum(d_hidden.astype(jnp.float32), axis=0)
        d_normed = dz_two + jnp.einsum(
            "rf,df->rd", d_hidden, w_in[which_layer], preferred_element_type=jnp.float32
        )
        dz_one, gain_one, shift_one = norm_one(d_normed)
        d_attn = dz_one.astype(jnp.bfloat16)
        g_attn_out = jnp.einsum("re,rd->ed", mixed, d_attn, preferred_element_type=jnp.float32)
        bias_one = jnp.sum(d_attn.astype(jnp.float32), axis=0)
        d_mixed = jnp.einsum(
            "rd,ed->re", d_attn, w_attn_out[which_layer], preferred_element_type=jnp.float32
        ).astype(jnp.bfloat16)
        whole = stored
        key_heads = whole[:, :, :width].reshape(wins, length, head_count, head_size)
        value_heads = whole[:, :, width:].reshape(wins, length, head_count, head_size)
        scores = scores_of(query_heads, key_heads, key_valid, scale)
        probs = jnp.exp(scores - top)
        grad_heads = d_mixed.reshape(wins, rows, head_count, head_size)
        d_probs = jnp.einsum(
            "wqhd,wkhd->whqk", grad_heads, value_heads, preferred_element_type=jnp.float32
        )
        centre = jnp.sum(probs * d_probs, axis=-1, keepdims=True)
        d_scores = (probs * (d_probs - centre)).astype(jnp.bfloat16)
        probs_low = probs.astype(jnp.bfloat16)
        d_query = (
            jnp.einsum("whqk,wkhd->wqhd", d_scores, key_heads, preferred_element_type=jnp.float32)
            * scale
        )
        d_query = d_query.reshape(flat, width).astype(jnp.bfloat16)
        span_rows = lax.axis_size("var") * rows
        d_key = (
            jnp.einsum("whqk,wqhd->kwhd", d_scores, query_heads, preferred_element_type=jnp.float32)
            * scale
        )
        d_value = jnp.einsum(
            "whqk,wqhd->kwhd", probs_low, grad_heads, preferred_element_type=jnp.float32
        )
        key_grads = lax.psum_scatter(
            jnp.concatenate(
                [d_key.reshape(span_rows, wins, width), d_value.reshape(span_rows, wins, width)],
                axis=2,
            ).astype(jnp.bfloat16),
            "var",
            scatter_dimension=0,
            tiled=True,
        ).astype(jnp.float32)
        key_grads = (
            jnp.transpose(key_grads, (1, 0, 2)).reshape(flat, 2 * width).astype(jnp.bfloat16)
        )
        d_joint = jnp.concatenate([d_query, key_grads], axis=1)
        g_qkv = jnp.einsum("rd,re->de", x_low, d_joint, preferred_element_type=jnp.float32)
        g_bias_qv = jnp.concatenate(
            [
                jnp.sum(d_query.astype(jnp.float32), axis=0),
                jnp.sum(key_grads[:, width:].astype(jnp.float32), axis=0),
            ]
        )
        grad = dz_one + jnp.einsum(
            "re,de->rd", d_joint, w_qkv[which_layer], preferred_element_type=jnp.float32
        )
        g_out_bias = jnp.stack([bias_one, bias_two])
        g_gain = jnp.stack([gain_one, gain_two])
        g_shift = jnp.stack([shift_one, shift_two])
        terms = (
            g_qkv,
            g_bias_qv,
            g_attn_out,
            g_out_bias,
            g_in,
            g_bias_in,
            g_ffn_out,
            g_gain,
            g_shift,
        )
        collected.append(terms)
    collected = collected[::-1]
    stacked = tuple((jnp.stack([entry[position] for entry in collected]) for position in range(9)))
    shards = (
        lax.psum_scatter(
            stacked[0].astype(jnp.bfloat16), "var", scatter_dimension=1, tiled=True
        ).astype(jnp.float32),
        lax.psum_scatter(
            stacked[1].astype(jnp.bfloat16), "var", scatter_dimension=1, tiled=True
        ).astype(jnp.float32),
        lax.psum_scatter(
            stacked[2].astype(jnp.bfloat16), "var", scatter_dimension=1, tiled=True
        ).astype(jnp.float32),
        lax.psum_scatter(
            stacked[3].astype(jnp.bfloat16), "var", scatter_dimension=2, tiled=True
        ).astype(jnp.float32),
        lax.psum_scatter(
            stacked[4].astype(jnp.bfloat16), "var", scatter_dimension=1, tiled=True
        ).astype(jnp.float32),
        lax.psum_scatter(
            stacked[5].astype(jnp.bfloat16), "var", scatter_dimension=1, tiled=True
        ).astype(jnp.float32),
        lax.psum_scatter(
            stacked[6].astype(jnp.bfloat16), "var", scatter_dimension=1, tiled=True
        ).astype(jnp.float32),
        lax.psum_scatter(
            stacked[7].astype(jnp.bfloat16), "var", scatter_dimension=2, tiled=True
        ).astype(jnp.float32),
        lax.psum_scatter(
            stacked[8].astype(jnp.bfloat16), "var", scatter_dimension=2, tiled=True
        ).astype(jnp.float32),
    )
    stacked = (
        lax.psum(shards[0].astype(jnp.bfloat16), "win").astype(jnp.float32),
        lax.psum(shards[1].astype(jnp.bfloat16), "win").astype(jnp.float32),
        lax.psum(shards[2].astype(jnp.bfloat16), "win").astype(jnp.float32),
        lax.psum(shards[3].astype(jnp.bfloat16), "win").astype(jnp.float32),
        lax.psum(shards[4].astype(jnp.bfloat16), "win").astype(jnp.float32),
        lax.psum(shards[5].astype(jnp.bfloat16), "win").astype(jnp.float32),
        lax.psum(shards[6].astype(jnp.bfloat16), "win").astype(jnp.float32),
        lax.psum(shards[7].astype(jnp.bfloat16), "win").astype(jnp.float32),
        lax.psum(shards[8].astype(jnp.bfloat16), "win").astype(jnp.float32),
    )
    grad_inputs = grad.reshape(wins, rows, width)
    return (
        layer_out,
        grad_inputs,
        stacked[0],
        stacked[1],
        stacked[2],
        stacked[3],
        stacked[4],
        stacked[5],
        stacked[6],
        stacked[7],
        stacked[8],
    )


def dot(left, right, left_dim, right_dim):
    return lax.dot_general(
        left, right, (((left_dim,), (right_dim,)), ((), ())), preferred_element_type=F32
    )


def flip(index, bit):
    return index + bit - 2 * bit * lax.rem(index // bit, 2)


def half_of(index, bit):
    return lax.rem(index // bit, 2)


def partner(axis, bit):
    win, var = lax.axis_index("win"), lax.axis_index("var")
    if axis == "win":
        return (flip(win, bit), var)
    return (win, flip(var, bit))


def greet(partners):
    barrier = pltpu.get_barrier_semaphore()
    for other in partners:
        pl.semaphore_signal(barrier, inc=1, device_id=other, device_id_type=MESH)
    pl.semaphore_wait(barrier, len(partners))


def assign(counts, wins, owners):
    each = wins // owners
    keys = [counts[w] * wins + w for w in range(wins)]
    for stop in range(wins - 1, 0, -1):
        for low in range(stop):
            first, second = keys[low], keys[low + 1]
            keys[low], keys[low + 1] = jnp.maximum(first, second), jnp.minimum(first, second)
    names = [lax.rem(key, wins) for key in keys]
    order = []
    for owner in range(owners):
        order += [names[owner], names[2 * owners - 1 - owner], names[2 * owners + owner]]
    return order


def spread_kernel(
    owners, counts, x, x_out, meta, x_stage, x_send, x_recv, own_sem
):
    wins, rows = x.shape[0], x.shape[1]
    each = wins // owners
    me, win = lax.axis_index("var"), lax.axis_index("win")
    others = [flip(me, 1), flip(me, 2), flip(flip(me, 1), 2)]
    barrier = pltpu.get_barrier_semaphore()
    for other in others:
        pl.semaphore_signal(barrier, inc=1, device_id=(win, other), device_id_type=MESH)
    order = assign(counts, wins, owners)
    for place in range(wins):
        meta[place] = order[place]
        x_stage[place] = x[order[place]]
    pl.semaphore_wait(barrier, len(others))

    sent = []
    for place, other in enumerate(others):
        sent.append(
            pltpu.make_async_remote_copy(
                src_ref=x_stage.at[pl.ds(other * each, each)],
                dst_ref=x_out.at[:, pl.ds(pl.multiple_of(me * rows, rows), rows), :],
                send_sem=x_send.at[place],
                recv_sem=x_recv.at[place],
                device_id=(win, other),
                device_id_type=MESH,
            )
        )
    for copy in sent:
        copy.start()
    own = pl.ds(pl.multiple_of(me * rows, rows), rows)
    own_x = pltpu.make_async_copy(x_stage.at[pl.ds(me * each, each)], x_out.at[:, own, :], own_sem)
    own_x.start()
    padded = jnp.int32(0)
    for place in range(each):
        name = jnp.int32(0)
        for owner in range(owners):
            name = jnp.where(me == owner, order[owner * each + place], name)
        meta[wins + place] = name
        meta[wins + each + place] = counts[name]
        padded = padded + ((counts[name] + 15) // 16) * 16
    meta[wins + 2 * each] = me
    meta[wins + 2 * each + 1] = padded

    own_x.wait()
    for copy in sent:
        copy.wait()


class Plan:
    def __init__(self, meta, wins, each):
        self.names = [meta[wins + place] for place in range(each)]
        self.counts = [meta[wins + each + place] for place in range(each)]
        self.starts = []
        total = jnp.int32(0)
        for count in self.counts:
            self.starts.append(total)
            total = total + ((count + 15) // 16) * 16
        self.total = total
        self.blocks = (total + 127) // 128

    def each_block(self, body):
        def step(block, carry):
            body(128, block, pl.ds(pl.multiple_of(block * 128, 128), 128))
            return carry

        lax.fori_loop(0, self.blocks, step, 0)

    def pick(self, values, window):
        chosen = values[0]
        for place in range(1, len(values)):
            chosen = jnp.where(window == place, values[place], chosen)
        return chosen

    def each_window(self, body):
        def step(window, carry):
            count = self.pick(self.counts, window)
            start = pl.multiple_of(self.pick(self.starts, window), 16)
            body(256, count, pl.ds(start, 256))

            return carry

        lax.fori_loop(0, len(self.counts), step, 0)


def marks(row_index, name, count, length):
    listed = row_index[pl.ds(name, 1), :]
    slot = lax.broadcasted_iota(jnp.int32, (length, length), 0)
    place = lax.broadcasted_iota(jnp.int32, (length, length), 1)
    hit = jnp.logical_and(slot == listed, place < count)
    return jnp.where(hit, 1.0, 0.0).astype(LOW)


def mean_of(values):
    return jnp.mean(values, axis=-1, keepdims=True)


def normalize(values):
    centre = values - mean_of(values)
    inverse = lax.rsqrt(mean_of(centre * centre) + EPS)
    return centre * inverse, inverse


def normalize_back(grad, gain, normal, inverse):
    scaled = grad * gain
    return inverse * (scaled - mean_of(scaled) - normal * mean_of(scaled * normal))


def two_heads(pair, lane_low, lane_high):
    return jnp.concatenate([pair * lane_low, pair * lane_high], axis=0)


def lane_masks(lanes):
    lane = lax.broadcasted_iota(jnp.int32, (1, lanes), 1)
    low = jnp.where(lane < lanes // 2, 1.0, 0.0)
    return low.astype(LOW), (1.0 - low).astype(LOW)


def join_heads(stacked):
    size, lanes = stacked.shape[0] // 2, stacked.shape[1]
    lane = lax.broadcasted_iota(jnp.int32, (size, lanes), 1)
    return jnp.where(lane < lanes // 2, stacked[:size], stacked[size:])


def forward_kernel(
    meta, row_index, x, w_qkv, w_attn, w_in, w_out, bias_qv, out_bias, bias_in, gain, shift,
    lefts_out, qkv_out, slope_out, normal_out, inverse_out, top_out, layer_out,
    wv_qkv, wv_attn, wv_in, wv_out, lefts, qkv, slope, normal, inverse, top, state,
    weight_sem, out_sem,
):
    each, length, width = x.shape
    wins = row_index.shape[0]
    layers = w_qkv.shape[0]
    hidden_width = w_in.shape[2]
    pieces = hidden_width // width
    part = width // pieces
    plan = Plan(meta, wins, each)
    weights = ((w_qkv, wv_qkv), (w_attn, wv_attn), (w_in, wv_in), (w_out, wv_out))

    def fetch(layer, which):
        source, target = weights[which]
        return pltpu.make_async_copy(
            source.at[layer], target.at[layer], weight_sem.at[layer, which]
        )

    for layer in range(layers):
        for which in range(4):
            fetch(layer, which).start()

    state[...] = jnp.zeros_like(state)
    for layer in range(layers):
        lefts[layer, 1] = jnp.zeros(lefts.shape[2:], LOW)
        qkv[layer] = jnp.zeros(qkv.shape[1:], LOW)
    for place in range(each):
        hits = marks(row_index, plan.names[place], plan.counts[place], length)
        start = pl.multiple_of(plan.starts[place], 16)
        state[pl.ds(start, length), :] = dot(hits, x[place], 0, 0)

    kept = (
        (lefts, lefts_out, lambda ref, layer, rows: ref.at[layer, :, rows, :]),
        (qkv, qkv_out, lambda ref, layer, rows: ref.at[layer, rows, :]),
        (slope, slope_out, lambda ref, layer, rows: ref.at[layer, rows, :]),
        (normal, normal_out, lambda ref, layer, rows: ref.at[layer, :, rows, :]),
        (inverse, inverse_out, lambda ref, layer, rows: ref.at[layer, rows, :]),
        (top, top_out, lambda ref, layer, rows: ref.at[layer, rows, :]),
    )

    def stores(layer, block, rows):
        return [
            pltpu.make_async_copy(
                view(source, layer, rows), view(target, layer, rows), out_sem.at[layer, which, block]
            )
            for which, (source, target, view) in enumerate(kept)
        ]

    lane_low, lane_high = lane_masks(128)

    def one_layer(layer, carry):
        fetch(layer, 0).wait()

        def project(size, block, rows):
            tokens = state[rows, :].astype(LOW)
            lefts[layer, 0, rows, :] = tokens
            for which in range(3):
                columns = slice(which * width, (which + 1) * width)
                joint = dot(tokens, wv_qkv[layer, :, columns], 1, 0)
                if which == 0:
                    joint = (joint + bias_qv[pl.ds(layer, 1), :width]).astype(LOW) * LOW(0.125)
                elif which == 2:
                    joint = (joint + bias_qv[pl.ds(layer, 1), width:]).astype(LOW)
                else:
                    joint = joint.astype(LOW)
                qkv[layer, rows, columns] = joint

        plan.each_block(project)

        def attend(size, count, rows):
            column = lax.broadcasted_iota(jnp.int32, (2 * size, size), 1)
            live = column < count

            def pair(which, carry):
                at = pl.multiple_of(which * 128, 128)
                query = two_heads(qkv[layer, rows, pl.ds(at, 128)], lane_low, lane_high)
                key = qkv[layer, rows, pl.ds(pl.multiple_of(at + width, 128), 128)]
                value = qkv[layer, rows, pl.ds(pl.multiple_of(at + 2 * width, 128), 128)]
                scores = jnp.where(live, dot(query, key, 1, 1), -1e30)
                peak = jnp.max(scores, axis=-1, keepdims=True)
                expo = jnp.exp(scores - peak)
                total = jnp.sum(expo, axis=-1, keepdims=True)
                probs = (expo * (1.0 / total)).astype(LOW)
                lefts[layer, 1, rows, pl.ds(at, 128)] = join_heads(dot(probs, value, 1, 0)).astype(LOW)
                logs = jnp.broadcast_to(peak + jnp.log(total), (2 * size, 128))
                top[layer, rows, pl.ds(at, 128)] = join_heads(logs)
                return carry

            lax.fori_loop(0, width // 128, pair, 0)

        plan.each_window(attend)
        for which in range(1, 4):
            fetch(layer, which).wait()

        def feed(size, block, rows):
            first = dot(lefts[layer, 1, rows, :], wv_attn[layer], 1, 0) + out_bias[layer, 0:1, :]
            one, inverse_one = normalize(state[rows, :] + first)
            normal[layer, 0, rows, :] = one
            after = one * gain[layer, 0:1, :] + shift[layer, 0:1, :]
            after_low = after.astype(LOW)
            lefts[layer, 2, rows, :] = after_low
            second = jnp.zeros((size, width), F32)
            for piece in range(pieces):
                columns = slice(piece * width, (piece + 1) * width)
                hidden = dot(after_low, wv_in[layer, :, columns], 1, 0) + bias_in[pl.ds(layer, 1), columns]
                squared = hidden * hidden
                bend = jnp.tanh(SMOOTH * hidden * (1.0 + CUBIC * squared))
                half = 0.5 * (1.0 + bend)
                active = (hidden * half).astype(LOW)
                rise = half + 0.5 * hidden * (1.0 - bend * bend) * (
                    SMOOTH * (1.0 + 3.0 * CUBIC * squared)
                )
                slope[layer, rows, columns] = rise.astype(LOW)
                for sub in range(pieces):
                    lefts[layer, 3 + sub, rows, piece * part : (piece + 1) * part] = active[
                        :, sub * part : (sub + 1) * part
                    ]
                second = second + dot(active, wv_out[layer, columns, :], 1, 0)
            two, inverse_two = normalize(after + second + out_bias[layer, 1:2, :])
            normal[layer, 1, rows, :] = two
            state[rows, :] = two * gain[layer, 1:2, :] + shift[layer, 1:2, :]
            lane = lax.broadcasted_iota(jnp.int32, (size, 128), 1)
            inverse[layer, rows, :] = jnp.where(lane < 64, inverse_one, inverse_two)
            for copy in stores(layer, block, rows):
                copy.start()

        plan.each_block(feed)
        return carry

    lax.fori_loop(0, layers, one_layer, 0)
    for place in range(each):
        hits = marks(row_index, plan.names[place], plan.counts[place], length)
        start = pl.multiple_of(plan.starts[place], 16)
        layer_out[place] = dot(hits, state[pl.ds(start, length), :].astype(LOW), 1, 0).astype(LOW)

    for layer in range(layers):

        def finish(size, block, rows, layer=layer):
            for copy in stores(layer, block, rows):
                copy.wait()

        plan.each_block(finish)


def backward_kernel(
    meta, row_index, g, w_qkv, w_attn, w_in, w_out, gain,
    qkv_in, slope_in, normal_in, inverse_in, top_in,
    rights_out, grad_out, sums,
    wv_qkv, wv_attn, wv_in, wv_out, rights, qkv, slope, normal, inverse, top, state, mixed_grad,
    weight_sem, in_sem, out_sem,
):
    each, length, width = g.shape
    wins = row_index.shape[0]
    layers = w_qkv.shape[0]
    hidden_width = w_in.shape[2]
    pieces = hidden_width // width
    plan = Plan(meta, wins, each)
    weights = ((w_out, wv_out), (w_in, wv_in), (w_attn, wv_attn), (w_qkv, wv_qkv))

    def fetch(layer, which):
        source, target = weights[which]
        return pltpu.make_async_copy(
            source.at[layer], target.at[layer], weight_sem.at[layer, which]
        )

    kept = (
        (normal_in, normal, lambda ref, layer, rows: ref.at[layer, :, rows, :]),
        (inverse_in, inverse, lambda ref, layer, rows: ref.at[layer, rows, :]),
        (slope_in, slope, lambda ref, layer, rows: ref.at[layer, rows, :]),
        (qkv_in, qkv, lambda ref, layer, rows: ref.at[layer, rows, :]),
        (top_in, top, lambda ref, layer, rows: ref.at[layer, rows, :]),
    )

    def loads(layer, block, rows):
        return [
            pltpu.make_async_copy(
                view(source, layer, rows), view(target, layer, rows), in_sem.at[layer, which, block]
            )
            for which, (source, target, view) in enumerate(kept)
        ]

    for layer in range(layers):
        qkv[layer, 128:] = jnp.zeros((qkv.shape[1] - 128, qkv.shape[2]), LOW)
    for layer in reversed(range(layers)):

        def begin(size, block, rows, layer=layer):
            for copy in loads(layer, block, rows):
                copy.start()

        fetch(layer, 0).start()
        plan.each_block(begin)
        for which in range(1, 4):
            fetch(layer, which).start()

    state[...] = jnp.zeros_like(state)
    mixed_grad[...] = jnp.zeros_like(mixed_grad)
    sums[...] = jnp.zeros_like(sums)
    for layer in range(layers):
        rights[layer, 0:3] = jnp.zeros((3,) + rights.shape[2:], LOW)
    for place in range(each):
        hits = marks(row_index, plan.names[place], plan.counts[place], length)
        start = pl.multiple_of(plan.starts[place], 16)
        state[pl.ds(start, length), :] = dot(hits, g[place], 0, 0)

    lane_low, lane_high = lane_masks(128)

    def add_rows(layer, place, values):
        sums[layer, place : place + 1, :] += jnp.sum(values, axis=0, keepdims=True)

    def one_layer(step, carry):
        layer = layers - 1 - step
        for which in range(3):
            fetch(layer, which).wait()

        def feed(size, block, rows):
            for copy in loads(layer, block, rows):
                copy.wait()
            grad = state[rows, :]
            two = normal[layer, 1, rows, :]
            add_rows(layer, 9, grad * two)
            add_rows(layer, 11, grad)
            back = normalize_back(grad, gain[layer, 1:2, :], two, inverse[layer, rows, 64:65])
            back_low = back.astype(LOW)
            rights[layer, 8, rows, :] = back_low
            add_rows(layer, 3, back_low.astype(F32))
            for piece in range(pieces):
                columns = slice(piece * width, (piece + 1) * width)
                active = dot(back_low, wv_out[layer, columns, :], 1, 1)
                hidden = (active * slope[layer, rows, columns].astype(F32)).astype(LOW)
                rights[layer, 4 + piece, rows, :] = hidden
                add_rows(layer, 4 + piece, hidden.astype(F32))
                back = back + dot(hidden, wv_in[layer, :, columns], 1, 1)
            one = normal[layer, 0, rows, :]
            add_rows(layer, 8, back * one)
            add_rows(layer, 10, back)
            back = normalize_back(back, gain[layer, 0:1, :], one, inverse[layer, rows, 0:1])
            back_low = back.astype(LOW)
            rights[layer, 3, rows, :] = back_low
            add_rows(layer, 2, back_low.astype(F32))
            mixed_grad[rows, :] = dot(back_low, wv_attn[layer], 1, 1).astype(LOW)
            state[rows, :] = back

        plan.each_block(feed)

        def attend(size, count, rows):
            row = lax.broadcasted_iota(jnp.int32, (2 * size, size), 0)
            column = lax.broadcasted_iota(jnp.int32, (2 * size, size), 1)
            row = jnp.where(row < size, row, row - size)
            live = jnp.logical_and(column < count, row < count)

            def pair(which, carry):
                at = pl.multiple_of(which * 128, 128)
                query = two_heads(qkv[layer, rows, pl.ds(at, 128)], lane_low, lane_high)
                key = qkv[layer, rows, pl.ds(pl.multiple_of(at + width, 128), 128)]
                value = qkv[layer, rows, pl.ds(pl.multiple_of(at + 2 * width, 128), 128)]
                grad = two_heads(mixed_grad[rows, pl.ds(at, 128)], lane_low, lane_high)
                logs = top[layer, rows, pl.ds(at, 128)]
                logs = jnp.concatenate([logs[:, 0:1], logs[:, 64:65]], axis=0)
                probs = jnp.where(live, jnp.exp(dot(query, key, 1, 1) - logs), 0.0)
                d_probs = dot(grad, value, 1, 1)
                centre = jnp.sum(probs * d_probs, axis=-1, keepdims=True)
                d_scores = (probs * (d_probs - centre)).astype(LOW)
                d_query = join_heads(dot(d_scores, key, 1, 0)) * 0.125
                rights[layer, 0, rows, pl.ds(at, 128)] = d_query.astype(LOW)
                rights[layer, 1, rows, pl.ds(at, 128)] = dot(d_scores, query, 0, 0).astype(LOW)
                rights[layer, 2, rows, pl.ds(at, 128)] = dot(probs.astype(LOW), grad, 0, 0).astype(LOW)
                return carry

            lax.fori_loop(0, width // 128, pair, 0)

        plan.each_window(attend)
        fetch(layer, 3).wait()

        def project(size, block, rows):
            grad = state[rows, :]
            for which in range(3):
                columns = slice(which * width, (which + 1) * width)
                piece = rights[layer, which, rows, :]
                grad = grad + dot(piece, wv_qkv[layer, :, columns], 1, 1)
                if which != 1:
                    add_rows(layer, which // 2, piece.astype(F32))
            state[rows, :] = grad
            pltpu.make_async_copy(
                rights.at[layer, :, rows, :], rights_out.at[layer, :, rows, :], out_sem.at[layer, block]
            ).start()

        plan.each_block(project)
        return carry

    lax.fori_loop(0, layers, one_layer, 0)
    for place in range(each):
        hits = marks(row_index, plan.names[place], plan.counts[place], length)
        start = pl.multiple_of(plan.starts[place], 16)
        grad_out[place] = dot(hits, state[pl.ds(start, length), :].astype(LOW), 1, 0).astype(LOW)

    for layer in range(layers):

        def finish(size, block, rows, layer=layer):
            pltpu.make_async_copy(
                rights.at[layer, :, rows, :], rights_out.at[layer, :, rows, :], out_sem.at[layer, block]
            ).wait()

        plan.each_block(finish)


LAGS = (0, 1, 3, 4, 5, 6, 7, 8, 9)
ROUTE = (("var", 1), ("var", 2), ("win", 1), ("win", 2), ("win", 4))


def merge_kernel(
    owners, meta, lefts, rights, sums, layer_out, grad,
    merged, sums_out, layer_back, grad_back,
    left_in, right_in, part, got_core, hold_x, got_x, hold_y, got_y, hold_a, got_a, hold_b, got_b,
    whole, sums_hold, sums_got,
    in_sem, send_sem, recv_sem, out_sem, sums_send, sums_recv, back_send, back_recv, own_sem,
):
    chunks = merged.shape[0]
    layers = lefts.shape[0]
    per_layer = chunks // layers
    packed, width = left_in.shape[1], left_in.shape[2]
    part_rows = part.shape[3]
    each = layer_out.shape[0]
    rows = layer_back.shape[1]
    win, var = lax.axis_index("win"), lax.axis_index("var")
    core, x_half = half_of(var, 1), half_of(var, 2)
    y_half, a_half, b_half = half_of(win, 1), half_of(win, 2), half_of(win, 4)
    others = [flip(var, 1), flip(var, 2), flip(flip(var, 1), 2)]
    route = [partner(axis, bit) for axis, bit in ROUTE]
    greet(route + [(win, others[2])])
    total = meta[meta.shape[0] - 1]

    def block_of(chunk):
        layer, place = layers - 1 - chunk // per_layer, lax.rem(chunk, per_layer)
        group, member = place // 4, lax.rem(place, 4)
        first, third = (2 - group) // 2, group // 2
        second = 1 - first - third
        alone = 1 - (member + 3) // 4
        left = first * (3 + member) + second * 2 + third * alone
        right = first * 8 + second * (4 + member) + third * (member - 1 + 4 * alone)
        return layer, left, right

    def loads(chunk):
        layer, left, right = block_of(chunk)
        slot = lax.rem(chunk, 2)
        return (
            pltpu.make_async_copy(lefts.at[layer, left], left_in.at[slot], in_sem.at[0, slot]),
            pltpu.make_async_copy(rights.at[layer, right], right_in.at[slot], in_sem.at[1, slot]),
        )

    quarter = part_rows // 2
    eighth = quarter // 2
    sixteenth = eighth // 2
    at_y = pl.multiple_of(y_half * quarter, sixteenth)
    at_a = pl.multiple_of(at_y + a_half * eighth, sixteenth)
    at_b = pl.multiple_of(at_a + b_half * sixteenth, sixteenth)

    def exchange(stage, chunk):
        if stage == 0:
            source, target = part.at[chunk, 1 - core], got_core.at[chunk]
        elif stage == 1:
            source, target = hold_x.at[chunk, 1 - x_half], got_x.at[chunk]
        elif stage == 2:
            source, target = hold_y.at[chunk, 1 - y_half], got_y.at[chunk]
        elif stage == 3:
            source, target = hold_a.at[chunk, 1 - a_half], got_a.at[chunk]
        elif stage == 4:
            source, target = hold_b.at[chunk, 1 - b_half], got_b.at[chunk]
        else:
            at, size = ((at_b, sixteenth), (at_a, eighth), (at_y, quarter))[stage - 5]
            source = whole.at[chunk, pl.ds(at, size), :]
            target = source
        return pltpu.make_async_remote_copy(
            src_ref=source,
            dst_ref=target,
            send_sem=send_sem.at[stage, chunk],
            recv_sem=recv_sem.at[stage, chunk],
            device_id=route[(0, 1, 2, 3, 4, 4, 3, 2)[stage]],
            device_id_type=MESH,
        )

    def out_copy(chunk):
        return pltpu.make_async_copy(whole.at[chunk], merged.at[chunk], out_sem.at[chunk])

    def produce(chunk):
        for copy in loads(chunk):
            copy.wait()
        slot = lax.rem(chunk, 2)
        live = lax.broadcasted_iota(jnp.int32, (packed, width), 0) < total
        left = jnp.where(live, left_in[slot], LOW(0))
        right = jnp.where(live, right_in[slot], LOW(0))
        product = dot(left, right, 0, 0).astype(LOW)
        for shard in range(owners):
            part[chunk, shard % 2, shard // 2] = product[shard * part_rows : (shard + 1) * part_rows]
        exchange(0, chunk).start()

    def add(mine, theirs):
        return (mine.astype(F32) + theirs.astype(F32)).astype(LOW)

    def take(stage, chunk):
        exchange(stage - 1, chunk).wait_recv()
        if stage == 1:
            hold_x[chunk] = add(part[chunk, core], got_core[chunk])
        elif stage == 2:
            hold_y[chunk] = add(hold_x[chunk, x_half], got_x[chunk]).reshape(hold_y.shape[1:])
        elif stage == 3:
            hold_a[chunk] = add(hold_y[chunk, y_half], got_y[chunk]).reshape(hold_a.shape[1:])
        elif stage == 4:
            hold_b[chunk] = add(hold_a[chunk, a_half], got_a[chunk]).reshape(hold_b.shape[1:])
        elif stage == 5:
            whole[chunk, pl.ds(at_b, sixteenth), :] = add(hold_b[chunk, b_half], got_b[chunk])
        if stage < 8:
            exchange(stage, chunk).start()
        else:
            out_copy(chunk).start()

    def sums_exchange(turn):
        return pltpu.make_async_remote_copy(
            src_ref=sums_hold.at[turn],
            dst_ref=sums_got.at[turn],
            send_sem=sums_send.at[turn],
            recv_sem=sums_recv.at[turn],
            device_id=route[turn],
            device_id_type=MESH,
        )

    def back_copies():
        sent = []
        for which, (source, target) in enumerate(((grad, grad_back), (layer_out, layer_back))):
            for place, other in enumerate(others):
                sent.append(
                    pltpu.make_async_remote_copy(
                        src_ref=source.at[:, pl.ds(pl.multiple_of(other * rows, rows), rows), :],
                        dst_ref=target.at[pl.ds(var * each, each)],
                        send_sem=back_send.at[which, place],
                        recv_sem=back_recv.at[which, place],
                        device_id=(win, other),
                        device_id_type=MESH,
                    )
                )
        return sent

    def own_copies():
        return [
            pltpu.make_async_copy(
                source.at[:, pl.ds(pl.multiple_of(var * rows, rows), rows), :],
                target.at[pl.ds(var * each, each)],
                own_sem.at[which],
            )
            for which, (source, target) in enumerate(((grad, grad_back), (layer_out, layer_back)))
        ]

    for copy in loads(0):
        copy.start()
    for copy in own_copies():
        copy.start()
    sums_hold[0] = sums[...]
    sums_exchange(0).start()

    def step(now, carry):
        @pl.when(now + 1 < chunks)
        def _():
            for copy in loads(now + 1):
                copy.start()

        @pl.when(now < chunks)
        def _():
            produce(now)

        for stage in range(1, 9):
            lag = LAGS[stage]

            @pl.when(jnp.logical_and(now >= lag, now < chunks + lag))
            def _(stage=stage, lag=lag):
                take(stage, now - lag)

        for turn in range(5):

            @pl.when(now == 2 * turn + 4)
            def _(turn=turn):
                sums_exchange(turn).wait_recv()
                summed = sums_hold[turn] + sums_got[turn]
                if turn < 4:
                    sums_hold[turn + 1] = summed
                    sums_exchange(turn + 1).start()
                else:
                    sums_out[...] = summed

        @pl.when(now == chunks + 1)
        def _():
            for copy in back_copies():
                copy.start()

        return carry

    lax.fori_loop(0, chunks + LAGS[8], step, 0)

    def settle(chunk, carry):
        for stage in range(8):
            exchange(stage, chunk).wait_send()
        out_copy(chunk).wait()
        return carry

    lax.fori_loop(0, chunks, settle, 0)
    for turn in range(5):
        sums_exchange(turn).wait_send()
    for copy in own_copies():
        copy.wait()
    for copy in back_copies():
        copy.wait()


SETTLED = (2, 3, 4, 5, 6, 7, 8)
LAG = 2
DEPTH = 4
Y_FIRST = (1,)
Z_FIRST = (4, 10)


class Network:
    def __init__(self, owners, part, got, whole, merged, send_sem, recv_sem, out_sem):
        self.owners, self.part, self.got, self.whole = owners, part, got, whole
        self.merged, self.send_sem, self.recv_sem, self.out_sem = merged, send_sem, recv_sem, out_sem
        self.chunks, self.rows = whole.shape[0], whole.shape[1]
        self.ring = part.shape[0]
        win, var = lax.axis_index("win"), lax.axis_index("var")
        self.win, self.var = win, var
        self.core = half_of(var, 1)
        self.along = {
            "core": (self.core, (win, flip(var, 1))),
            "x": (half_of(var, 2), (win, flip(var, 2))),
            "y": (half_of(win, 1), (flip(win, 1), var)),
            "z": (half_of(win, 2), (flip(win, 2), var)),
            "w": (half_of(win, 4), (flip(win, 4), var)),
        }
        unit, at, self.places = self.rows // 8, 0, {}
        for stage, name in ((7, "y"), (6, "z"), (5, "w")):
            size = (1 << (stage - 5)) * unit
            at = pl.multiple_of(at + self.along[name][0] * size, size)
            self.places[stage] = (at, size)

    @staticmethod
    def way(chunk):
        place = chunk % 12

        def among(chosen):
            return sum(1 - ((place - one) * (place - one) + 143) // 144 for one in chosen)

        return among(Y_FIRST), among(Z_FIRST)

    def hop(self, stage, chunk):
        name = ("core", "x", "y", "z", "w", "w", "z", "y")[stage]
        if stage not in (1, 2, 3):
            return self.along[name]
        y_first, z_first = self.way(chunk)
        shares = {
            1: ((1 - y_first - z_first, "x"), (y_first, "y"), (z_first, "z")),
            2: ((1 - y_first - z_first, "y"), (y_first + z_first, "x")),
            3: ((1 - z_first, "z"), (z_first, "y")),
        }[stage]
        half, win, var = 0, 0, 0
        for share, name in shares:
            bit, (to_win, to_var) = self.along[name]
            half, win, var = half + share * bit, win + share * to_win, var + share * to_var
        return half, (win, var)

    def part_of(self, stage, half):
        size = self.got[stage].shape[1]
        return pl.ds(pl.multiple_of(half * size, 16), size)

    def exchange(self, stage, chunk):
        half, beyond = self.hop(stage, chunk)
        if stage == 0:
            source, target = self.part.at[chunk % self.ring, 1 - half], self.got[0].at[chunk]
        elif stage < 5:
            source, target = self.got[stage - 1].at[chunk, self.part_of(stage, 1 - half), :], self.got[stage].at[chunk]
        else:
            at, size = self.places[stage]
            source = target = self.whole.at[chunk, pl.ds(at, size), :]
        return pltpu.make_async_remote_copy(
            src_ref=source,
            dst_ref=target,
            send_sem=self.send_sem.at[stage, chunk],
            recv_sem=self.recv_sem.at[stage, chunk],
            device_id=beyond,
            device_id_type=MESH,
        )

    def out_copy(self, chunk):
        return pltpu.make_async_copy(self.whole.at[chunk], self.merged.at[chunk], self.out_sem.at[chunk])

    def emit(self, chunk, place, left, right):
        product = dot(left, right, 0, 0).astype(LOW)
        slot = chunk % self.ring

        @pl.when(chunk >= self.ring)
        def _():
            self.exchange(0, chunk - self.ring).wait_send()

        rows, quarter = self.rows, self.rows // 4
        y_first, z_first = self.way(place)
        for shard in range(self.owners):
            core, x = shard % 2, shard // 2
            for y in range(2):
                for z in range(2):
                    straight, over_y, over_z = 4 * x + 2 * y + z, 4 * y + 2 * x + z, 4 * z + 2 * x + y
                    at = straight + y_first * (over_y - straight) + z_first * (over_z - straight)
                    here = shard * rows + (2 * y + z) * quarter
                    self.part[slot, core, pl.ds(at * quarter, quarter), :] = product[here : here + quarter]
        self.exchange(0, chunk).start()

    def take(self, stage, chunk):
        def add(mine, target):
            return (mine.astype(F32) + target[chunk].astype(F32)).astype(LOW)

        self.exchange(stage - 1, chunk).wait_recv()
        if stage == 1:
            target = self.got[0]
            target[chunk] = add(self.part[chunk % self.ring, self.core], target)
        elif stage <= 4:
            half, _ = self.hop(stage - 1, chunk)
            target = self.got[stage - 1]
            target[chunk] = add(self.got[stage - 2][chunk, self.part_of(stage - 1, half), :], target)
        elif stage == 5:
            half, _ = self.hop(4, chunk)
            at, unit = self.places[5]
            self.whole[chunk, pl.ds(at, unit), :] = add(self.got[3][chunk, self.part_of(4, half), :], self.got[4])
        if stage == 1:

            @pl.when(chunk < DEPTH)
            def _():
                self.exchange(1, chunk).start()
        elif stage < 8:
            self.exchange(stage, chunk).start()
        else:
            self.out_copy(chunk).start()

    def pump(self, turn):
        for place, stage in enumerate(SETTLED):
            chunk = turn - LAG * place

            @pl.when(jnp.logical_and(chunk >= 0, chunk < self.chunks))
            def _(stage=stage, chunk=chunk):
                self.take(stage, chunk)

            if place == 0:

                @pl.when(turn + DEPTH < self.chunks)
                def _():
                    self.exchange(1, turn + DEPTH).start()

    def settle(self, chunk):
        for stage in range(1, 8):
            self.exchange(stage, chunk).wait_send()
        self.out_copy(chunk).wait()

    def settle_ring(self):
        for chunk in range(self.chunks - self.ring, self.chunks):
            self.exchange(0, chunk).wait_send()


def packed_kernel(
    owners, size,
    windows, row_index, inputs, cotangent, w_qkv, w_attn, w_in, w_out, bias_qv, out_bias, bias_in, gain, shift,
    merged, sums_out, layer_back, grad_back, meta,
    x_stage, x, most, most_got, wv_qkv, wv_attn, wv_in, wv_out, g_stage, g, spots, state, lefts, rights, qkv, slope,
    normal, inverse, top, mixed_grad, last_right, sums, part, got_core, got_one, got_two, got_three, got_four, whole,
    sums_hold, sums_got,
    weight_sem, send_sem, recv_sem, out_sem, sums_send, sums_recv, far_send, far_recv, own_sem, most_send, most_recv,
):
    each, length, width = x.shape
    wins, rows = cotangent.shape[0], cotangent.shape[1]
    layers = w_qkv.shape[0]
    hidden_width = w_in.shape[2]
    pieces = hidden_width // width
    strip = width // pieces
    pairs = width // 128
    got = (got_core, got_one, got_two, got_three, got_four)
    layer_out, grad_out = x, g
    net = Network(owners, part, got, whole, merged, send_sem, recv_sem, out_sem)
    win, var = net.win, net.var
    others = [flip(var, 1), flip(var, 2), flip(flip(var, 1), 2)]
    weights = ((w_qkv, wv_qkv), (w_attn, wv_attn), (w_in, wv_in), (w_out, wv_out))

    def fetch(layer, which):
        source, target = weights[which]
        return pltpu.make_async_copy(source.at[layer], target.at[layer], weight_sem.at[layer, which])

    for layer in range(layers):
        for which in range(4):
            fetch(layer, which).start()

    barrier = pltpu.get_barrier_semaphore()
    across = [(flip(win, bit), var) for bit in (1, 2, 4)]
    friends = [(win, other) for other in others] + across
    for friend in friends:
        pl.semaphore_signal(barrier, inc=1, device_id=friend, device_id_type=MESH)
    order = assign(windows, wins, owners)
    for place in range(wins):
        meta[place] = order[place]
        x_stage[place] = inputs[order[place]]
    meta[wins] = var
    pl.semaphore_wait(barrier, len(friends))
    mine = pl.ds(pl.multiple_of(var * rows, rows), rows)

    def remote(source, target, which, place, other):
        return pltpu.make_async_remote_copy(
            src_ref=source,
            dst_ref=target,
            send_sem=far_send.at[which, place],
            recv_sem=far_recv.at[which, place],
            device_id=(win, other),
            device_id_type=MESH,
        )

    def to_owners(stage, target, which):
        return [
            remote(stage.at[pl.ds(other * each, each)], target.at[:, mine, :], which, place, other)
            for place, other in enumerate(others)
        ] + [pltpu.make_async_copy(stage.at[pl.ds(var * each, each)], target.at[:, mine, :], own_sem.at[which])]

    def to_slots(source, target, which):
        home = target.at[pl.ds(var * each, each)]
        return [
            remote(source.at[:, pl.ds(pl.multiple_of(other * rows, rows), rows), :], home, which, place, other)
            for place, other in enumerate(others)
        ] + [pltpu.make_async_copy(source.at[:, mine, :], home, own_sem.at[which])]

    for copy in to_owners(x_stage, x, 3):
        copy.start()
    for place in range(wins):
        g_stage[place] = cotangent[order[place]]

    names, counts = [], []
    for place in range(each):
        name = order[place]
        for owner in range(1, owners):
            name = jnp.where(var == owner, order[owner * each + place], name)
        names.append(name)
        counts.append(windows[name])

    shares = counts[0] + counts[2] <= BLOCKS[0]
    starts = [jnp.int32(0), jnp.int32(BLOCKS[0]), jnp.where(shares, counts[0], BLOCKS[0] + counts[1])]
    for place in range(each):
        hits = marks(row_index, names[place], counts[place], length)
        along = lax.broadcasted_iota(jnp.int32, (length, size), 0) + starts[place]
        moved = jnp.where(lax.broadcasted_iota(jnp.int32, (length, size), 1) == along, 1.0, 0.0).astype(LOW)
        spots[place * length : (place + 1) * length] = dot(hits, moved, 1, 0).astype(LOW)

    row = lax.broadcasted_iota(jnp.int32, (size, 128), 0)
    lane = lax.broadcasted_iota(jnp.int32, (size, 128), 1)
    owner = jnp.full((size, 128), each, jnp.int32)
    for place in range(each):
        inside = jnp.logical_and(row >= starts[place], row < starts[place] + counts[place])
        owner = jnp.where(inside, place, owner)
    key_mark = jnp.where(lane == owner, 1.0, 0.0).astype(LOW)
    query_mark = jnp.where(lane == owner, jnp.where(lane < each, 0.0, -1e30), -1e30).astype(LOW)
    lane_low, lane_high = lane_masks(128)

    largest = jnp.int32(0)
    for owner in range(owners):
        held = [windows[order[owner * each + place]] for place in range(each)]
        second = jnp.where(held[0] + held[2] <= BLOCKS[0], held[1], held[1] + held[2])
        largest = jnp.maximum(largest, second)
    most[0] = jnp.full(most.shape[1:], largest, jnp.int32)
    for turn, friend in enumerate(across):
        copy = pltpu.make_async_remote_copy(
            src_ref=most.at[turn],
            dst_ref=most_got.at[turn],
            send_sem=most_send.at[turn],
            recv_sem=most_recv.at[turn],
            device_id=friend,
            device_id_type=MESH,
        )
        copy.start()
        copy.wait()
        most[turn + 1] = jnp.maximum(most[turn], most_got[turn])
    meta[wins + 1] = jnp.max(most[len(across)])
    *away, home = to_owners(x_stage, x, 3)
    for copy in away:
        copy.wait_send()
    for copy in to_owners(g_stage, g, 0):
        copy.start()
    for copy in away:
        copy.wait_recv()
    home.wait()
    state[...] = dot(spots[...], x[...].reshape(each * length, width), 0, 0)
    fetch(0, 0).wait()

    spans = []
    for block in BLOCKS:
        first = spans[-1].stop if spans else 0
        spans.append(slice(first, first + block))

    def masked_scores(layer, at, span):
        query = two_heads(qkv[layer, span, pl.ds(at, 128)], lane_low, lane_high)
        key = qkv[layer, span, pl.ds(at + width, 128)]
        value = qkv[layer, span, pl.ds(at + 2 * width, 128)]
        allowed = jnp.concatenate([query_mark[span], query_mark[span]], axis=0)
        scores = dot(
            jnp.concatenate([key, key_mark[span]], axis=1), jnp.concatenate([query, allowed], axis=1), 1, 1
        )
        return query, key, value, scores

    def forward_layer(layer, carry):
        @pl.when(layer > 0)
        def _():
            fetch(layer, 0).wait()

        tokens = state[...].astype(LOW)
        lefts[layer, 0] = tokens
        for which in range(3):
            columns = slice(which * width, (which + 1) * width)
            joint = dot(tokens, wv_qkv[layer, :, columns], 1, 0)
            if which == 0:
                joint = (joint + bias_qv[pl.ds(layer, 1), :width]).astype(LOW) * LOW(0.125)
            elif which == 2:
                joint = (joint + bias_qv[pl.ds(layer, 1), width:]).astype(LOW)
            else:
                joint = joint.astype(LOW)
            qkv[layer, :, columns] = joint
        for pair, span in [(pair, span) for pair in range(pairs) for span in spans]:
            at = pair * 128
            _, _, value, scores = masked_scores(layer, at, span)
            peak = jnp.max(scores, axis=0, keepdims=True)
            expo = jnp.exp(scores - peak)
            total = jnp.sum(expo, axis=0, keepdims=True)
            probs = (expo * (1.0 / total)).astype(LOW)
            lefts[layer, 1, span, pl.ds(at, 128)] = join_heads(dot(probs, value, 0, 0)).astype(LOW)
            top[layer, pair, :, 2 * span.start : 2 * span.stop] = peak + jnp.log(total)
        for which in range(1, 4):
            fetch(layer, which).wait()
        first = dot(lefts[layer, 1], wv_attn[layer], 1, 0) + out_bias[layer, 0:1, :]
        one, inverse_one = normalize(state[...] + first)
        normal[layer, 0] = one.astype(LOW)
        after = one * gain[layer, 0:1, :] + shift[layer, 0:1, :]
        after_low = after.astype(LOW)
        lefts[layer, 2] = after_low
        second = jnp.zeros((size, width), F32)
        for piece in range(pieces):
            columns = slice(piece * width, (piece + 1) * width)
            hidden = dot(after_low, wv_in[layer, :, columns], 1, 0) + bias_in[pl.ds(layer, 1), columns]
            squared = hidden * hidden
            bend = jnp.tanh(hidden * (SMOOTH + SMOOTH * CUBIC * squared))
            half = 0.5 + 0.5 * bend
            active = (hidden * half).astype(LOW)
            rise = half + (hidden * half) * (1.0 - bend) * (SMOOTH + SMOOTH * 3.0 * CUBIC * squared)
            slope[layer, :, columns] = rise.astype(LOW)
            for sub in range(pieces):
                lefts[layer, 3 + sub, :, piece * strip : (piece + 1) * strip] = active[
                    :, sub * strip : (sub + 1) * strip
                ]
            second = second + dot(active, wv_out[layer, columns, :], 1, 0)
        two, inverse_two = normalize(after + second + out_bias[layer, 1:2, :])
        normal[layer, 1] = two.astype(LOW)
        state[...] = two * gain[layer, 1:2, :] + shift[layer, 1:2, :]
        lanes = lax.broadcasted_iota(jnp.int32, (size, 128), 1)
        inverse[layer] = jnp.where(lanes < 64, inverse_one, inverse_two)
        return carry

    lax.fori_loop(0, layers, forward_layer, 0)
    layer_out[...] = dot(spots[...], state[...].astype(LOW), 1, 0).astype(LOW).reshape(layer_out.shape)
    for copy in to_owners(g_stage, g, 0):
        copy.wait()
    state[...] = dot(spots[...], g[...].reshape(each * length, width), 0, 0)
    sums[...] = jnp.zeros_like(sums)

    def add_rows(layer, place, values):
        sums[layer, place : place + 1, :] += jnp.sum(values, axis=0, keepdims=True)

    per_layer = net.chunks // layers

    def backward_layer(step, carry):
        layer = layers - 1 - step
        first = step * per_layer
        turn = step * 7

        def emit(place, left, right):
            net.emit(first + place, place, left, right)

        def take(place):
            net.take(1, first + place)

        grad = state[...]
        two = normal[layer, 1].astype(F32)
        back = normalize_back(grad, gain[layer, 1:2, :], two, inverse[layer, :, 64:65])
        back_low = back.astype(LOW)
        last_right[...] = back_low

        def outer(piece, carry):
            emit(piece, lefts[layer, 3 + piece], last_right[...])

            @pl.when(piece > 0)
            def _():
                take(piece - 1)

            return carry

        lax.fori_loop(0, pieces, outer, 0, unroll=4)
        add_rows(layer, 9, grad * two)
        add_rows(layer, 11, grad)
        add_rows(layer, 3, back_low.astype(F32))
        state[...] = back

        def inner(piece, carry):
            columns = pl.ds(pl.multiple_of(piece * width, width), width)
            active = dot(last_right[...], wv_out[layer, columns, :], 1, 1)
            hidden = (active * slope[layer, :, columns].astype(F32)).astype(LOW)
            sums[layer, pl.ds(4 + piece, 1), :] = jnp.sum(hidden.astype(F32), axis=0, keepdims=True)
            rights[0] = hidden
            emit(pieces + piece, lefts[layer, 2], rights[0])
            state[...] += dot(rights[0], wv_in[layer, :, columns], 1, 1)
            take(pieces + piece - 1)

            @pl.when(piece > 0)
            def _():
                net.pump(turn + piece - 1)

            return carry

        lax.fori_loop(0, pieces, inner, 0)
        back = state[...]
        one = normal[layer, 0].astype(F32)
        add_rows(layer, 8, back * one)
        add_rows(layer, 10, back)
        back = normalize_back(back, gain[layer, 0:1, :], one, inverse[layer, :, 0:1])
        back_low = back.astype(LOW)
        emit(8, lefts[layer, 1], back_low)
        take(7)
        add_rows(layer, 2, back_low.astype(F32))
        mixed_grad[...] = dot(back_low, wv_attn[layer], 1, 1).astype(LOW)
        state[...] = back
        net.pump(turn + 3)
        for pair, span in [(pair, span) for pair in range(pairs) for span in spans]:
            at = pair * 128
            query, key, value, scores = masked_scores(layer, at, span)
            grads = two_heads(mixed_grad[span, pl.ds(at, 128)], lane_low, lane_high)
            probs = jnp.exp(scores - top[layer, pair, :, 2 * span.start : 2 * span.stop])
            d_probs = dot(value, grads, 1, 1)
            centre = jnp.sum(probs * d_probs, axis=0, keepdims=True)
            d_scores = (probs * (d_probs - centre)).astype(LOW)
            d_query = join_heads(dot(d_scores, key, 0, 0)) * 0.125
            rights[0, span, pl.ds(at, 128)] = d_query.astype(LOW)
            rights[1, span, pl.ds(at, 128)] = dot(d_scores, query, 1, 0).astype(LOW)
            rights[2, span, pl.ds(at, 128)] = dot(probs.astype(LOW), grads, 1, 0).astype(LOW)
        take(8)
        net.pump(turn + 4)

        def last(which, carry):
            emit(9 + which, lefts[layer, 0], rights[which])

            @pl.when(which > 0)
            def _():
                take(8 + which)

            return carry

        lax.fori_loop(0, 3, last, 0, unroll=3)
        net.pump(turn + 5)
        grad = state[...]
        for which in range(3):
            piece = rights[which]
            grad = grad + dot(piece, wv_qkv[layer, :, which * width : (which + 1) * width], 1, 1)
            if which != 1:
                add_rows(layer, which // 2, piece.astype(F32))
        state[...] = grad
        take(11)
        net.pump(turn + 6)
        return carry

    lax.fori_loop(0, layers, backward_layer, 0)
    first_turn = 7 * layers
    settled = LAG * (len(SETTLED) - 1) + 1
    grad_out[...] = dot(spots[...], state[...].astype(LOW), 1, 0).astype(LOW).reshape(grad_out.shape)

    route = [partner(axis, bit) for axis, bit in ROUTE]

    def sums_exchange(step):
        return pltpu.make_async_remote_copy(
            src_ref=sums_hold.at[step],
            dst_ref=sums_got.at[step],
            send_sem=sums_send.at[step],
            recv_sem=sums_recv.at[step],
            device_id=route[step],
            device_id_type=MESH,
        )

    sums_hold[0] = sums[...]
    sums_exchange(0).start()

    def step(now, carry):
        net.pump(now)
        net.settle(now - settled)

        @pl.when(now == net.chunks - 1)
        def _():
            for copy in to_slots(grad_out, grad_back, 2) + to_slots(layer_out, layer_back, 1):
                copy.start()

        for place in range(5):

            @pl.when(now == first_turn + 1 + 2 * place)
            def _(place=place):
                sums_exchange(place).wait_recv()
                summed = sums_hold[place] + sums_got[place]
                if place < 4:
                    sums_hold[place + 1] = summed
                    sums_exchange(place + 1).start()
                else:
                    sums_out[...] = summed

        return carry

    lax.fori_loop(first_turn, net.chunks + LAG * (len(SETTLED) - 1), step, 0)
    for chunk in [*range(first_turn - settled), *range(net.chunks - 1, net.chunks)]:
        net.settle(chunk)
    net.settle_ring()
    for place in range(5):
        sums_exchange(place).wait_send()
    for copy in to_slots(layer_out, layer_back, 1) + to_slots(grad_out, grad_back, 2):
        copy.wait()


def finish_kernel(
    at_var, meta, sums, merged, layer_back, grad_back,
    layer_out, grad_inputs, qkv, attn, in_, out, bias_qv, out_bias, bias_in, gain, shift,
    chunks, layer_in, grad_in, grad_wide, qkv_wide, attn_wide, in_wide, out_wide, in_sem, out_sem,
):
    wins, rows = layer_back.shape[0], layer_back.shape[1]
    layers, width = qkv.shape[0], merged.shape[2]
    part_rows = merged.shape[1]
    per_layer = merged.shape[0] // layers
    loads = [
        pltpu.make_async_copy(grad_back, grad_in, in_sem.at[0]),
        pltpu.make_async_copy(layer_back, layer_in, in_sem.at[1]),
    ] + [
        pltpu.make_async_copy(
            merged.at[pl.ds(half * per_layer, per_layer)], chunks.at[pl.ds(half * per_layer, per_layer)], in_sem.at[2 + half]
        )
        for half in range(layers)
    ]
    for load in loads:
        load.start()

    def home(place):
        window = meta[place]
        return (
            pltpu.make_async_copy(grad_wide.at[place], grad_inputs.at[window], out_sem.at[0, place]),
            pltpu.make_async_copy(layer_in.at[place], layer_out.at[window], out_sem.at[1, place]),
        )

    def outs(layer):
        return [
            pltpu.make_async_copy(source.at[layer], target.at[layer], out_sem.at[2 + layer, which])
            for which, (source, target) in enumerate(
                ((qkv_wide, qkv), (attn_wide, attn), (in_wide, in_), (out_wide, out))
            )
        ]

    loads[0].wait()
    loads[1].wait()

    def send(place, carry):
        grad_wide[place] = grad_in[place].astype(F32)
        for copy in home(place):
            copy.start()
        return carry

    lax.fori_loop(0, wins, send, 0)
    for half in range(layers):
        loads[2 + half].wait()
        layer, base = layers - 1 - half, half * per_layer

        def widen(block, carry, layer=layer, base=base):
            at = pl.multiple_of(block * 32, 32)
            here = pl.ds(at, 32)
            for which in range(4):
                columns = slice(which * width, (which + 1) * width)
                there = pl.ds(pl.multiple_of(at + which * part_rows, 32), 32)
                out_wide[layer, there, :] = chunks[base + which, here, :].astype(F32)
                in_wide[layer, here, columns] = chunks[base + 4 + which, here, :].astype(F32)
                if which < 3:
                    qkv_wide[layer, here, columns] = chunks[base + 9 + which, here, :].astype(F32)
            attn_wide[layer, here, :] = chunks[base + 8, here, :].astype(F32)
            return carry

        lax.fori_loop(0, part_rows // 32, widen, 0)
        for copy in outs(layer):
            copy.start()

    var = meta[at_var]
    narrow = out_bias.shape[2]
    at = pl.multiple_of(var * narrow, narrow)
    wide = bias_qv.shape[1]
    for layer in range(layers):
        half = width // wide
        bias_qv[layer : layer + 1, :] = sums[
            layer, pl.ds(var // half, 1), pl.ds(pl.multiple_of(lax.rem(var, half) * wide, wide), wide)
        ]
        bias_in[layer : layer + 1, :] = sums[layer, pl.ds(4 + var, 1), :]
        out_bias[layer] = sums[layer, 2:4, pl.ds(at, narrow)]
        gain[layer] = sums[layer, 8:10, pl.ds(at, narrow)]
        shift[layer] = sums[layer, 10:12, pl.ds(at, narrow)]

    def settle(place, carry):
        for copy in home(place):
            copy.wait()
        return carry

    lax.fori_loop(0, wins, settle, 0)
    for layer in range(layers):
        for copy in outs(layer):
            copy.wait()


def gather_kernel(owners, meta, x, x_out, x_stage, x_send, x_recv, own_sem):
    wins, rows = x.shape[0], x.shape[1]
    each = wins // owners
    me, win = lax.axis_index("var"), lax.axis_index("win")
    others = [(win, flip(me, 1)), (win, flip(me, 2)), (win, flip(flip(me, 1), 2))]
    for place in range(wins):
        x_stage[place] = x[meta[place]]
    greet(others)
    own = pl.ds(pl.multiple_of(me * rows, rows), rows)
    copies = [pltpu.make_async_copy(x_stage.at[pl.ds(me * each, each)], x_out.at[:, own, :], own_sem)]
    for place, other in enumerate(others):
        copies.append(
            pltpu.make_async_remote_copy(
                src_ref=x_stage.at[pl.ds(other[1] * each, each)],
                dst_ref=x_out.at[:, own, :],
                send_sem=x_send.at[place],
                recv_sem=x_recv.at[place],
                device_id=other,
                device_id_type=MESH,
            )
        )
    for copy in copies:
        copy.start()
    for copy in copies:
        copy.wait()


def in_vmem(count):
    return [pl.BlockSpec(memory_space=pltpu.VMEM)] * count


def anywhere(count):
    return [pl.BlockSpec(memory_space=pl.ANY)] * count


def in_smem():
    return [pl.BlockSpec(memory_space=pltpu.SMEM)]


def shaped(shape, kind=LOW):
    return jax.ShapeDtypeStruct(shape, kind)


def whole_windows(
    inputs, counts, row_index, w_qkv, bias_qv, w_attn_out, out_bias, w_in, bias_in, w_ffn_out,
    norm_gain, norm_bias, cotangent,
):
    wins, rows, width = inputs.shape
    owners, groups = lax.axis_size("var"), lax.axis_size("win")
    each, length = wins // owners, rows * owners
    packed = each * length
    layers, hidden_width = w_in.shape[0], w_in.shape[2]
    dma = pltpu.SemaphoreType.DMA

    def params(**more):
        return pltpu.CompilerParams(vmem_limit_bytes=VMEM_BYTES, **more)

    weights = (w_qkv, w_attn_out, w_in, w_ffn_out)
    weight_space = [pltpu.VMEM(weight.shape, LOW) for weight in weights]
    narrow = width // owners
    chunks = layers * 12
    part_rows = width // owners
    half, quarter, eighth = part_rows // 2, part_rows // 4, part_rows // 8
    sums_shape = (layers, 16, width)

    def space(*shape):
        return pltpu.VMEM((chunks,) + shape + (width,), LOW)

    def finish(at_var, meta, merged, sums, layer_back, grad_back):
        rows_shape = (wins, rows, width)
        large = [
            shaped((layers, narrow, 3 * width), F32),
            shaped((layers, narrow, width), F32),
            shaped((layers, narrow, hidden_width), F32),
            shaped((layers, hidden_width // owners, width), F32),
        ]
        layer_out, grad_inputs, *rest = pl.pallas_call(
            functools.partial(finish_kernel, at_var),
            name="finish",
            out_shape=[shaped(rows_shape), shaped(rows_shape, F32)]
            + large
            + [
                shaped((layers, 2 * narrow), F32),
                shaped((layers, 2, narrow), F32),
                shaped((layers, hidden_width // owners), F32),
                shaped((layers, 2, narrow), F32),
                shaped((layers, 2, narrow), F32),
            ],
            in_specs=in_smem() + in_vmem(1) + anywhere(3),
            out_specs=anywhere(6) + in_vmem(5),
            scratch_shapes=[pltpu.VMEM(merged.shape, LOW)]
            + [pltpu.VMEM(rows_shape, LOW)] * 2
            + [pltpu.VMEM(rows_shape, F32)]
            + [pltpu.VMEM(entry.shape, F32) for entry in large]
            + [dma((2 + layers,)), dma((2 + layers, wins))],
            compiler_params=params(),
        )(meta, sums, merged, layer_back, grad_back)
        qkv, attn, in_, out, qv, biases, hidden, gain, shift = rest
        return layer_out, grad_inputs, qkv, qv, attn, biases, in_, hidden, out, gain, shift

    def packed_way():
        size = PACKED
        return pl.pallas_call(
            functools.partial(packed_kernel, owners, size),
            name="packed",
            out_shape=[
                shaped((chunks, part_rows, width)),
                shaped(sums_shape, F32),
                shaped((wins, rows, width)),
                shaped((wins, rows, width)),
                shaped((wins + 2,), jnp.int32),
            ],
            in_specs=in_smem() + in_vmem(3) + anywhere(4) + in_vmem(5),
            out_specs=anywhere(1) + in_vmem(1) + anywhere(2) + in_smem(),
            scratch_shapes=[
                pltpu.VMEM((wins, rows, width), LOW),
                pltpu.VMEM((each, length, width), LOW),
                pltpu.VMEM((4, 8, 128), jnp.int32),
                pltpu.VMEM((3, 8, 128), jnp.int32),
            ]
            + weight_space
            + [
                pltpu.VMEM((wins, rows, width), LOW),
                pltpu.VMEM((each, length, width), LOW),
                pltpu.VMEM((each * length, size), LOW),
                pltpu.VMEM((size, width), F32),
                pltpu.VMEM((layers, 7, size, width), LOW),
                pltpu.VMEM((3, size, width), LOW),
                pltpu.VMEM((layers, size, 3 * width), LOW),
                pltpu.VMEM((layers, size, hidden_width), LOW),
                pltpu.VMEM((layers, 2, size, width), LOW),
                pltpu.VMEM((layers, size, 128), F32),
                pltpu.VMEM((layers, width // 128, 1, 2 * size), F32),
                pltpu.VMEM((size, width), LOW),
                pltpu.VMEM((size, width), LOW),
                pltpu.VMEM(sums_shape, F32),
                pltpu.VMEM((4, 2, 2 * part_rows, width), LOW),
                space(2 * part_rows),
                space(part_rows),
                space(half),
                space(quarter),
                space(eighth),
                space(part_rows),
            ]
            + [pltpu.VMEM((5,) + sums_shape, F32)] * 2
            + [dma((layers, 4)), dma((8, chunks)), dma((8, chunks)), dma((chunks,))]
            + [dma((5,))] * 2
            + [dma((4, owners - 1))] * 2
            + [dma((4,))]
            + [dma((3,))] * 2,
            compiler_params=params(collective_id=2, has_side_effects=True),
        )(
            counts, row_index, inputs, cotangent, *weights, bias_qv, out_bias, bias_in, norm_gain, norm_bias
        )

    def ragged_way():
        x, meta = pl.pallas_call(
            functools.partial(spread_kernel, owners),
            name="spread",
            out_shape=[shaped((each, length, width)), shaped((wins + 2 * each + 2,), jnp.int32)],
            in_specs=in_smem() + in_vmem(1),
            out_specs=anywhere(1) + in_smem(),
            scratch_shapes=[
                pltpu.VMEM((wins, rows, width), LOW),
            ]
            + [dma((owners - 1,))] * 2
            + [dma],
            compiler_params=params(collective_id=0, has_side_effects=True),
        )(counts, inputs)
        g = pl.pallas_call(
            functools.partial(gather_kernel, owners),
            name="gather",
            out_shape=shaped((each, length, width)),
            in_specs=in_smem() + in_vmem(1),
            out_specs=pl.BlockSpec(memory_space=pl.ANY),
            scratch_shapes=[pltpu.VMEM((wins, rows, width), LOW)] + [dma((owners - 1,))] * 2 + [dma],
            compiler_params=params(collective_id=3, has_side_effects=True),
        )(meta, cotangent)
        kept = [
            shaped((layers, packed, 3 * width)),
            shaped((layers, packed, hidden_width)),
            shaped((layers, 2, packed, width), F32),
            shaped((layers, packed, 128), F32),
            shaped((layers, packed, width), F32),
        ]
        kept_space = [pltpu.VMEM(entry.shape, entry.dtype) for entry in kept]
        lefts_shape = shaped((layers, 7, packed, width))
        lefts, *stash, layer_rows = pl.pallas_call(
            forward_kernel,
            name="forward",
            out_shape=[lefts_shape] + kept + [shaped((each, length, width))],
            in_specs=in_smem() + in_vmem(2) + anywhere(4) + in_vmem(5),
            out_specs=anywhere(6) + in_vmem(1),
            scratch_shapes=weight_space
            + [pltpu.VMEM(lefts_shape.shape, LOW)]
            + kept_space
            + [pltpu.VMEM((packed, width), F32), dma((layers, 4)), dma((layers, 6, 6))],
            compiler_params=params(),
        )(meta, row_index, x, *weights, bias_qv, out_bias, bias_in, norm_gain, norm_bias)

        rights_shape = shaped((layers, 9, packed, width))
        rights, grad_rows, sums = pl.pallas_call(
            backward_kernel,
            name="backward",
            out_shape=[rights_shape, shaped((each, length, width)), shaped((layers, 16, width), F32)],
            in_specs=in_smem() + in_vmem(2) + anywhere(4) + in_vmem(1) + anywhere(5),
            out_specs=anywhere(1) + in_vmem(2),
            scratch_shapes=weight_space
            + [pltpu.VMEM(rights_shape.shape, LOW)]
            + kept_space
            + [
                pltpu.VMEM((packed, width), F32),
                pltpu.VMEM((packed, width), LOW),
                dma((layers, 4)),
                dma((layers, 5, 6)),
                dma((layers, 6)),
            ],
            compiler_params=params(),
        )(meta, row_index, g, *weights, norm_gain, *stash)

        merged, sums, layer_back, grad_back = pl.pallas_call(
            functools.partial(merge_kernel, owners),
            name="merge",
            out_shape=[
                shaped((chunks, part_rows, width)),
                shaped(sums.shape, F32),
                shaped((wins, rows, width)),
                shaped((wins, rows, width)),
            ],
            in_specs=in_smem() + anywhere(2) + in_vmem(3),
            out_specs=anywhere(1) + in_vmem(1) + anywhere(2),
            scratch_shapes=[pltpu.VMEM((2, packed, width), LOW)] * 2
            + [
                space(2, 2, part_rows),
                space(2, part_rows),
                space(2, part_rows),
                space(part_rows),
                space(2, half),
                space(half),
                space(2, quarter),
                space(quarter),
                space(2, eighth),
                space(eighth),
                space(part_rows),
            ]
            + [pltpu.VMEM((5,) + sums.shape, F32)] * 2
            + [dma((2, 2)), dma((8, chunks)), dma((8, chunks)), dma((chunks,))]
            + [dma((5,))] * 2
            + [dma((2, owners - 1))] * 2
            + [dma((2,))],
            compiler_params=params(collective_id=1, has_side_effects=True),
        )(meta, lefts, rights, sums, layer_rows, grad_rows)
        return finish(wins + 2 * each, meta, merged, sums, layer_back, grad_back)

    *sums_up, order = packed_way()
    return lax.cond(order[wins + 1] <= BLOCKS[1], lambda: finish(wins, order, *sums_up), ragged_way)


def choose(*arrays):
    wins, rows, width = arrays[0].shape
    owners, groups = lax.axis_size("var"), lax.axis_size("win")
    fits = owners == 4 and groups == 8 and wins % owners == 0 and rows % 16 == 0
    fits = fits and (wins // owners, rows * owners, width, arrays[7].shape[2]) == (3, 256, 512, 2048)
    return whole_windows(*arrays) if fits else per_device(*arrays)


def solution(mesh):
    return jax.shard_map(
        choose,
        mesh=mesh,
        in_specs=(
            P("win", "var", None),
            P("win"),
            P("win", None),
            P(),
            P(),
            P(),
            P(),
            P(),
            P(),
            P(),
            P(),
            P(),
            P("win", "var", None),
        ),
        out_specs=(
            P("win", "var", None),
            P("win", "var", None),
            P(None, "var", None),
            P(None, "var"),
            P(None, "var", None),
            P(None, None, "var"),
            P(None, "var", None),
            P(None, "var"),
            P(None, "var", None),
            P(None, None, "var"),
            P(None, None, "var"),
        ),
        check_vma=False,
    )
```
